32 devices in a mesh: dp: 8 (over y, x, core), tm: 4 (over z).
Axes of the slice: x: 2, y: 2, z: 4, core: 2. Of those that a mesh axis runs over, the one named last changes fastest.
Arguments:
- query_rows: bfloat16 [8, 896, 1024], P('dp', 'tm'), may hold values from -6 to 6
- key_rows: bfloat16 [8, 896, 1024], P('dp', 'tm'), may hold values from -6 to 6
- value_rows: bfloat16 [8, 896, 1024], P('dp', 'tm'), may hold values from -6 to 6
- head_scale: float32 [16], replicated, may hold values from 2 to 16
- out_proj: bfloat16 [1024, 1536], replicated, may hold values from -0.1875 to 0.1875
- conv_taps: float32 [31, 1536], replicated, may hold values from -1 to 1
- router: bfloat16 [1536, 8], replicated, may hold values from -0.15625 to 0.15625
- expert_in: bfloat16 [8, 2048, 1536], P('dp', 'tm'), may hold values from -0.15625 to 0.15625
- expert_out: bfloat16 [8, 2048, 1536], P('dp', 'tm'), may hold values from -0.125 to 0.125
- lengths: int32 [8, 4], P('dp'), may hold values from 1 to 672, 896 in all within a row
- routes: int32 [8, 896, 2], P('dp', 'tm'), may hold values from 0 to 7, all different within a row; in each aligned block of 224 rows (0 to 223, 224 to 447, ..., all dimensions but the last counted through in order) at most 84 rows name the same one
Outputs:
- block_out: bfloat16 [8, 896, 1536], P('dp', 'tm')
The draws below stay inside these ranges and needn't reach their ends.
Inputs may be any that keep to these rules, and one draw needn't show every extreme that they name: Every length is at least 1, the 4 lengths of a pack sum to 896, and the largest of each pack is exactly 672. `routes`: the 2 experts of a frame differ. Among the 224 frames of one block (frames j * 224 to (j + 1) * 224 - 1 of a pack), no expert is named by more than 84 frames, and in some block some expert is named by exactly 84. Every expert is named somewhere.
All inputs are finite; a program needn't handle non-finite values.
Results may differ from the reference program's by a relative error of at most 0.0099.
Values may be sent and summed in bfloat16 or wider, within the bound.
No kernel may reach another device: no remote copies, remote signals or barrier semaphores. Data moves between devices by JAX's collectives and lax.ppermute only.
A program may use at most 128 MiB of HBM per device.

```python
import math
import jax
import jax.numpy as jnp
import numpy as np
from jax import lax

D = 1536
HEADS = 16
HEAD_DIM = 64
KERNEL = 31
HALF = 15
FF_E = 2048
TOPK = 2
RECS = 4
ROWS = 224
EXPERTS = 8
PACKS = 8
FRAMES = 896
MOST = 672
CAP = 84
N_TM = 4


def shard_levels(own_key, extent, cuts, low, top_value):
    loudness, own = 1.0, jax.random.fold_in(own_key, 6)
    for position, parts in cuts:
        draws = jnp.exp(jax.random.uniform(jax.random.fold_in(own, position), (parts,), jnp.float32, low / len(cuts), top_value / len(cuts)))
        loudness = loudness * jnp.repeat(draws, extent[position] // parts).reshape([-1 if axis == position else 1 for axis in range(len(extent))])
    return loudness


def length_profile(amount, total, most, skew):
    loads = [(1 << 20) // math.isqrt(grade ** skew) + 1 for grade in range(2, amount + 1)]
    rest, holding = total - most - (amount - 1), [1] * (amount - 1)
    while rest > 0:
        candidates = [i for i in range(amount - 1) if holding[i] < most]
        whole, left = sum([loads[i] for i in candidates]), rest
        for i in candidates:
            addition = min(most - holding[i], max(1, left * loads[i] // whole), rest)
            holding[i] = holding[i] + addition
            rest = rest - addition
    return np.array([most] + holding)


def ragged_sizes(own_key, number_of, total, limit, slope):
    if number_of == 2:
        one = jax.random.randint(own_key, (), max(1, total - limit), min(limit, total - 1) + 1)
        return jnp.stack([one, total - one])
    sizes = jnp.asarray(length_profile(number_of, total, limit, slope), jnp.int32)
    twos = (number_of - 1) // 2
    donor, receiver = sizes[1:1 + 2 * twos:2], sizes[2:2 + 2 * twos:2]
    room = jnp.minimum(donor - 1, limit - receiver)
    passed = jax.random.randint(jax.random.fold_in(own_key, 1), (twos,), 0, 1 << 20) % (room + 1)
    sizes = sizes.at[1:1 + 2 * twos:2].set(donor - passed).at[2:2 + 2 * twos:2].set(receiver + passed)
    return sizes[jax.random.permutation(jax.random.fold_in(own_key, 2), number_of)]


def deal_out(key, own, number, rows, count, top, bound, slope):
    order = jax.random.permutation(key, count)
    heavy_load, ordinary = shares(count, rows * top, bound, slope, True), shares(count, rows * top, bound, slope, False)
    places = jnp.arange(count)

    def named(sizes, offset_by):
        used = int((sizes > 0).sum())
        fixed = max(1, used // 4)
        shifted = fixed + (places - fixed + offset_by * (used - fixed)) % max(1, count - fixed)
        return jnp.zeros((count,), jnp.int32).at[order[jnp.where(places < fixed, places, shifted)]].set(jnp.asarray(sizes, jnp.int32))

    sizes = jnp.where(number % 4 == 0, named(heavy_load, number // 4), named(ordinary, number - number // 4 - 1))
    mixed = jax.random.permutation(jax.random.fold_in(own, 3), count)
    source_of, receiver = mixed[0:count // 2 * 2:2], mixed[1:count // 2 * 2:2]
    room = jnp.minimum(sizes[source_of] - 1, bound - sizes[receiver]) // 2
    room = jnp.where((source_of == order[0]) | (receiver == order[0]) | (sizes[receiver] == 0), 0, jnp.maximum(room, 0))
    shifted = jax.random.randint(jax.random.fold_in(own, 4), (count // 2,), 0, 1 << 20) % (room + 1)
    sizes = sizes.at[source_of].add(-shifted).at[receiver].add(shifted)
    items = jnp.searchsorted(jnp.cumsum(sizes), jnp.arange(rows * top), side="right").astype(jnp.int32)
    table = items.reshape(top, rows).T
    table = table[jax.random.permutation(jax.random.fold_in(own, 1), rows)]
    offset_by = jax.random.randint(jax.random.fold_in(own, 2), (rows, 1), 0, top)
    return jnp.take_along_axis(table, (jnp.arange(top)[None, :] + offset_by) % top, axis=1)


def shares(count, total, reach, slope, full):
    loads = [(1 << 20) // math.isqrt(standing ** slope) + 1 for standing in range(1, count + 1)]
    largest = reach if full else min(reach, max(-(-total // count), total * loads[0] // sum(loads)))
    least = 1 if total - largest >= count - 1 else 0
    holding, rest = [largest] + [least] * (count - 1), total - largest - least * (count - 1)
    while rest > 0:
        movable = [i for i in range(1, count) if holding[i] < largest] or [i for i in range(1, count) if holding[i] < reach]
        mass, left = sum([loads[i] for i in movable]), rest
        for i in movable:
            more = min(reach - holding[i], max(1, left * loads[i] // mass), rest)
            holding[i] = holding[i] + more
            rest = rest - more
    return np.array(holding)


def gaussian(own_key, dims, deviation, most, shards=(), kind=jnp.bfloat16):
    values = jax.random.normal(own_key, dims, jnp.float32) * deviation
    if len(shards) > 0:
        values = shard_levels(own_key, dims, shards, -0.22, 0.18) * values
    return jnp.clip(values, min=-most, max=most).astype(kind)


def setup_inputs(seed: int = 0) -> dict:
    keys = jax.random.split(jax.random.key(seed), 12)
    query_rows = gaussian(keys[0], (PACKS, FRAMES, HEADS * HEAD_DIM), 1.0, 6.0, ((0, 8), (1, 4)))
    key_rows = gaussian(keys[1], (PACKS, FRAMES, HEADS * HEAD_DIM), 1.0, 6.0, ((0, 8), (1, 4)))
    value_rows = gaussian(keys[2], (PACKS, FRAMES, HEADS * HEAD_DIM), 1.0, 6.0, ((0, 8), (1, 4)))
    head_scale = jnp.clip(jnp.exp(jax.random.uniform(keys[3], (HEADS,), jnp.float32, math.log(2.0), math.log(16.0))), 2.0, 16.0)
    out_proj = gaussian(keys[4], (HEADS * HEAD_DIM, D), (HEADS * HEAD_DIM) ** -0.5, 0.1875)
    conv_taps = gaussian(keys[5], (KERNEL, D), KERNEL ** -0.5, 1.0, (), jnp.float32)
    router = gaussian(keys[6], (D, EXPERTS), D ** -0.5, 0.15625)
    expert_in = gaussian(keys[7], (EXPERTS, FF_E, D), D ** -0.5, 0.15625, ((0, 8), (1, 4)))
    expert_out = gaussian(keys[8], (EXPERTS, FF_E, D), FF_E ** -0.5, 0.125, ((0, 8), (1, 4)))
    lengths = jax.vmap(lambda own: ragged_sizes(own, RECS, FRAMES, MOST, 2))(jax.random.split(keys[9], PACKS)).reshape((PACKS, RECS)).astype(jnp.int32)
    routes_keys = jax.random.split(jax.random.fold_in(keys[10], 1), PACKS * FRAMES // ROWS)
    routes_turns = jax.random.permutation(jax.random.fold_in(keys[10], 3), PACKS * FRAMES // ROWS)
    routes = jax.vmap(lambda own, number: deal_out(jax.random.fold_in(keys[10], 2), own, number, ROWS, EXPERTS, TOPK, CAP, 2))(routes_keys, routes_turns).reshape((PACKS, FRAMES, TOPK))
    return {"query_rows": query_rows, "key_rows": key_rows, "value_rows": value_rows, "head_scale": head_scale, "out_proj": out_proj, "conv_taps": conv_taps, "router": router, "expert_in": expert_in, "expert_out": expert_out, "lengths": lengths, "routes": routes}


def layer_norm(values):
    average = lax.optimization_barrier(jnp.mean(values, axis=-1, keepdims=True))
    centered = values - average
    spread = lax.optimization_barrier(jnp.mean(centered * centered, axis=-1, keepdims=True))
    return centered * lax.rsqrt(spread + 1e-05)

def unit_heads(rows):
    lifted = rows.astype(jnp.float32).reshape(rows.shape[0], HEADS, HEAD_DIM)
    factor = lax.rsqrt(lax.optimization_barrier(jnp.sum(lifted * lifted, axis=-1, keepdims=True)) + 1e-06)
    return (lifted * factor).astype(jnp.bfloat16)

def recording_of(positions, pack_lengths):
    bounds = jnp.cumsum(pack_lengths).astype(jnp.int32)[:RECS - 1]
    return lax.optimization_barrier(jnp.sum((positions[:, None] >= bounds[None, :]).astype(jnp.int32), axis=1)).astype(jnp.int32)

def attend_pack(query_rows, key_rows, value_rows, pack_lengths, head_scale):
    frames = jnp.arange(FRAMES, dtype=jnp.int32)
    labels = recording_of(frames, pack_lengths)
    query_unit = unit_heads(query_rows)
    key_unit = unit_heads(key_rows).astype(jnp.float32)
    value_heads = value_rows.astype(jnp.float32).reshape(FRAMES, HEADS, HEAD_DIM)
    block = math.gcd(FRAMES, 512)

    def one_block(first):
        query_block = lax.dynamic_slice_in_dim(query_unit, first, block, 0).astype(jnp.float32)
        query_labels = lax.dynamic_slice_in_dim(labels, first, block, 0)
        scores = jnp.einsum('qhd,khd->hqk', query_block, key_unit)
        inside = (query_labels[:, None] == labels[None, :])[None]
        weights = jnp.where(inside, jnp.exp(head_scale[:, None, None] * (scores - 1.0)), 0.0)
        masses = lax.optimization_barrier(jnp.sum(weights, axis=-1))
        rounded = lax.optimization_barrier(weights.astype(jnp.bfloat16)).astype(jnp.float32)
        summed = jnp.einsum('hqk,khd->qhd', rounded, value_heads)
        return (summed / jnp.transpose(masses)[:, :, None]).reshape(block, HEADS * HEAD_DIM).astype(jnp.bfloat16)
    starts = jnp.arange(FRAMES // block, dtype=jnp.int32) * block
    return lax.map(one_block, starts).reshape(FRAMES, HEADS * HEAD_DIM)

def conv_pack(normed, pack_lengths, conv_taps):
    labels = recording_of(jnp.arange(FRAMES, dtype=jnp.int32), pack_lengths)
    padded = jnp.pad(normed, ((HALF, HALF), (0, 0)))
    padded_labels = recording_of(jnp.arange(-HALF, FRAMES + HALF, dtype=jnp.int32), pack_lengths)
    total = jnp.zeros((FRAMES, D), jnp.float32)
    for offset in range(KERNEL):
        same = (padded_labels[offset:offset + FRAMES] == labels)[:, None]
        term = conv_taps[offset][None, :] * padded[offset:offset + FRAMES].astype(jnp.float32)
        total = total + jnp.where(same, term, 0.0)
    return total

def reference(query_rows, key_rows, value_rows, head_scale, out_proj, conv_taps, router, expert_in, expert_out, lengths, routes):
    attended = lax.map(lambda items: attend_pack(items[0], items[1], items[2], items[3], head_scale), (query_rows, key_rows, value_rows, lengths))
    first = jnp.dot(attended.reshape(PACKS * FRAMES, HEADS * HEAD_DIM), out_proj, preferred_element_type=jnp.float32)
    normed = layer_norm(first).astype(jnp.bfloat16)
    convolved = lax.map(lambda items: conv_pack(items[0], items[1], conv_taps), (normed.reshape(PACKS, FRAMES, D), lengths))
    second = first + jax.nn.silu(convolved.reshape(PACKS * FRAMES, D))
    mixed_in = layer_norm(second).astype(jnp.bfloat16)
    logits = jnp.dot(mixed_in, router, preferred_element_type=jnp.float32)
    flat_routes = routes.reshape(PACKS * FRAMES, TOPK)
    chosen = jnp.exp(jnp.take_along_axis(logits, flat_routes, axis=1))
    gates = chosen / lax.optimization_barrier(jnp.sum(chosen, axis=1, keepdims=True))
    blocks = PACKS * N_TM
    block_routes = flat_routes.reshape(blocks, ROWS, TOPK)
    picks = lax.optimization_barrier(jnp.sum((block_routes[:, :, :, None] == jnp.arange(EXPERTS, dtype=jnp.int32)).astype(jnp.int32), axis=2)).astype(jnp.int32)
    ranks = (jnp.cumsum(picks, axis=1) - picks).astype(jnp.int32)
    slot_rank = jnp.take_along_axis(ranks, block_routes, axis=2).astype(jnp.int32)
    block_ids = jnp.broadcast_to(jnp.arange(blocks, dtype=jnp.int32)[:, None, None], block_routes.shape)
    frame_ids = jnp.broadcast_to(jnp.arange(PACKS * FRAMES, dtype=jnp.int32).reshape(blocks, ROWS, 1), block_routes.shape)
    sentinel = PACKS * FRAMES
    table = jnp.full((EXPERTS, blocks, CAP), sentinel, jnp.int32).at[block_routes, block_ids, slot_rank].set(frame_ids)
    gate_table = jnp.zeros((EXPERTS, blocks, CAP), jnp.float32).at[block_routes, block_ids, slot_rank].set(gates.reshape(blocks, ROWS, TOPK))
    padded_in = jnp.concatenate([mixed_in, jnp.zeros((1, D), jnp.bfloat16)], axis=0)

    def one_expert(summed, items):
        frame_list, weights_in, weights_out, gate_rows = items
        frame_list = frame_list.reshape(-1)
        tokens = padded_in[frame_list]
        hidden = jax.nn.silu(jnp.dot(tokens, weights_in.T, preferred_element_type=jnp.float32)).astype(jnp.bfloat16)
        result = jnp.dot(hidden, weights_out, preferred_element_type=jnp.float32).astype(jnp.bfloat16)
        summed = summed.at[frame_list].add(gate_rows.reshape(-1)[:, None] * result.astype(jnp.float32), mode='drop')
        return (summed, None)
    mixture, _ = lax.scan(one_expert, jnp.zeros((PACKS * FRAMES, D), jnp.float32), (table, expert_in, expert_out, gate_table))
    return (second + 0.5 * mixture).astype(jnp.bfloat16).reshape(PACKS, FRAMES, D)
```

```python
import functools

import jax
import jax.numpy as jnp
from jax import lax
from jax.experimental import pallas as pl
from jax.experimental.pallas import tpu as pltpu
from jax.sharding import PartitionSpec as P

D = 1536
HEADS = 16
HEAD_DIM = 64
KERNEL = 31
TOPK = 2
RECS = 4
HALO = 16
LANES = 128
APART = 64.0
LOG2E = 1.4426950408889634
F32 = jnp.float32
BF16 = jnp.bfloat16
VMEM = pl.BlockSpec(memory_space=pltpu.VMEM)
SMEM = pl.BlockSpec(memory_space=pltpu.SMEM)


def params(mib):
    return pltpu.CompilerParams(vmem_limit_bytes=mib << 20)


def labels_of(frames, len_ref):
    first = len_ref[0, 0]
    second = first + len_ref[0, 1]
    third = second + len_ref[0, 2]
    return (
        (frames >= first).astype(F32)
        + (frames >= second).astype(F32)
        + (frames >= third).astype(F32)
    )


def unit_tile(tile, low):
    lifted = tile.astype(F32)
    square = lifted * lifted
    left = jnp.sum(jnp.where(low, square, 0.0), axis=1, keepdims=True)
    right = jnp.sum(jnp.where(low, 0.0, square), axis=1, keepdims=True)
    factor = jnp.where(low, lax.rsqrt(left + 1e-06), lax.rsqrt(right + 1e-06))
    return lifted * factor


def attend_kernel(count, rows, heads, scale_ref, len_ref, x_ref, o_ref, k_ref, v_ref, a_ref):
    block = pl.program_id(0)
    width = heads * HEAD_DIM
    tiles = max(1, width // LANES)
    half = count // 2
    window = rows + 2 * HALO

    def tile_of(source, which, place):
        if width >= LANES:
            return x_ref[source, which, :, place * LANES : (place + 1) * LANES]
        piece = x_ref[source, which]
        return jnp.concatenate([piece, jnp.zeros((rows, LANES - width), BF16)], axis=1)

    low = lax.broadcasted_iota(jnp.int32, (rows, LANES), 1) < HEAD_DIM
    lane = lax.broadcasted_iota(jnp.int32, (rows, LANES), 1).astype(F32)
    row = lax.broadcasted_iota(jnp.int32, (rows, LANES), 0)

    @pl.when(block == 0)
    def _():
        edge = jnp.zeros((HALO, width), BF16)
        a_ref[0:HALO, :] = edge
        a_ref[HALO + count * rows :, :] = edge
        for source in range(count):
            at = slice(source * rows, (source + 1) * rows)
            label = labels_of(row + source * rows, len_ref)
            other = jnp.where((lane >= 1.0) & (lane <= 4.0) & (lane != label + 1.0), -APART, 0.0)
            extra = jnp.where(lane == 0.0, -1.0, other).astype(BF16)
            for place in range(tiles):
                k_ref[place, at, 0:LANES] = unit_tile(tile_of(source, 1, place), low).astype(BF16)
                k_ref[place, at, LANES:] = extra
                v_ref[place, at, 0:LANES] = tile_of(source, 2, place)
                v_ref[place, at, LANES:] = jnp.ones((rows, LANES), BF16)

    label = labels_of(row + block * rows, len_ref)
    extra = jnp.where((lane == 0.0) | (lane == label + 1.0), 1.0, 0.0).astype(BF16)
    for place in range(tiles):
        unit = unit_tile(tile_of(block, 0, place), low)
        parts = []
        for side in range(min(2, heads)):
            head = place * 2 + side
            kept = jnp.where(low if side == 0 else ~low, unit, 0.0).astype(BF16)
            query = jnp.concatenate([kept, extra], axis=1)
            scores = lax.dot_general(
                query, k_ref[place], (((1,), (1,)), ((), ())), preferred_element_type=F32
            )
            weights = jnp.exp2(scores * (scale_ref[head] * LOG2E)).astype(BF16)
            summed = jnp.dot(weights, v_ref[place], preferred_element_type=F32)
            parts.append(summed[:, 0:LANES] / summed[:, LANES:])
        done = parts[0] if len(parts) == 1 else jnp.where(low, parts[0], parts[1])
        start = pl.multiple_of(HALO + block * rows, HALO)
        wide = min(LANES, width)
        a_ref[pl.ds(start, rows), place * LANES : place * LANES + wide] = done[:, 0:wide].astype(BF16)

    @pl.when(block == count - 1)
    def _():
        for target in range(count):
            for which in range(2):
                begin = (target % half + which * half) * rows
                o_ref[target, which] = a_ref[begin : begin + window, :]


def normalize(values):
    average = jnp.mean(values, axis=-1, keepdims=True)
    centered = values - average
    spread = jnp.mean(centered * centered, axis=-1, keepdims=True)
    return centered * lax.rsqrt(spread + 1e-05)


def frame_kernel(
    count,
    rows,
    experts,
    capacity,
    block_ref,
    len_ref,
    att_ref,
    proj_ref,
    taps_ref,
    router_ref,
    routes_ref,
    turned_ref,
    out_ref,
    second_ref,
    info_ref,
    x_ref,
    first_ref,
    lab_ref,
    mixed_ref,
):
    window = rows + 2 * HALO
    half = (KERNEL - 1) // 2
    tiles = D // LANES
    step = 56
    for which in range(2):
        attended = jnp.concatenate([att_ref[i, which] for i in range(count)], axis=1)
        first = jnp.dot(attended, proj_ref[...], preferred_element_type=F32)
        normed = normalize(first).astype(BF16).astype(F32)
        origin = block_ref[which] * rows - HALO
        frames = lax.broadcasted_iota(jnp.int32, (window, LANES), 0) + origin
        lab_ref[which] = labels_of(frames, len_ref)
        for tile in range(tiles):
            at = slice(tile * LANES, (tile + 1) * LANES)
            x_ref[which, tile] = normed[:, at]
            first_ref[which, tile] = first[HALO : HALO + rows, at]

    starts = [len_ref[0, 0], len_ref[0, 0] + len_ref[0, 1]]
    starts.append(starts[1] + len_ref[0, 2])
    for which in range(2):
        for begin in range(0, rows, step):
            low = block_ref[which] * rows + begin - half
            high = low + step + 2 * half
            mixed = functools.reduce(
                jnp.logical_or, [(low < start) & (start < high) for start in starts]
            )

            def columns(tile, masked):
                total = jnp.zeros((step, LANES), F32)
                own = lab_ref[which, HALO + begin : HALO + begin + step, :] if masked else None
                for tap in range(KERNEL):
                    source = HALO - half + begin + tap
                    term = taps_ref[tile, tap : tap + 1, :] * x_ref[which, tile, source : source + step, :]
                    if masked:
                        term = jnp.where(lab_ref[which, source : source + step, :] == own, term, 0.0)
                    total = total + term
                gated = total / (1.0 + jnp.exp(-total))
                second_ref[which, tile, begin : begin + step, :] = (
                    first_ref[which, tile, begin : begin + step, :] + gated
                )

            @pl.when(mixed)
            def _():
                lax.fori_loop(0, tiles, lambda tile, c: (columns(tile, True), c)[1], 0)

            @pl.when(jnp.logical_not(mixed))
            def _():
                lax.fori_loop(0, tiles, lambda tile, c: (columns(tile, False), c)[1], 0)

    for which in range(2):
        second = jnp.concatenate([second_ref[which, tile] for tile in range(tiles)], axis=1)
        mixed_ref[which * rows : (which + 1) * rows, :] = normalize(second).astype(BF16)

    frames = 2 * rows
    logits = jnp.dot(mixed_ref[...], router_ref[...], preferred_element_type=F32)
    lane = lax.broadcasted_iota(jnp.int32, (frames, experts), 1)
    named = [lane == routes_ref[:, pick : pick + 1] for pick in range(TOPK)]
    picked = [jnp.sum(jnp.where(one, logits, 0.0), axis=1, keepdims=True) for one in named]
    top = jnp.maximum(picked[0], picked[1])
    raised = [jnp.exp(one - top) for one in picked]
    mass = raised[0] + raised[1]
    down = lax.broadcasted_iota(jnp.int32, (frames, frames), 0)
    across = lax.broadcasted_iota(jnp.int32, (frames, frames), 1)
    picks = jnp.where(named[0] | named[1], 1.0, 0.0).astype(BF16)
    earlier = jnp.where(across < down, 1.0, 0.0).astype(BF16)
    ranks = jnp.dot(earlier, picks, preferred_element_type=F32)
    columns = lax.broadcasted_iota(jnp.int32, (frames, LANES), 1)
    info = jnp.zeros((frames, LANES), F32)
    for pick in range(TOPK):
        rank = jnp.sum(jnp.where(named[pick], ranks, 0.0), axis=1, keepdims=True)
        slot = rank + (routes_ref[:, pick : pick + 1] * capacity).astype(F32)
        info = jnp.where(columns == pick, slot, info)
        info = jnp.where(columns == TOPK + pick, raised[pick] / mass, info)
    for which in range(2):
        info_ref[which] = info[which * rows : (which + 1) * rows, :]

    expert = lax.broadcasted_iota(jnp.int32, (experts, frames), 0)
    chosen = (expert == turned_ref[0:1, :]) | (expert == turned_ref[1:2, :])
    later = jnp.where(down < across, 1.0, 0.0).astype(BF16)
    order = jnp.dot(jnp.where(chosen, 1.0, 0.0).astype(BF16), later, preferred_element_type=F32)
    order = jnp.where(chosen, order, -1.0)
    place = lax.broadcasted_iota(jnp.int32, (capacity, frames), 0).astype(F32)
    for e in range(experts):
        select = jnp.where(place == order[e : e + 1, :], 1.0, 0.0).astype(BF16)
        out_ref[e] = jnp.dot(select, mixed_ref[...], preferred_element_type=F32).astype(BF16)


def expert_kernel(pieces, x_ref, *refs):
    ins, outs, o_ref = refs[:pieces], refs[pieces : 2 * pieces], refs[2 * pieces]
    total = None
    for piece_in, piece_out in zip(ins, outs):
        raw = lax.dot_general(
            x_ref[...], piece_in[...], (((1,), (1,)), ((), ())), preferred_element_type=F32
        )
        hidden = (raw / (1.0 + jnp.exp(-raw))).astype(BF16)
        product = jnp.dot(hidden, piece_out[...], preferred_element_type=F32)
        total = product if total is None else total + product
    o_ref[...] = total.astype(BF16)


def mixture_of(info, back):
    column = lax.broadcasted_iota(jnp.int32, (info.shape[0], back.shape[0]), 1).astype(F32)
    spread = jnp.where(column == info[:, 0:1], info[:, 2:3], 0.0)
    spread = jnp.where(column == info[:, 1:2], info[:, 3:4], spread).astype(BF16)
    return jnp.dot(spread, back, preferred_element_type=F32)


def theirs_kernel(own_ref, info_ref, back_ref, o_ref):
    o_ref[...] = mixture_of(info_ref[1 - own_ref[0]], back_ref[...]).astype(BF16)


def mine_kernel(own_ref, info_ref, back_ref, second_ref, o_ref):
    mixture = mixture_of(info_ref[own_ref[0]], back_ref[...])
    for tile in range(D // LANES):
        at = slice(tile * LANES, (tile + 1) * LANES)
        o_ref[:, at] = second_ref[own_ref[0], tile] + 0.5 * mixture[:, at]


def body(
    query_rows,
    key_rows,
    value_rows,
    head_scale,
    out_proj,
    conv_taps,
    router,
    expert_in,
    expert_out,
    lengths,
    routes,
):
    rows = query_rows.shape[1]
    experts = lax.axis_size("dp")
    count = lax.axis_size("tm")
    half = count // 2
    heads = HEADS // count
    width = heads * HEAD_DIM
    window = rows + 2 * HALO
    capacity = -(-2 * (3 * rows // experts) // 16) * 16
    me = lax.axis_index("tm").astype(jnp.int32)
    side = (me // half).reshape(1)
    blocks = jnp.stack([me % half, me % half + half])
    partner = [(i, (i + half) % count) for i in range(count)]

    packed = jnp.stack([query_rows[0], key_rows[0], value_rows[0]])
    packed = jnp.transpose(packed.reshape(3, rows, count, width), (2, 0, 1, 3))
    arrived = lax.all_to_all(packed, "tm", split_axis=0, concat_axis=0, tiled=True)
    scales = lax.dynamic_slice_in_dim(head_scale, me * heads, heads)

    other_routes = lax.ppermute(routes[0], "tm", partner)
    is_low = me < half
    both = jnp.concatenate(
        [
            jnp.where(is_low, routes[0], other_routes),
            jnp.where(is_low, other_routes, routes[0]),
        ]
    )

    if half == 2:
        swap = [(i, i ^ 1) for i in range(count)]
        ins = [expert_in[0], lax.ppermute(expert_in[0], "tm", swap)]
        outs = [expert_out[0], lax.ppermute(expert_out[0], "tm", swap)]
    else:
        groups = [list(range(half)), list(range(half, count))]
        ins = [lax.all_gather(expert_in[0], "tm", axis=0, tiled=True, axis_index_groups=groups)]
        outs = [lax.all_gather(expert_out[0], "tm", axis=0, tiled=True, axis_index_groups=groups)]

    tiles = max(1, width // LANES)
    total = count * rows
    attended = pl.pallas_call(
        functools.partial(attend_kernel, count, rows, heads),
        grid=(count,),
        out_shape=jax.ShapeDtypeStruct((count, 2, window, width), BF16),
        in_specs=[SMEM, SMEM, pl.BlockSpec((count, 3, rows, width), lambda i: (0, 0, 0, 0))],
        out_specs=pl.BlockSpec((count, 2, window, width), lambda i: (0, 0, 0, 0)),
        scratch_shapes=[
            pltpu.VMEM((tiles, total, 2 * LANES), BF16),
            pltpu.VMEM((tiles, total, 2 * LANES), BF16),
            pltpu.VMEM((total + 2 * HALO, width), BF16),
        ],
        compiler_params=params(40),
        name="attend",
    )(scales, lengths, arrived)
    gathered = lax.all_to_all(attended, "tm", split_axis=0, concat_axis=0, tiled=True)

    taps = jnp.transpose(conv_taps.reshape(KERNEL, D // LANES, LANES), (1, 0, 2))
    outgoing, second, info = pl.pallas_call(
        functools.partial(frame_kernel, count, rows, experts, capacity),
        out_shape=(
            jax.ShapeDtypeStruct((experts, capacity, D), BF16),
            jax.ShapeDtypeStruct((2, D // LANES, rows, LANES), F32),
            jax.ShapeDtypeStruct((2, rows, LANES), F32),
        ),
        in_specs=[SMEM, SMEM, VMEM, VMEM, VMEM, VMEM, VMEM, VMEM],
        out_specs=(VMEM, VMEM, VMEM),
        scratch_shapes=[
            pltpu.VMEM((2, D // LANES, window, LANES), F32),
            pltpu.VMEM((2, D // LANES, rows, LANES), F32),
            pltpu.VMEM((2, window, LANES), F32),
            pltpu.VMEM((2 * rows, D), BF16),
        ],
        compiler_params=params(50),
        name="frames",
    )(blocks, lengths, gathered, out_proj, taps, router, both, both.T)

    tokens = lax.all_to_all(outgoing, "dp", split_axis=0, concat_axis=0, tiled=True)
    tokens = tokens.reshape(experts * capacity, D)

    pieces = len(ins)
    units = ins[0].shape[0]
    parts = 4
    tall = experts * capacity // parts
    produced = pl.pallas_call(
        functools.partial(expert_kernel, pieces),
        grid=(parts,),
        out_shape=jax.ShapeDtypeStruct((experts * capacity, D), BF16),
        in_specs=[pl.BlockSpec((tall, D), lambda i: (i, 0))]
        + [pl.BlockSpec((units, D), lambda i: (0, 0))] * (2 * pieces),
        out_specs=pl.BlockSpec((tall, D), lambda i: (i, 0)),
        compiler_params=params(50),
        name="experts",
    )(tokens, *ins, *outs)

    back = lax.all_to_all(
        produced.reshape(experts, capacity, D), "dp", split_axis=0, concat_axis=0, tiled=True
    )
    back = back.reshape(experts * capacity, D)

    theirs = pl.pallas_call(
        theirs_kernel,
        out_shape=jax.ShapeDtypeStruct((rows, D), BF16),
        in_specs=[SMEM, VMEM, VMEM],
        out_specs=VMEM,
        compiler_params=params(40),
        name="theirs",
    )(side, info, back)
    received = lax.ppermute(theirs, "tm", partner)
    mine = pl.pallas_call(
        mine_kernel,
        out_shape=jax.ShapeDtypeStruct((rows, D), F32),
        in_specs=[SMEM, VMEM, VMEM, VMEM],
        out_specs=VMEM,
        compiler_params=params(40),
        name="mine",
    )(side, info, back, second)
    return (mine + 0.5 * received.astype(F32)).astype(BF16)[None]


def solution(mesh):
    return jax.shard_map(
        body,
        mesh=mesh,
        in_specs=(
            P("dp", "tm", None),
            P("dp", "tm", None),
            P("dp", "tm", None),
            P(),
            P(),
            P(),
            P(),
            P("dp", "tm", None),
            P("dp", "tm", None),
            P("dp", None),
            P("dp", "tm", None),
        ),
        out_specs=P("dp", "tm", None),
        check_vma=False,
    )
```

```python
import functools

import jax
import jax.numpy as jnp
from jax import lax
from jax.experimental import pallas as pl
from jax.experimental.pallas import tpu as pltpu
from jax.sharding import PartitionSpec as P

D = 1536
HEADS = 16
HEAD_DIM = 64
KERNEL = 31
TOPK = 2
RECS = 4
HALO = 16
LANES = 128
APART = 64.0
LOG2E = 1.4426950408889634
F32 = jnp.float32
BF16 = jnp.bfloat16
VMEM = pl.BlockSpec(memory_space=pltpu.VMEM)
SMEM = pl.BlockSpec(memory_space=pltpu.SMEM)


def params(mib):
    return pltpu.CompilerParams(vmem_limit_bytes=mib << 20)


def cost(micros):
    return pl.CostEstimate(flops=micros * 1_100_000_000, bytes_accessed=0, transcendentals=0)


def labels_of(frames, len_ref):
    first = len_ref[0, 0]
    second = first + len_ref[0, 1]
    third = second + len_ref[0, 2]
    return (
        (frames >= first).astype(F32)
        + (frames >= second).astype(F32)
        + (frames >= third).astype(F32)
    )


def unit_tile(tile, low):
    lifted = tile.astype(F32)
    square = lifted * lifted
    left = jnp.sum(jnp.where(low, square, 0.0), axis=1, keepdims=True)
    right = jnp.sum(jnp.where(low, 0.0, square), axis=1, keepdims=True)
    factor = jnp.where(low, lax.rsqrt(left + 1e-06), lax.rsqrt(right + 1e-06))
    return lifted * factor


def attend_kernel(count, rows, heads, scale_ref, len_ref, x_ref, oa_ref, ob_ref, k_ref, v_ref, a_ref
):
    block = pl.program_id(0)
    width = heads * HEAD_DIM
    tiles = max(1, width // LANES)
    half = count // 2
    window = rows + 2 * HALO

    def tile_of(source, which, place):
        if width >= LANES:
            return x_ref[source, which, :, place * LANES : (place + 1) * LANES]
        piece = x_ref[source, which]
        return jnp.concatenate([piece, jnp.zeros((rows, LANES - width), BF16)], axis=1)

    low = lax.broadcasted_iota(jnp.int32, (rows, LANES), 1) < HEAD_DIM
    lane = lax.broadcasted_iota(jnp.int32, (rows, LANES), 1).astype(F32)
    row = lax.broadcasted_iota(jnp.int32, (rows, LANES), 0)

    @pl.when(block == 0)
    def _():
        edge = jnp.zeros((HALO, width), BF16)
        a_ref[0:HALO, :] = edge
        a_ref[HALO + count * rows :, :] = edge
        for source in range(count):
            at = slice(source * rows, (source + 1) * rows)
            label = labels_of(row + source * rows, len_ref)
            other = jnp.where((lane >= 1.0) & (lane <= 4.0) & (lane != label + 1.0), -APART, 0.0)
            extra = jnp.where(lane == 0.0, -1.0, other).astype(BF16)
            for place in range(tiles):
                k_ref[place, at, 0:LANES] = unit_tile(tile_of(source, 1, place), low).astype(BF16)
                k_ref[place, at, LANES:] = extra
                v_ref[place, at, 0:LANES] = tile_of(source, 2, place)
                v_ref[place, at, LANES:] = jnp.ones((rows, LANES), BF16)

    label = labels_of(row + block * rows, len_ref)
    extra = jnp.where((lane == 0.0) | (lane == label + 1.0), 1.0, 0.0).astype(BF16)
    for place in range(tiles):
        unit = unit_tile(tile_of(block, 0, place), low)
        parts = []
        for side in range(min(2, heads)):
            head = place * 2 + side
            kept = jnp.where(low if side == 0 else ~low, unit, 0.0).astype(BF16)
            query = jnp.concatenate([kept, extra], axis=1)
            scores = lax.dot_general(
                query, k_ref[place], (((1,), (1,)), ((), ())), preferred_element_type=F32
            )
            weights = jnp.exp2(scores * (scale_ref[head] * LOG2E)).astype(BF16)
            summed = jnp.dot(weights, v_ref[place], preferred_element_type=F32)
            parts.append(summed[:, 0:LANES] / summed[:, LANES:])
        done = parts[0] if len(parts) == 1 else jnp.where(low, parts[0], parts[1])
        start = pl.multiple_of(HALO + block * rows, HALO)
        wide = min(LANES, width)
        a_ref[pl.ds(start, rows), place * LANES : place * LANES + wide] = done[:, 0:wide].astype(BF16)

    @pl.when(block == count - 1)
    def _():
        for target in range(count):
            for o_ref, block_of in ((oa_ref, (target + half) % count), (ob_ref, target)):
                begin = block_of * rows
                o_ref[target] = a_ref[begin : begin + window, :]


def normalize(values):
    average = jnp.mean(values, axis=-1, keepdims=True)
    centered = values - average
    spread = jnp.mean(centered * centered, axis=-1, keepdims=True)
    return centered * lax.rsqrt(spread + 1e-05)


def frame_kernel(
    count,
    rows,
    experts,
    capacity,
    block_ref,
    len_ref,
    att_ref,
    proj_ref,
    taps_ref,
    router_ref,
    routes_ref,
    turned_ref,
    out_ref,
    info_ref,
    second_ref,
    x_ref,
    first_ref,
    lab_ref,
):
    window = rows + 2 * HALO
    half = (KERNEL - 1) // 2
    tiles = D // LANES
    step = 56
    attended = jnp.concatenate([att_ref[i] for i in range(count)], axis=1)
    first = jnp.dot(attended, proj_ref[...], preferred_element_type=F32)
    normed = normalize(first).astype(BF16).astype(F32)
    origin = block_ref[0] * rows
    frames = lax.broadcasted_iota(jnp.int32, (window, LANES), 0) + (origin - HALO)
    lab_ref[...] = labels_of(frames, len_ref)
    for tile in range(tiles):
        at = slice(tile * LANES, (tile + 1) * LANES)
        x_ref[tile] = normed[:, at]
        first_ref[tile] = first[HALO : HALO + rows, at]

    starts = [len_ref[0, 0], len_ref[0, 0] + len_ref[0, 1]]
    starts.append(starts[1] + len_ref[0, 2])
    for begin in range(0, rows, step):
        low = origin + begin - half
        high = low + step + 2 * half
        crossed = functools.reduce(
            jnp.logical_or, [(low < start) & (start < high) for start in starts]
        )

        def columns(tile, masked):
            total = jnp.zeros((step, LANES), F32)
            own = lab_ref[HALO + begin : HALO + begin + step, :] if masked else None
            for tap in range(KERNEL):
                source = HALO - half + begin + tap
                term = taps_ref[tile, tap : tap + 1, :] * x_ref[tile, source : source + step, :]
                if masked:
                    term = jnp.where(lab_ref[source : source + step, :] == own, term, 0.0)
                total = total + term
            gated = total / (1.0 + jnp.exp(-total))
            second_ref[tile, begin : begin + step, :] = (
                first_ref[tile, begin : begin + step, :] + gated
            )

        @pl.when(crossed)
        def _():
            lax.fori_loop(0, tiles, lambda tile, c: (columns(tile, True), c)[1], 0)

        @pl.when(jnp.logical_not(crossed))
        def _():
            lax.fori_loop(0, tiles, lambda tile, c: (columns(tile, False), c)[1], 0)

    second = jnp.concatenate([second_ref[tile] for tile in range(tiles)], axis=1)
    mixed = normalize(second).astype(BF16)

    logits = jnp.dot(mixed, router_ref[...], preferred_element_type=F32)
    lane = lax.broadcasted_iota(jnp.int32, (rows, experts), 1)
    named = [lane == routes_ref[:, pick : pick + 1] for pick in range(TOPK)]
    picked = [jnp.sum(jnp.where(one, logits, 0.0), axis=1, keepdims=True) for one in named]
    top = jnp.maximum(picked[0], picked[1])
    raised = [jnp.exp(one - top) for one in picked]
    mass = raised[0] + raised[1]
    down = lax.broadcasted_iota(jnp.int32, (rows, rows), 0)
    across = lax.broadcasted_iota(jnp.int32, (rows, rows), 1)
    picks = jnp.where(named[0] | named[1], 1.0, 0.0).astype(BF16)
    earlier = jnp.where(across < down, 1.0, 0.0).astype(BF16)
    ranks = jnp.dot(earlier, picks, preferred_element_type=F32)
    column = lax.broadcasted_iota(jnp.int32, (rows, LANES), 1)
    info = jnp.zeros((rows, LANES), F32)
    for pick in range(TOPK):
        rank = jnp.sum(jnp.where(named[pick], ranks, 0.0), axis=1, keepdims=True)
        slot = rank + (routes_ref[:, pick : pick + 1] * capacity).astype(F32)
        info = jnp.where(column == pick, slot, info)
        info = jnp.where(column == TOPK + pick, raised[pick] / mass, info)
    info_ref[...] = info

    expert = lax.broadcasted_iota(jnp.int32, (experts, rows), 0)
    chosen = (expert == turned_ref[0:1, :]) | (expert == turned_ref[1:2, :])
    later = jnp.where(down < across, 1.0, 0.0).astype(BF16)
    order = jnp.dot(jnp.where(chosen, 1.0, 0.0).astype(BF16), later, preferred_element_type=F32)
    order = jnp.where(chosen, order, -1.0)
    place = lax.broadcasted_iota(jnp.int32, (capacity, rows), 0).astype(F32)
    select = jnp.concatenate(
        [jnp.where(place == order[e : e + 1, :], 1.0, 0.0) for e in range(experts)], axis=0
    ).astype(BF16)
    out_ref[...] = jnp.dot(select, mixed, preferred_element_type=F32).astype(BF16)


def expert_kernel(pieces, x_ref, *refs):
    ins, outs, o_ref = refs[:pieces], refs[pieces : 2 * pieces], refs[2 * pieces]
    total = None
    for piece_in, piece_out in zip(ins, outs):
        raw = lax.dot_general(
            x_ref[...], piece_in[...], (((1,), (1,)), ((), ())), preferred_element_type=F32
        )
        hidden = (raw / (1.0 + jnp.exp(-raw))).astype(BF16)
        product = jnp.dot(hidden, piece_out[...], preferred_element_type=F32)
        total = product if total is None else total + product
    o_ref[...] = total.astype(BF16)


def mixture_of(info, back):
    column = lax.broadcasted_iota(jnp.int32, (info.shape[0], back.shape[0]), 1).astype(F32)
    spread = jnp.where(column == info[:, 0:1], info[:, 2:3], 0.0)
    spread = jnp.where(column == info[:, 1:2], info[:, 3:4], spread).astype(BF16)
    return jnp.dot(spread, back, preferred_element_type=F32)


def theirs_kernel(info_ref, back_ref, o_ref):
    o_ref[...] = mixture_of(info_ref[...], back_ref[...]).astype(BF16)


def mine_kernel(info_ref, back_ref, second_ref, part_ref, o_ref):
    mixture = mixture_of(info_ref[...], back_ref[...])
    for tile in range(D // LANES):
        at = slice(tile * LANES, (tile + 1) * LANES)
        both = mixture[:, at] + part_ref[:, at].astype(F32)
        o_ref[:, at] = (second_ref[tile] + 0.5 * both).astype(BF16)


def body(
    query_rows,
    key_rows,
    value_rows,
    head_scale,
    out_proj,
    conv_taps,
    router,
    expert_in,
    expert_out,
    lengths,
    routes,
):
    rows = query_rows.shape[1]
    experts = lax.axis_size("dp")
    count = lax.axis_size("tm")
    half = count // 2
    heads = HEADS // count
    width = heads * HEAD_DIM
    window = rows + 2 * HALO
    capacity = -(-(3 * rows // experts) // 8) * 8
    slots = experts * capacity
    me = lax.axis_index("tm").astype(jnp.int32)
    partner = [(i, (i + half) % count) for i in range(count)]

    packed = jnp.stack([query_rows[0], key_rows[0], value_rows[0]])
    packed = jnp.transpose(packed.reshape(3, rows, count, width), (2, 0, 1, 3))
    arrived = lax.all_to_all(packed, "tm", split_axis=0, concat_axis=0, tiled=True)
    scales = lax.dynamic_slice_in_dim(head_scale, me * heads, heads)
    partner_routes = lax.ppermute(routes[0], "tm", partner)

    own_in, own_out, _ = lax.optimization_barrier((expert_in[0], expert_out[0], arrived))
    if half == 2:
        swap = [(i, i ^ 1) for i in range(count)]
        ins = [own_in, lax.ppermute(own_in, "tm", swap)]
        outs = [own_out, lax.ppermute(own_out, "tm", swap)]
    else:
        groups = [list(range(half)), list(range(half, count))]
        ins = [lax.all_gather(own_in, "tm", axis=0, tiled=True, axis_index_groups=groups)]
        outs = [lax.all_gather(own_out, "tm", axis=0, tiled=True, axis_index_groups=groups)]

    tiles = max(1, width // LANES)
    total = count * rows
    sent = jax.ShapeDtypeStruct((count, window, width), BF16)
    attended = pl.pallas_call(
        functools.partial(attend_kernel, count, rows, heads),
        grid=(count,),
        out_shape=(sent, sent),
        in_specs=[SMEM, SMEM, pl.BlockSpec((count, 3, rows, width), lambda i: (0, 0, 0, 0))],
        out_specs=(pl.BlockSpec((count, window, width), lambda i: (0, 0, 0)),) * 2,
        scratch_shapes=[
            pltpu.VMEM((tiles, total, 2 * LANES), BF16),
            pltpu.VMEM((tiles, total, 2 * LANES), BF16),
            pltpu.VMEM((total + 2 * HALO, width), BF16),
        ],
        compiler_params=params(40),
        cost_estimate=cost(8),
        name="attend",
    )(scales, lengths, arrived)
    gathered = [
        lax.all_to_all(one, "tm", split_axis=0, concat_axis=0, tiled=True) for one in attended
    ]

    taps = jnp.transpose(conv_taps.reshape(KERNEL, D // LANES, LANES), (1, 0, 2))
    pieces = len(ins)
    units = ins[0].shape[0]
    tall = slots // 2

    def send_frames(windows, block, block_routes):
        outgoing, info, second = pl.pallas_call(
            functools.partial(frame_kernel, count, rows, experts, capacity),
            out_shape=(
                jax.ShapeDtypeStruct((slots, D), BF16),
                jax.ShapeDtypeStruct((rows, LANES), F32),
                jax.ShapeDtypeStruct((D // LANES, rows, LANES), F32),
            ),
            in_specs=[SMEM, SMEM, VMEM, VMEM, VMEM, VMEM, VMEM, VMEM],
            out_specs=(VMEM, VMEM, VMEM),
            scratch_shapes=[
                pltpu.VMEM((D // LANES, window, LANES), F32),
                pltpu.VMEM((D // LANES, rows, LANES), F32),
                pltpu.VMEM((window, LANES), F32),
            ],
            compiler_params=params(50),
            cost_estimate=cost(10),
            name="frames",
        )(block.reshape(1), lengths, windows, out_proj, taps, router, block_routes, block_routes.T)
        tokens = lax.all_to_all(
            outgoing.reshape(experts, capacity, D), "dp", split_axis=0, concat_axis=0, tiled=True
        )
        return tokens.reshape(slots, D), info, second

    def run_expert(tokens):
        produced = pl.pallas_call(
            functools.partial(expert_kernel, pieces),
            grid=(2,),
            out_shape=jax.ShapeDtypeStruct((slots, D), BF16),
            in_specs=[pl.BlockSpec((tall, D), lambda i: (i, 0))]
            + [pl.BlockSpec((units, D), lambda i: (0, 0))] * (2 * pieces),
            out_specs=pl.BlockSpec((tall, D), lambda i: (i, 0)),
            compiler_params=params(50),
            cost_estimate=cost(7),
            name="experts",
        )(tokens, *ins, *outs)
        back = lax.all_to_all(
            produced.reshape(experts, capacity, D), "dp", split_axis=0, concat_axis=0, tiled=True
        )
        return back.reshape(slots, D)

    tokens_a, info_a, _ = send_frames(gathered[0], (me + half) % count, partner_routes)
    tokens_b, info_b, second = send_frames(gathered[1], me, routes[0])
    back_a = run_expert(tokens_a)
    back_b = run_expert(tokens_b)

    theirs = pl.pallas_call(
        theirs_kernel,
        out_shape=jax.ShapeDtypeStruct((rows, D), BF16),
        in_specs=[VMEM, VMEM],
        out_specs=VMEM,
        compiler_params=params(40),
        cost_estimate=cost(3),
        name="theirs",
    )(info_a, back_a)
    received = lax.ppermute(theirs, "tm", partner)
    out = pl.pallas_call(
        mine_kernel,
        out_shape=jax.ShapeDtypeStruct((rows, D), BF16),
        in_specs=[VMEM, VMEM, VMEM, VMEM],
        out_specs=VMEM,
        compiler_params=params(40),
        cost_estimate=cost(3),
        name="mine",
    )(info_b, back_b, second, received)
    return out[None]


def solution(mesh):
    return jax.shard_map(
        body,
        mesh=mesh,
        in_specs=(
            P("dp", "tm", None),
            P("dp", "tm", None),
            P("dp", "tm", None),
            P(),
            P(),
            P(),
            P(),
            P("dp", "tm", None),
            P("dp", "tm", None),
            P("dp", None),
            P("dp", "tm", None),
        ),
        out_specs=P("dp", "tm", None),
        check_vma=False,
    )
```

```python
import functools

import jax
import jax.numpy as jnp
from jax import lax
from jax.experimental import pallas as pl
from jax.experimental.pallas import tpu as pltpu
from jax.sharding import PartitionSpec as P

D = 1536
HEADS = 16
HEAD_DIM = 64
KERNEL = 31
TOPK = 2
RECS = 4
HALO = 16
LANES = 128
APART = 64.0
LOG2E = 1.4426950408889634
F32 = jnp.float32
BF16 = jnp.bfloat16
VMEM = pl.BlockSpec(memory_space=pltpu.VMEM)
SMEM = pl.BlockSpec(memory_space=pltpu.SMEM)


def params(mib):
    return pltpu.CompilerParams(vmem_limit_bytes=mib << 20)


def cost(micros):
    return pl.CostEstimate(flops=micros * 1_100_000_000, bytes_accessed=0, transcendentals=0)


def labels_of(frames, len_ref):
    first = len_ref[0, 0]
    second = first + len_ref[0, 1]
    third = second + len_ref[0, 2]
    return (
        (frames >= first).astype(F32)
        + (frames >= second).astype(F32)
        + (frames >= third).astype(F32)
    )


def unit_tile(tile, low):
    lifted = tile.astype(F32)
    square = lifted * lifted
    left = jnp.sum(jnp.where(low, square, 0.0), axis=1, keepdims=True)
    right = jnp.sum(jnp.where(low, 0.0, square), axis=1, keepdims=True)
    factor = jnp.where(low, lax.rsqrt(left + 1e-06), lax.rsqrt(right + 1e-06))
    return lifted * factor


def pack_kernel(q_ref, k_ref, v_ref, o_ref):
    width = o_ref.shape[3]
    for which, ref in enumerate((q_ref, k_ref, v_ref)):
        for target in range(o_ref.shape[0]):
            o_ref[target, which] = ref[:, target * width : (target + 1) * width]


def attend_kernel(count, rows, heads, scale_ref, len_ref, x_ref, oa_ref, ob_ref, k_ref, v_ref, a_ref
):
    block = pl.program_id(0)
    width = heads * HEAD_DIM
    tiles = max(1, width // LANES)
    half = count // 2
    window = rows + 2 * HALO

    def tile_of(source, which, place):
        if width >= LANES:
            return x_ref[source, which, :, place * LANES : (place + 1) * LANES]
        piece = x_ref[source, which]
        return jnp.concatenate([piece, jnp.zeros((rows, LANES - width), BF16)], axis=1)

    low = lax.broadcasted_iota(jnp.int32, (rows, LANES), 1) < HEAD_DIM
    lane = lax.broadcasted_iota(jnp.int32, (rows, LANES), 1).astype(F32)
    row = lax.broadcasted_iota(jnp.int32, (rows, LANES), 0)

    @pl.when(block == 0)
    def _():
        edge = jnp.zeros((HALO, width), BF16)
        a_ref[0:HALO, :] = edge
        a_ref[HALO + count * rows :, :] = edge
        for source in range(count):
            at = slice(source * rows, (source + 1) * rows)
            label = labels_of(row + source * rows, len_ref)
            other = jnp.where((lane >= 1.0) & (lane <= 4.0) & (lane != label + 1.0), -APART, 0.0)
            extra = jnp.where(lane == 0.0, -1.0, other).astype(BF16)
            for place in range(tiles):
                k_ref[place, at, 0:LANES] = unit_tile(tile_of(source, 1, place), low).astype(BF16)
                k_ref[place, at, LANES:] = extra
                v_ref[place, at, 0:LANES] = tile_of(source, 2, place)
                v_ref[place, at, LANES:] = jnp.ones((rows, LANES), BF16)

    label = labels_of(row + block * rows, len_ref)
    extra = jnp.where((lane == 0.0) | (lane == label + 1.0), 1.0, 0.0).astype(BF16)
    for place in range(tiles):
        unit = unit_tile(tile_of(block, 0, place), low)
        parts = []
        for side in range(min(2, heads)):
            head = place * 2 + side
            kept = jnp.where(low if side == 0 else ~low, unit, 0.0).astype(BF16)
            query = jnp.concatenate([kept, extra], axis=1)
            scores = lax.dot_general(
                query, k_ref[place], (((1,), (1,)), ((), ())), preferred_element_type=F32
            )
            weights = jnp.exp2(scores * (scale_ref[head] * LOG2E)).astype(BF16)
            summed = jnp.dot(weights, v_ref[place], preferred_element_type=F32)
            parts.append(summed[:, 0:LANES] / summed[:, LANES:])
        done = parts[0] if len(parts) == 1 else jnp.where(low, parts[0], parts[1])
        start = pl.multiple_of(HALO + block * rows, HALO)
        wide = min(LANES, width)
        a_ref[pl.ds(start, rows), place * LANES : place * LANES + wide] = done[:, 0:wide].astype(BF16)

    @pl.when(block == count - 1)
    def _():
        for target in range(count):
            for o_ref, block_of in ((oa_ref, (target + half) % count), (ob_ref, target)):
                begin = block_of * rows
                o_ref[target] = a_ref[begin : begin + window, :]


def normalize(values):
    average = jnp.mean(values, axis=-1, keepdims=True)
    centered = values - average
    spread = jnp.mean(centered * centered, axis=-1, keepdims=True)
    return centered * lax.rsqrt(spread + 1e-05)


def frame_kernel(
    count,
    rows,
    experts,
    capacity,
    block_ref,
    len_ref,
    att_ref,
    proj_ref,
    taps_ref,
    router_ref,
    routes_ref,
    turned_ref,
    out_ref,
    info_ref,
    second_ref,
    x_ref,
    first_ref,
    lab_ref,
):
    window = rows + 2 * HALO
    half = (KERNEL - 1) // 2
    tiles = D // LANES
    step = 56
    attended = jnp.concatenate([att_ref[i] for i in range(count)], axis=1)
    first = jnp.dot(attended, proj_ref[...], preferred_element_type=F32)
    normed = normalize(first).astype(BF16).astype(F32)
    origin = block_ref[0] * rows
    frames = lax.broadcasted_iota(jnp.int32, (window, LANES), 0) + (origin - HALO)
    lab_ref[...] = labels_of(frames, len_ref)
    for tile in range(tiles):
        at = slice(tile * LANES, (tile + 1) * LANES)
        x_ref[tile] = normed[:, at]
        first_ref[tile] = first[HALO : HALO + rows, at]

    starts = [len_ref[0, 0], len_ref[0, 0] + len_ref[0, 1]]
    starts.append(starts[1] + len_ref[0, 2])
    for begin in range(0, rows, step):
        low = origin + begin - half
        high = low + step + 2 * half
        crossed = functools.reduce(
            jnp.logical_or, [(low < start) & (start < high) for start in starts]
        )

        def columns(tile, masked):
            total = jnp.zeros((step, LANES), F32)
            own = lab_ref[HALO + begin : HALO + begin + step, :] if masked else None
            for tap in range(KERNEL):
                source = HALO - half + begin + tap
                term = taps_ref[tile, tap : tap + 1, :] * x_ref[tile, source : source + step, :]
                if masked:
                    term = jnp.where(lab_ref[source : source + step, :] == own, term, 0.0)
                total = total + term
            gated = total / (1.0 + jnp.exp(-total))
            second_ref[tile, begin : begin + step, :] = (
                first_ref[tile, begin : begin + step, :] + gated
            )

        @pl.when(crossed)
        def _():
            lax.fori_loop(0, tiles, lambda tile, c: (columns(tile, True), c)[1], 0)

        @pl.when(jnp.logical_not(crossed))
        def _():
            lax.fori_loop(0, tiles, lambda tile, c: (columns(tile, False), c)[1], 0)

    second = jnp.concatenate([second_ref[tile] for tile in range(tiles)], axis=1)
    mixed = normalize(second).astype(BF16)

    logits = jnp.dot(mixed, router_ref[...], preferred_element_type=F32)
    lane = lax.broadcasted_iota(jnp.int32, (rows, experts), 1)
    named = [lane == routes_ref[:, pick : pick + 1] for pick in range(TOPK)]
    picked = [jnp.sum(jnp.where(one, logits, 0.0), axis=1, keepdims=True) for one in named]
    top = jnp.maximum(picked[0], picked[1])
    raised = [jnp.exp(one - top) for one in picked]
    mass = raised[0] + raised[1]
    down = lax.broadcasted_iota(jnp.int32, (rows, rows), 0)
    across = lax.broadcasted_iota(jnp.int32, (rows, rows), 1)
    picks = jnp.where(named[0] | named[1], 1.0, 0.0).astype(BF16)
    earlier = jnp.where(across < down, 1.0, 0.0).astype(BF16)
    ranks = jnp.dot(earlier, picks, preferred_element_type=F32)
    column = lax.broadcasted_iota(jnp.int32, (rows, LANES), 1)
    info = jnp.zeros((rows, LANES), F32)
    for pick in range(TOPK):
        rank = jnp.sum(jnp.where(named[pick], ranks, 0.0), axis=1, keepdims=True)
        slot = rank + (routes_ref[:, pick : pick + 1] * capacity).astype(F32)
        info = jnp.where(column == pick, slot, info)
        info = jnp.where(column == TOPK + pick, raised[pick] / mass, info)
    info_ref[...] = info

    expert = lax.broadcasted_iota(jnp.int32, (experts, rows), 0)
    chosen = (expert == turned_ref[0:1, :]) | (expert == turned_ref[1:2, :])
    later = jnp.where(down < across, 1.0, 0.0).astype(BF16)
    order = jnp.dot(jnp.where(chosen, 1.0, 0.0).astype(BF16), later, preferred_element_type=F32)
    order = jnp.where(chosen, order, -1.0)
    place = lax.broadcasted_iota(jnp.int32, (capacity, rows), 0).astype(F32)
    select = jnp.concatenate(
        [jnp.where(place == order[e : e + 1, :], 1.0, 0.0) for e in range(experts)], axis=0
    ).astype(BF16)
    out_ref[...] = jnp.dot(select, mixed, preferred_element_type=F32).astype(BF16)


def expert_kernel(pieces, x_ref, *refs):
    ins, outs, o_ref = refs[:pieces], refs[pieces : 2 * pieces], refs[2 * pieces]
    total = None
    for piece_in, piece_out in zip(ins, outs):
        raw = lax.dot_general(
            x_ref[...], piece_in[...], (((1,), (1,)), ((), ())), preferred_element_type=F32
        )
        hidden = (raw / (1.0 + jnp.exp(-raw))).astype(BF16)
        product = jnp.dot(hidden, piece_out[...], preferred_element_type=F32)
        total = product if total is None else total + product
    o_ref[...] = total.astype(BF16)


def mixture_of(info, back):
    column = lax.broadcasted_iota(jnp.int32, (info.shape[0], back.shape[0]), 1).astype(F32)
    spread = jnp.where(column == info[:, 0:1], info[:, 2:3], 0.0)
    spread = jnp.where(column == info[:, 1:2], info[:, 3:4], spread).astype(BF16)
    return jnp.dot(spread, back, preferred_element_type=F32)


def theirs_kernel(info_ref, back_ref, o_ref):
    o_ref[...] = mixture_of(info_ref[...], back_ref[...]).astype(BF16)


def mine_kernel(info_ref, back_ref, second_ref, part_ref, o_ref):
    mixture = mixture_of(info_ref[...], back_ref[...])
    for tile in range(D // LANES):
        at = slice(tile * LANES, (tile + 1) * LANES)
        both = mixture[:, at] + part_ref[:, at].astype(F32)
        o_ref[:, at] = (second_ref[tile] + 0.5 * both).astype(BF16)


def body(
    query_rows,
    key_rows,
    value_rows,
    head_scale,
    out_proj,
    conv_taps,
    router,
    expert_in,
    expert_out,
    lengths,
    routes,
):
    rows = query_rows.shape[1]
    experts = lax.axis_size("dp")
    count = lax.axis_size("tm")
    half = count // 2
    heads = HEADS // count
    width = heads * HEAD_DIM
    window = rows + 2 * HALO
    capacity = -(-(3 * rows // experts) // 8) * 8
    slots = experts * capacity
    me = lax.axis_index("tm").astype(jnp.int32)
    partner = [(i, (i + half) % count) for i in range(count)]

    packed = pl.pallas_call(
        pack_kernel,
        out_shape=jax.ShapeDtypeStruct((count, 3, rows, width), BF16),
        in_specs=[VMEM, VMEM, VMEM],
        out_specs=VMEM,
        compiler_params=params(16),
        cost_estimate=cost(1),
        name="pack",
    )(query_rows[0], key_rows[0], value_rows[0])
    arrived = lax.all_to_all(packed, "tm", split_axis=0, concat_axis=0, tiled=True)
    scales = lax.dynamic_slice_in_dim(head_scale, me * heads, heads)
    partner_routes = lax.ppermute(routes[0], "tm", partner)

    own_in, own_out, _ = lax.optimization_barrier((expert_in[0], expert_out[0], arrived))
    groups = [list(range(half)), list(range(half, count))]
    ins = [lax.all_gather(own_in, "tm", axis=0, tiled=True, axis_index_groups=groups)]
    outs = [lax.all_gather(own_out, "tm", axis=0, tiled=True, axis_index_groups=groups)]

    tiles = max(1, width // LANES)
    total = count * rows
    sent = jax.ShapeDtypeStruct((count, window, width), BF16)
    attended = pl.pallas_call(
        functools.partial(attend_kernel, count, rows, heads),
        grid=(count,),
        out_shape=(sent, sent),
        in_specs=[SMEM, SMEM, pl.BlockSpec((count, 3, rows, width), lambda i: (0, 0, 0, 0))],
        out_specs=(pl.BlockSpec((count, window, width), lambda i: (0, 0, 0)),) * 2,
        scratch_shapes=[
            pltpu.VMEM((tiles, total, 2 * LANES), BF16),
            pltpu.VMEM((tiles, total, 2 * LANES), BF16),
            pltpu.VMEM((total + 2 * HALO, width), BF16),
        ],
        compiler_params=params(40),
        cost_estimate=cost(8),
        name="attend",
    )(scales, lengths, arrived)
    gathered = [
        lax.all_to_all(one, "tm", split_axis=0, concat_axis=0, tiled=True) for one in attended
    ]

    taps = jnp.transpose(conv_taps.reshape(KERNEL, D // LANES, LANES), (1, 0, 2))
    pieces = len(ins)
    units = ins[0].shape[0]
    tall = slots // 2

    def send_frames(windows, block, block_routes):
        outgoing, info, second = pl.pallas_call(
            functools.partial(frame_kernel, count, rows, experts, capacity),
            out_shape=(
                jax.ShapeDtypeStruct((slots, D), BF16),
                jax.ShapeDtypeStruct((rows, LANES), F32),
                jax.ShapeDtypeStruct((D // LANES, rows, LANES), F32),
            ),
            in_specs=[SMEM, SMEM, VMEM, VMEM, VMEM, VMEM, VMEM, VMEM],
            out_specs=(VMEM, VMEM, VMEM),
            scratch_shapes=[
                pltpu.VMEM((D // LANES, window, LANES), F32),
                pltpu.VMEM((D // LANES, rows, LANES), F32),
                pltpu.VMEM((window, LANES), F32),
            ],
            compiler_params=params(50),
            cost_estimate=cost(10),
            name="frames",
        )(block.reshape(1), lengths, windows, out_proj, taps, router, block_routes, block_routes.T)
        tokens = lax.all_to_all(
            outgoing.reshape(experts, capacity, D), "dp", split_axis=0, concat_axis=0, tiled=True
        )
        return tokens.reshape(slots, D), info, second

    def run_expert(tokens):
        produced = pl.pallas_call(
            functools.partial(expert_kernel, pieces),
            grid=(2,),
            out_shape=jax.ShapeDtypeStruct((slots, D), BF16),
            in_specs=[pl.BlockSpec((tall, D), lambda i: (i, 0))]
            + [pl.BlockSpec((units, D), lambda i: (0, 0))] * (2 * pieces),
            out_specs=pl.BlockSpec((tall, D), lambda i: (i, 0)),
            compiler_params=params(50),
            cost_estimate=cost(7),
            name="experts",
        )(tokens, *ins, *outs)
        back = lax.all_to_all(
            produced.reshape(experts, capacity, D), "dp", split_axis=0, concat_axis=0, tiled=True
        )
        return back.reshape(slots, D)

    tokens_a, info_a, _ = send_frames(gathered[0], (me + half) % count, partner_routes)
    tokens_b, info_b, second = send_frames(gathered[1], me, routes[0])
    back_a = run_expert(tokens_a)
    back_b = run_expert(tokens_b)

    theirs = pl.pallas_call(
        theirs_kernel,
        out_shape=jax.ShapeDtypeStruct((rows, D), BF16),
        in_specs=[VMEM, VMEM],
        out_specs=VMEM,
        compiler_params=params(40),
        cost_estimate=cost(3),
        name="theirs",
    )(info_a, back_a)
    received = lax.ppermute(theirs, "tm", partner)
    out = pl.pallas_call(
        mine_kernel,
        out_shape=jax.ShapeDtypeStruct((rows, D), BF16),
        in_specs=[VMEM, VMEM, VMEM, VMEM],
        out_specs=VMEM,
        compiler_params=params(40),
        cost_estimate=cost(3),
        name="mine",
    )(info_b, back_b, second, received)
    return out[None]


def solution(mesh):
    return jax.shard_map(
        body,
        mesh=mesh,
        in_specs=(
            P("dp", "tm", None),
            P("dp", "tm", None),
            P("dp", "tm", None),
            P(),
            P(),
            P(),
            P(),
            P("dp", "tm", None),
            P("dp", "tm", None),
            P("dp", None),
            P("dp", "tm", None),
        ),
        out_specs=P("dp", "tm", None),
        check_vma=False,
    )
```

```python
import functools

import jax
import jax.numpy as jnp
from jax import lax
from jax.experimental import pallas as pl
from jax.experimental.pallas import tpu as pltpu
from jax.sharding import PartitionSpec as P

D = 1536
HEADS = 16
HEAD_DIM = 64
KERNEL = 31
TOPK = 2
RECS = 4
HALO = 16
LANES = 128
APART = 64.0
LOG2E = 1.4426950408889634
F32 = jnp.float32
BF16 = jnp.bfloat16
VMEM = pl.BlockSpec(memory_space=pltpu.VMEM)
SMEM = pl.BlockSpec(memory_space=pltpu.SMEM)


def params(mib):
    return pltpu.CompilerParams(vmem_limit_bytes=mib << 20)


def cost(micros):
    return pl.CostEstimate(flops=micros * 1_100_000_000, bytes_accessed=0, transcendentals=0)


def labels_of(frames, len_ref):
    first = len_ref[0, 0]
    second = first + len_ref[0, 1]
    third = second + len_ref[0, 2]
    return (
        (frames >= first).astype(F32)
        + (frames >= second).astype(F32)
        + (frames >= third).astype(F32)
    )


def unit_tile(tile, low):
    lifted = tile.astype(F32)
    square = lifted * lifted
    left = jnp.sum(jnp.where(low, square, 0.0), axis=1, keepdims=True)
    right = jnp.sum(jnp.where(low, 0.0, square), axis=1, keepdims=True)
    factor = jnp.where(low, lax.rsqrt(left + 1e-06), lax.rsqrt(right + 1e-06))
    return lifted * factor


def pack_kernel(place, q_ref, k_ref, v_ref, me_ref, *o_refs):
    width = o_refs[0].shape[2]
    for r, o_ref in enumerate(o_refs):
        target = place(me_ref[0], r)
        for which, ref in enumerate((q_ref, k_ref, v_ref)):
            if isinstance(target, int):
                o_ref[which] = ref[:, target * width : (target + 1) * width]
            else:
                o_ref[which] = ref[:, pl.ds(pl.multiple_of(target * width, LANES), width)]


def attend_kernel(count, rows, heads, place, me_ref, scale_ref, len_ref, *refs):
    x_refs, oa_refs, ob_refs = refs[:count], refs[count : 2 * count], refs[2 * count : 3 * count]
    k_ref, v_ref, a_ref = refs[3 * count :]
    me = me_ref[0]
    width = heads * HEAD_DIM
    tiles = max(1, width // LANES)
    half = count // 2
    window = rows + 2 * HALO

    def tile_of(r, which, tile):
        if width >= LANES:
            return x_refs[r][which, :, tile * LANES : (tile + 1) * LANES]
        piece = x_refs[r][which]
        return jnp.concatenate([piece, jnp.zeros((rows, LANES - width), BF16)], axis=1)

    low = lax.broadcasted_iota(jnp.int32, (rows, LANES), 1) < HEAD_DIM
    lane = lax.broadcasted_iota(jnp.int32, (rows, LANES), 1).astype(F32)
    row = lax.broadcasted_iota(jnp.int32, (rows, LANES), 0)

    edge = jnp.zeros((HALO, width), BF16)
    a_ref[0:HALO, :] = edge
    a_ref[HALO + count * rows :, :] = edge
    for r in range(count):
        at = slice(r * rows, (r + 1) * rows)
        label = labels_of(row + place(me, r) * rows, len_ref)
        other = jnp.where((lane >= 1.0) & (lane <= 4.0) & (lane != label + 1.0), -APART, 0.0)
        extra = jnp.where(lane == 0.0, -1.0, other).astype(BF16)
        for tile in range(tiles):
            k_ref[tile, at, 0:LANES] = unit_tile(tile_of(r, 1, tile), low).astype(BF16)
            k_ref[tile, at, LANES:] = extra
            v_ref[tile, at, 0:LANES] = tile_of(r, 2, tile)
            v_ref[tile, at, LANES:] = jnp.ones((rows, LANES), BF16)

    for r in range(count):
        block = place(me, r)
        label = labels_of(row + block * rows, len_ref)
        extra = jnp.where((lane == 0.0) | (lane == label + 1.0), 1.0, 0.0).astype(BF16)
        for tile in range(tiles):
            unit = unit_tile(tile_of(r, 0, tile), low)
            parts = []
            for side in range(min(2, heads)):
                head = tile * 2 + side
                kept = jnp.where(low if side == 0 else ~low, unit, 0.0).astype(BF16)
                query = jnp.concatenate([kept, extra], axis=1)
                scores = lax.dot_general(
                    query, k_ref[tile], (((1,), (1,)), ((), ())), preferred_element_type=F32
                )
                weights = jnp.exp2(scores * (scale_ref[head] * LOG2E)).astype(BF16)
                summed = jnp.dot(weights, v_ref[tile], preferred_element_type=F32)
                parts.append(summed[:, 0:LANES] / summed[:, LANES:])
            done = parts[0] if len(parts) == 1 else jnp.where(low, parts[0], parts[1])
            start = pl.multiple_of(HALO + block * rows, HALO)
            wide = min(LANES, width)
            a_ref[pl.ds(start, rows), tile * LANES : tile * LANES + wide] = done[:, 0:wide].astype(BF16)

    for r in range(count):
        target = place(me, r)
        for o_ref, block in ((oa_refs[r], target ^ half), (ob_refs[r], target)):
            o_ref[...] = a_ref[pl.ds(pl.multiple_of(block * rows, HALO), window), :]


def normalize(values):
    average = jnp.mean(values, axis=-1, keepdims=True)
    centered = values - average
    spread = jnp.mean(centered * centered, axis=-1, keepdims=True)
    return centered * lax.rsqrt(spread + 1e-05)


def frame_kernel(
    count,
    rows,
    experts,
    capacity,
    place,
    flip,
    me_ref,
    expert_ref,
    len_ref,
    proj_ref,
    taps_ref,
    router_ref,
    routes_ref,
    turned_ref,
    *refs,
):
    att_refs, out_refs = refs[:count], refs[count : count + experts]
    info_ref, second_ref, x_ref, first_ref, lab_ref = refs[count + experts :]
    me = me_ref[0]
    width = att_refs[0].shape[1]
    window = rows + 2 * HALO
    half = (KERNEL - 1) // 2
    tiles = D // LANES
    step = 56
    first = jnp.zeros((window, D), F32)
    for r in range(count):
        begin = pl.multiple_of(place(me, r) * width, HEAD_DIM)
        first = first + jnp.dot(
            att_refs[r][...], proj_ref[pl.ds(begin, width), :], preferred_element_type=F32
        )
    normed = normalize(first).astype(BF16).astype(F32)
    origin = (me ^ flip) * rows
    frames = lax.broadcasted_iota(jnp.int32, (window, LANES), 0) + (origin - HALO)
    lab_ref[...] = labels_of(frames, len_ref)
    for tile in range(tiles):
        at = slice(tile * LANES, (tile + 1) * LANES)
        x_ref[tile] = normed[:, at]
        first_ref[tile] = first[HALO : HALO + rows, at]

    starts = [len_ref[0, 0], len_ref[0, 0] + len_ref[0, 1]]
    starts.append(starts[1] + len_ref[0, 2])
    for begin in range(0, rows, step):
        low = origin + begin - half
        high = low + step + 2 * half
        crossed = functools.reduce(
            jnp.logical_or, [(low < start) & (start < high) for start in starts]
        )

        def columns(tile, masked):
            total = jnp.zeros((step, LANES), F32)
            own = lab_ref[HALO + begin : HALO + begin + step, :] if masked else None
            for tap in range(KERNEL):
                source = HALO - half + begin + tap
                term = taps_ref[tile, tap : tap + 1, :] * x_ref[tile, source : source + step, :]
                if masked:
                    term = jnp.where(lab_ref[source : source + step, :] == own, term, 0.0)
                total = total + term
            gated = total / (1.0 + jnp.exp(-total))
            second_ref[tile, begin : begin + step, :] = (
                first_ref[tile, begin : begin + step, :] + gated
            )

        @pl.when(crossed)
        def _():
            lax.fori_loop(0, tiles, lambda tile, c: (columns(tile, True), c)[1], 0)

        @pl.when(jnp.logical_not(crossed))
        def _():
            lax.fori_loop(0, tiles, lambda tile, c: (columns(tile, False), c)[1], 0)

    second = jnp.concatenate([second_ref[tile] for tile in range(tiles)], axis=1)
    mixed = normalize(second).astype(BF16)

    logits = jnp.dot(mixed, router_ref[...], preferred_element_type=F32)
    lane = lax.broadcasted_iota(jnp.int32, (rows, experts), 1)
    named = [lane == routes_ref[:, pick : pick + 1] for pick in range(TOPK)]
    picked = [jnp.sum(jnp.where(one, logits, 0.0), axis=1, keepdims=True) for one in named]
    top = jnp.maximum(picked[0], picked[1])
    raised = [jnp.exp(one - top) for one in picked]
    mass = raised[0] + raised[1]
    down = lax.broadcasted_iota(jnp.int32, (rows, rows), 0)
    across = lax.broadcasted_iota(jnp.int32, (rows, rows), 1)
    picks = jnp.where(named[0] | named[1], 1.0, 0.0).astype(BF16)
    earlier = jnp.where(across < down, 1.0, 0.0).astype(BF16)
    ranks = jnp.dot(earlier, picks, preferred_element_type=F32)
    column = lax.broadcasted_iota(jnp.int32, (rows, LANES), 1)
    info = jnp.zeros((rows, LANES), F32)
    for pick in range(TOPK):
        rank = jnp.sum(jnp.where(named[pick], ranks, 0.0), axis=1, keepdims=True)
        place_of = routes_ref[:, pick : pick + 1] ^ expert_ref[0]
        slot = rank + (place_of * capacity).astype(F32)
        info = jnp.where(column == pick, slot, info)
        info = jnp.where(column == TOPK + pick, raised[pick] / mass, info)
    info_ref[...] = info

    expert = lax.broadcasted_iota(jnp.int32, (experts, rows), 0) ^ expert_ref[0]
    chosen = (expert == turned_ref[0:1, :]) | (expert == turned_ref[1:2, :])
    later = jnp.where(down < across, 1.0, 0.0).astype(BF16)
    order = jnp.dot(jnp.where(chosen, 1.0, 0.0).astype(BF16), later, preferred_element_type=F32)
    order = jnp.where(chosen, order, -1.0)
    slot = lax.broadcasted_iota(jnp.int32, (capacity, rows), 0).astype(F32)
    for e in range(0, experts, 2):
        select = jnp.concatenate(
            [jnp.where(slot == order[e + k : e + k + 1, :], 1.0, 0.0) for k in range(2)], axis=0
        ).astype(BF16)
        moved = jnp.dot(select, mixed, preferred_element_type=F32)
        out_refs[e][...] = moved[0:capacity].astype(BF16)
        out_refs[e + 1][...] = moved[capacity:].astype(BF16)


def joined(left_ref, right_ref):
    both = [left_ref[...].astype(F32), right_ref[...].astype(F32)]
    return jnp.concatenate(both, axis=0).astype(BF16)


def expert_kernel(experts, pieces, *refs):
    x_refs, refs = refs[:experts], refs[experts:]
    ins, outs, o_refs = refs[:pieces], refs[pieces : 2 * pieces], refs[2 * pieces :]
    capacity = x_refs[0].shape[0]
    for e in range(0, experts, 2):
        tokens = joined(x_refs[e], x_refs[e + 1])
        total = jnp.zeros((2 * capacity, D), F32)
        for piece_in, piece_out in zip(ins, outs):
            raw = lax.dot_general(
                tokens, piece_in[...], (((1,), (1,)), ((), ())), preferred_element_type=F32
            )
            hidden = (raw / (1.0 + jnp.exp(-raw))).astype(BF16)
            total = total + jnp.dot(hidden, piece_out[...], preferred_element_type=F32)
        o_refs[e][...] = total[0:capacity].astype(BF16)
        o_refs[e + 1][...] = total[capacity:].astype(BF16)


def mixture_of(info, back_refs):
    capacity = back_refs[0].shape[0]
    total = jnp.zeros((info.shape[0], D), F32)
    column = lax.broadcasted_iota(jnp.int32, (info.shape[0], 2 * capacity), 1).astype(F32)
    for e in range(0, len(back_refs), 2):
        spread = jnp.where(column == info[:, 0:1] - e * capacity, info[:, 2:3], 0.0)
        spread = jnp.where(column == info[:, 1:2] - e * capacity, info[:, 3:4], spread)
        total = total + jnp.dot(
            spread.astype(BF16), joined(back_refs[e], back_refs[e + 1]), preferred_element_type=F32
        )
    return total


def theirs_kernel(info_ref, *refs):
    refs[-1][...] = mixture_of(info_ref[...], refs[:-1]).astype(BF16)


def mine_kernel(info_ref, second_ref, part_ref, *refs):
    o_ref = refs[-1]
    mixture = mixture_of(info_ref[...], refs[:-1])
    for tile in range(D // LANES):
        at = slice(tile * LANES, (tile + 1) * LANES)
        both = mixture[:, at] + part_ref[:, at].astype(F32)
        o_ref[:, at] = (second_ref[tile] + 0.5 * both).astype(BF16)


def crossed(count, direct, me, r):
    return me ^ r if direct else r


def trade(arrays, axis, direct=True):
    count = len(arrays)
    if not direct:
        mixed = lax.all_to_all(jnp.stack(arrays), axis, split_axis=0, concat_axis=0, tiled=True)
        return [mixed[r] for r in range(count)]
    moved = {
        r: lax.ppermute(arrays[r], axis, [(i, i ^ r) for i in range(count)])
        for r in range(count - 1, 0, -1)
    }
    return [arrays[0]] + [moved[r] for r in range(1, count)]


def tied(arrays, marker):
    return lax.optimization_barrier((*arrays, marker))[:-1]


def body(
    query_rows,
    key_rows,
    value_rows,
    head_scale,
    out_proj,
    conv_taps,
    router,
    expert_in,
    expert_out,
    lengths,
    routes,
):
    rows = query_rows.shape[1]
    experts = lax.axis_size("dp")
    count = lax.axis_size("tm")
    half = count // 2
    heads = HEADS // count
    width = heads * HEAD_DIM
    window = rows + 2 * HALO
    capacity = -(-(3 * rows // experts) // 8) * 8
    direct = width % LANES == 0
    me = lax.axis_index("tm").astype(jnp.int32).reshape(1)
    expert = lax.axis_index("dp").astype(jnp.int32).reshape(1)
    partner = [(i, i ^ half) for i in range(count)]
    place = functools.partial(crossed, count, direct)

    packed = pl.pallas_call(
        functools.partial(pack_kernel, place),
        out_shape=(jax.ShapeDtypeStruct((3, rows, width), BF16),) * count,
        in_specs=[VMEM, VMEM, VMEM, SMEM],
        out_specs=(VMEM,) * count,
        compiler_params=params(16),
        cost_estimate=cost(1),
        name="pack",
    )(query_rows[0], key_rows[0], value_rows[0], me)
    arrived = trade(packed, "tm", direct)
    scales = lax.dynamic_slice_in_dim(head_scale, me[0] * heads, heads)
    partner_routes = lax.ppermute(routes[0], "tm", partner)

    tiles = max(1, width // LANES)
    total = count * rows
    sent = jax.ShapeDtypeStruct((window, width), BF16)
    attended = pl.pallas_call(
        functools.partial(attend_kernel, count, rows, heads, place),
        out_shape=(sent,) * (2 * count),
        in_specs=[SMEM, SMEM, SMEM] + [VMEM] * count,
        out_specs=(VMEM,) * (2 * count),
        scratch_shapes=[
            pltpu.VMEM((tiles, total, 2 * LANES), BF16),
            pltpu.VMEM((tiles, total, 2 * LANES), BF16),
            pltpu.VMEM((total + 2 * HALO, width), BF16),
        ],
        compiler_params=params(32),
        cost_estimate=cost(1),
        name="attend",
    )(me, scales, lengths, *arrived)
    gathered_a = trade(attended[:count], "tm", direct)
    gathered_b = trade(attended[count:], "tm", direct)

    if half == 2:
        swap = [(i, i ^ 1) for i in range(count)]
        units = expert_in.shape[1]
        cut = units // 2
        (early,) = tied((expert_in[0, :cut],), packed[1])
        late = tied((expert_in[0, cut:], expert_out[0, :cut], expert_out[0, cut:]), gathered_a[-1])
        moved = [lax.ppermute(one, "tm", swap) for one in (early, *late)]
        ins = [expert_in[0], moved[0], moved[1]]
        outs = [expert_out[0], moved[2], moved[3]]
    else:
        groups = [list(range(half)), list(range(half, count))]
        ins = [lax.all_gather(expert_in[0], "tm", axis=0, tiled=True, axis_index_groups=groups)]
        outs = [lax.all_gather(expert_out[0], "tm", axis=0, tiled=True, axis_index_groups=groups)]

    taps = jnp.transpose(conv_taps.reshape(KERNEL, D // LANES, LANES), (1, 0, 2))
    pieces = len(ins)
    chunk = jax.ShapeDtypeStruct((capacity, D), BF16)

    def send_frames(windows, flip, block_routes):
        made = pl.pallas_call(
            functools.partial(frame_kernel, count, rows, experts, capacity, place, flip),
            out_shape=(chunk,) * experts
            + (
                jax.ShapeDtypeStruct((rows, LANES), F32),
                jax.ShapeDtypeStruct((D // LANES, rows, LANES), F32),
            ),
            in_specs=[SMEM, SMEM, SMEM] + [VMEM] * (5 + count),
            out_specs=(VMEM,) * (experts + 2),
            scratch_shapes=[
                pltpu.VMEM((D // LANES, window, LANES), F32),
                pltpu.VMEM((D // LANES, rows, LANES), F32),
                pltpu.VMEM((window, LANES), F32),
            ],
            compiler_params=params(32),
            cost_estimate=cost(1),
            name="frames",
        )(me, expert, lengths, out_proj, taps, router, block_routes, block_routes.T, *windows)
        return trade(made[:experts], "dp"), made[experts], made[experts + 1]

    def run_expert(tokens):
        produced = pl.pallas_call(
            functools.partial(expert_kernel, experts, pieces),
            out_shape=(chunk,) * experts,
            in_specs=[VMEM] * (experts + 2 * pieces),
            out_specs=(VMEM,) * experts,
            compiler_params=params(32),
            cost_estimate=cost(1),
            name="experts",
        )(*tokens, *ins, *outs)
        return trade(produced, "dp")

    tokens_a, info_a, _ = send_frames(gathered_a, half, partner_routes)
    tokens_b, info_b, second = send_frames(gathered_b, 0, routes[0])
    back_a = run_expert(tokens_a)
    back_b = run_expert(tokens_b)

    theirs = pl.pallas_call(
        theirs_kernel,
        out_shape=jax.ShapeDtypeStruct((rows, D), BF16),
        in_specs=[VMEM] * (1 + experts),
        out_specs=VMEM,
        compiler_params=params(24),
        cost_estimate=cost(1),
        name="theirs",
    )(info_a, *back_a)
    received = lax.ppermute(theirs, "tm", partner)
    out = pl.pallas_call(
        mine_kernel,
        out_shape=jax.ShapeDtypeStruct((rows, D), BF16),
        in_specs=[VMEM] * (3 + experts),
        out_specs=VMEM,
        compiler_params=params(24),
        cost_estimate=cost(1),
        name="mine",
    )(info_b, second, received, *back_b)
    return out[None]


def solution(mesh):
    return jax.shard_map(
        body,
        mesh=mesh,
        in_specs=(
            P("dp", "tm", None),
            P("dp", "tm", None),
            P("dp", "tm", None),
            P(),
            P(),
            P(),
            P(),
            P("dp", "tm", None),
            P("dp", "tm", None),
            P("dp", None),
            P("dp", "tm", None),
        ),
        out_specs=P("dp", "tm", None),
        check_vma=False,
    )
```

```python
import functools

import jax
import jax.numpy as jnp
from jax import lax
from jax.experimental import pallas as pl
from jax.experimental.pallas import tpu as pltpu
from jax.sharding import PartitionSpec as P

D = 1536
HEADS = 16
HEAD_DIM = 64
KERNEL = 31
TOPK = 2
RECS = 4
HALO = 16
LANES = 128
APART = 64.0
LOG2E = 1.4426950408889634
F32 = jnp.float32
BF16 = jnp.bfloat16
VMEM = pl.BlockSpec(memory_space=pltpu.VMEM)
SMEM = pl.BlockSpec(memory_space=pltpu.SMEM)


def params(mib):
    return pltpu.CompilerParams(vmem_limit_bytes=mib << 20)


def cost(micros):
    return pl.CostEstimate(flops=micros * 1_100_000_000, bytes_accessed=0, transcendentals=0)


def labels_of(frames, len_ref):
    first = len_ref[0, 0]
    second = first + len_ref[0, 1]
    third = second + len_ref[0, 2]
    return (
        (frames >= first).astype(F32)
        + (frames >= second).astype(F32)
        + (frames >= third).astype(F32)
    )


def unit_tile(tile, low):
    lifted = tile.astype(F32)
    square = lifted * lifted
    left = jnp.sum(jnp.where(low, square, 0.0), axis=1, keepdims=True)
    right = jnp.sum(jnp.where(low, 0.0, square), axis=1, keepdims=True)
    factor = jnp.where(low, lax.rsqrt(left + 1e-06), lax.rsqrt(right + 1e-06))
    return lifted * factor


def pack_kernel(place, me_ref, q_ref, k_ref, v_ref, *refs):
    o_refs, sem_ref = refs[:-1], refs[-1]
    width = o_refs[0].shape[2]
    copies = []
    for r in range(len(o_refs) - 1, -1, -1):
        target = place(me_ref[0], r)
        for which, ref in enumerate((q_ref, k_ref, v_ref)):
            if width % LANES == 0:
                columns = pl.ds(pl.multiple_of(target * width, LANES), width)
                copy = pltpu.make_async_copy(
                    ref.at[:, columns], o_refs[r].at[which], sem_ref.at[r * 3 + which]
                )
                copy.start()
                copies.append(copy)
            else:
                o_refs[r][which] = ref[:, target * width : (target + 1) * width]
    for copy in copies:
        copy.wait()


def attend_kernel(count, rows, heads, place, me_ref, scale_ref, len_ref, *refs):
    x_refs, oa_refs, ob_refs = refs[:count], refs[count : 2 * count], refs[2 * count : 3 * count]
    k_ref, v_ref, a_ref = refs[3 * count :]
    me = me_ref[0]
    width = heads * HEAD_DIM
    tiles = max(1, width // LANES)
    half = count // 2
    window = rows + 2 * HALO

    def tile_of(r, which, tile):
        if width >= LANES:
            return x_refs[r][which, :, tile * LANES : (tile + 1) * LANES]
        piece = x_refs[r][which]
        return jnp.concatenate([piece, jnp.zeros((rows, LANES - width), BF16)], axis=1)

    low = lax.broadcasted_iota(jnp.int32, (rows, LANES), 1) < HEAD_DIM
    lane = lax.broadcasted_iota(jnp.int32, (rows, LANES), 1).astype(F32)
    row = lax.broadcasted_iota(jnp.int32, (rows, LANES), 0)

    edge = jnp.zeros((HALO, width), BF16)
    a_ref[0:HALO, :] = edge
    a_ref[HALO + count * rows :, :] = edge
    for r in range(count):
        at = slice(r * rows, (r + 1) * rows)
        label = labels_of(row + place(me, r) * rows, len_ref)
        other = jnp.where((lane >= 1.0) & (lane <= 4.0) & (lane != label + 1.0), -APART, 0.0)
        extra = jnp.where(lane == 0.0, -1.0, other).astype(BF16)
        for tile in range(tiles):
            k_ref[tile, at, 0:LANES] = unit_tile(tile_of(r, 1, tile), low).astype(BF16)
            k_ref[tile, at, LANES:] = extra
            v_ref[tile, at, 0:LANES] = tile_of(r, 2, tile)
            v_ref[tile, at, LANES:] = jnp.ones((rows, LANES), BF16)

    for r in range(count):
        block = place(me, r)
        label = labels_of(row + block * rows, len_ref)
        extra = jnp.where((lane == 0.0) | (lane == label + 1.0), 1.0, 0.0).astype(BF16)
        for tile in range(tiles):
            unit = unit_tile(tile_of(r, 0, tile), low)
            parts = []
            for side in range(min(2, heads)):
                head = tile * 2 + side
                kept = jnp.where(low if side == 0 else ~low, unit, 0.0).astype(BF16)
                query = jnp.concatenate([kept, extra], axis=1)
                scores = lax.dot_general(
                    query, k_ref[tile], (((1,), (1,)), ((), ())), preferred_element_type=F32
                )
                weights = jnp.exp2(scores * (scale_ref[head] * LOG2E)).astype(BF16)
                summed = jnp.dot(weights, v_ref[tile], preferred_element_type=F32)
                parts.append(summed[:, 0:LANES] / summed[:, LANES:])
            done = parts[0] if len(parts) == 1 else jnp.where(low, parts[0], parts[1])
            start = pl.multiple_of(HALO + block * rows, HALO)
            wide = min(LANES, width)
            a_ref[pl.ds(start, rows), tile * LANES : tile * LANES + wide] = done[:, 0:wide].astype(BF16)

    for r in range(count):
        target = place(me, r)
        for o_ref, block in ((oa_refs[r], target ^ half), (ob_refs[r], target)):
            o_ref[...] = a_ref[pl.ds(pl.multiple_of(block * rows, HALO), window), :]


def normalize(values):
    average = jnp.mean(values, axis=-1, keepdims=True)
    centered = values - average
    spread = jnp.mean(centered * centered, axis=-1, keepdims=True)
    return centered * lax.rsqrt(spread + 1e-05)


def frame_kernel(
    count,
    rows,
    experts,
    capacity,
    place,
    flip,
    me_ref,
    expert_ref,
    len_ref,
    proj_ref,
    taps_ref,
    router_ref,
    routes_ref,
    turned_ref,
    *refs,
):
    att_refs, out_refs = refs[:count], refs[count:-5]
    info_ref, second_ref, x_ref, first_ref, lab_ref = refs[-5:]
    me = me_ref[0]
    turn = expert_ref[0] if len(out_refs) > 1 else 0
    width = att_refs[0].shape[1]
    window = rows + 2 * HALO
    half = (KERNEL - 1) // 2
    tiles = D // LANES
    step = 56
    first = jnp.zeros((window, D), F32)
    for r in range(count):
        begin = pl.multiple_of(place(me, r) * width, HEAD_DIM)
        first = first + jnp.dot(
            att_refs[r][...], proj_ref[pl.ds(begin, width), :], preferred_element_type=F32
        )
    normed = normalize(first).astype(BF16).astype(F32)
    origin = (me ^ flip) * rows
    frames = lax.broadcasted_iota(jnp.int32, (window, LANES), 0) + (origin - HALO)
    lab_ref[...] = labels_of(frames, len_ref)
    for tile in range(tiles):
        at = slice(tile * LANES, (tile + 1) * LANES)
        x_ref[tile] = normed[:, at]
        first_ref[tile] = first[HALO : HALO + rows, at]

    starts = [len_ref[0, 0], len_ref[0, 0] + len_ref[0, 1]]
    starts.append(starts[1] + len_ref[0, 2])
    for begin in range(0, rows, step):
        low = origin + begin - half
        high = low + step + 2 * half
        crossed = functools.reduce(
            jnp.logical_or, [(low < start) & (start < high) for start in starts]
        )

        def columns(tile, masked):
            total = jnp.zeros((step, LANES), F32)
            own = lab_ref[HALO + begin : HALO + begin + step, :] if masked else None
            for tap in range(KERNEL):
                source = HALO - half + begin + tap
                term = taps_ref[tile, tap : tap + 1, :] * x_ref[tile, source : source + step, :]
                if masked:
                    term = jnp.where(lab_ref[source : source + step, :] == own, term, 0.0)
                total = total + term
            gated = total / (1.0 + jnp.exp(-total))
            second_ref[tile, begin : begin + step, :] = (
                first_ref[tile, begin : begin + step, :] + gated
            )

        @pl.when(crossed)
        def _():
            lax.fori_loop(0, tiles, lambda tile, c: (columns(tile, True), c)[1], 0)

        @pl.when(jnp.logical_not(crossed))
        def _():
            lax.fori_loop(0, tiles, lambda tile, c: (columns(tile, False), c)[1], 0)

    second = jnp.concatenate([second_ref[tile] for tile in range(tiles)], axis=1)
    mixed = normalize(second).astype(BF16)

    logits = jnp.dot(mixed, router_ref[...], preferred_element_type=F32)
    lane = lax.broadcasted_iota(jnp.int32, (rows, experts), 1)
    named = [lane == routes_ref[:, pick : pick + 1] for pick in range(TOPK)]
    picked = [jnp.sum(jnp.where(one, logits, 0.0), axis=1, keepdims=True) for one in named]
    top = jnp.maximum(picked[0], picked[1])
    raised = [jnp.exp(one - top) for one in picked]
    mass = raised[0] + raised[1]
    down = lax.broadcasted_iota(jnp.int32, (rows, rows), 0)
    across = lax.broadcasted_iota(jnp.int32, (rows, rows), 1)
    picks = jnp.where(named[0] | named[1], 1.0, 0.0).astype(BF16)
    earlier = jnp.where(across < down, 1.0, 0.0).astype(BF16)
    ranks = jnp.dot(earlier, picks, preferred_element_type=F32)
    column = lax.broadcasted_iota(jnp.int32, (rows, LANES), 1)
    info = jnp.zeros((rows, LANES), F32)
    for pick in range(TOPK):
        rank = jnp.sum(jnp.where(named[pick], ranks, 0.0), axis=1, keepdims=True)
        place_of = routes_ref[:, pick : pick + 1] ^ turn
        slot = rank + (place_of * capacity).astype(F32)
        info = jnp.where(column == pick, slot, info)
        info = jnp.where(column == TOPK + pick, raised[pick] / mass, info)
    info_ref[...] = info

    expert = lax.broadcasted_iota(jnp.int32, (experts, rows), 0) ^ turn
    chosen = (expert == turned_ref[0:1, :]) | (expert == turned_ref[1:2, :])
    later = jnp.where(down < across, 1.0, 0.0).astype(BF16)
    order = jnp.dot(jnp.where(chosen, 1.0, 0.0).astype(BF16), later, preferred_element_type=F32)
    order = jnp.where(chosen, order, -1.0)
    slot = lax.broadcasted_iota(jnp.int32, (capacity, rows), 0).astype(F32)
    select = jnp.concatenate(
        [jnp.where(slot == order[e : e + 1, :], 1.0, 0.0) for e in range(experts)], axis=0
    ).astype(BF16)
    scatter(out_refs, jnp.dot(select, mixed, preferred_element_type=F32))


def joined(refs):
    if len(refs) == 1:
        return refs[0][...]
    return jnp.concatenate([ref[...].astype(F32) for ref in refs], axis=0).astype(BF16)


def scatter(refs, values):
    tall = values.shape[0] // len(refs)
    for e, ref in enumerate(refs):
        ref[...] = values[e * tall : (e + 1) * tall].astype(BF16)


def expert_kernel(chunks, me_ref, in_ref, *refs):
    x_refs, out_refs, o_refs = refs[:chunks], refs[chunks:-chunks], refs[-chunks:]
    tokens = joined(x_refs)
    total = jnp.zeros((tokens.shape[0], D), F32)
    units = out_refs[0].shape[0]
    for place, out_ref in enumerate(out_refs):
        begin = 0 if len(out_refs) == 1 else pl.multiple_of(((me_ref[0] & 1) ^ place) * units, 16)
        raw = lax.dot_general(
            tokens,
            in_ref[pl.ds(begin, units), :],
            (((1,), (1,)), ((), ())),
            preferred_element_type=F32,
        )
        hidden = (raw / (1.0 + jnp.exp(-raw))).astype(BF16)
        total = total + jnp.dot(hidden, out_ref[...], preferred_element_type=F32)
    scatter(o_refs, total)


def mixture_of(info, back_refs):
    back = joined(back_refs)
    column = lax.broadcasted_iota(jnp.int32, (info.shape[0], back.shape[0]), 1).astype(F32)
    spread = jnp.where(column == info[:, 0:1], info[:, 2:3], 0.0)
    spread = jnp.where(column == info[:, 1:2], info[:, 3:4], spread).astype(BF16)
    return jnp.dot(spread, back, preferred_element_type=F32)


def theirs_kernel(info_ref, *refs):
    refs[-1][...] = mixture_of(info_ref[...], refs[:-1]).astype(BF16)


def mine_kernel(info_ref, second_ref, part_ref, *refs):
    o_ref = refs[-1]
    mixture = mixture_of(info_ref[...], refs[:-1])
    for tile in range(D // LANES):
        at = slice(tile * LANES, (tile + 1) * LANES)
        both = mixture[:, at] + part_ref[:, at].astype(F32)
        o_ref[:, at] = (second_ref[tile] + 0.5 * both).astype(BF16)


def crossed(count, direct, me, r):
    return me ^ r if direct else r


def trade(arrays, axis, direct=True):
    count = len(arrays)
    if not direct:
        mixed = lax.all_to_all(jnp.stack(arrays), axis, split_axis=0, concat_axis=0, tiled=True)
        return [mixed[r] for r in range(count)]
    moved = {
        r: lax.ppermute(arrays[r], axis, [(i, i ^ r) for i in range(count)])
        for r in range(count - 1, 0, -1)
    }
    return [arrays[0]] + [moved[r] for r in range(1, count)]


def tied(arrays, marker):
    return lax.optimization_barrier((*arrays, marker))[:-1]


def body(
    query_rows,
    key_rows,
    value_rows,
    head_scale,
    out_proj,
    conv_taps,
    router,
    expert_in,
    expert_out,
    lengths,
    routes,
):
    rows = query_rows.shape[1]
    experts = lax.axis_size("dp")
    count = lax.axis_size("tm")
    half = count // 2
    heads = HEADS // count
    width = heads * HEAD_DIM
    window = rows + 2 * HALO
    capacity = -(-(3 * rows // experts) // 8) * 8
    direct = width % LANES == 0
    me = lax.axis_index("tm").astype(jnp.int32).reshape(1)
    expert = lax.axis_index("dp").astype(jnp.int32).reshape(1)
    partner = [(i, i ^ half) for i in range(count)]
    place = functools.partial(crossed, count, direct)

    packed = pl.pallas_call(
        functools.partial(pack_kernel, place),
        out_shape=(jax.ShapeDtypeStruct((3, rows, width), BF16),) * count,
        in_specs=[SMEM] + [pl.BlockSpec(memory_space=pltpu.HBM) if direct else VMEM] * 3,
        out_specs=(VMEM,) * count,
        scratch_shapes=[pltpu.SemaphoreType.DMA((3 * count,))],
        compiler_params=params(60),
        cost_estimate=cost(1),
        name="pack",
    )(me, query_rows[0], key_rows[0], value_rows[0])
    arrived = trade(packed, "tm", direct)
    scales = lax.dynamic_slice_in_dim(head_scale, me[0] * heads, heads)
    partner_routes = lax.ppermute(routes[0], "tm", partner)

    tiles = max(1, width // LANES)
    total = count * rows
    sent = jax.ShapeDtypeStruct((window, width), BF16)
    attended = pl.pallas_call(
        functools.partial(attend_kernel, count, rows, heads, place),
        out_shape=(sent,) * (2 * count),
        in_specs=[SMEM, SMEM, SMEM] + [VMEM] * count,
        out_specs=(VMEM,) * (2 * count),
        scratch_shapes=[
            pltpu.VMEM((tiles, total, 2 * LANES), BF16),
            pltpu.VMEM((tiles, total, 2 * LANES), BF16),
            pltpu.VMEM((total + 2 * HALO, width), BF16),
        ],
        compiler_params=params(16),
        cost_estimate=cost(6),
        name="attend",
    )(me, scales, lengths, *arrived)
    gathered_a = trade(attended[:count], "tm", direct)
    gathered_b = trade(attended[count:], "tm", direct)

    groups = [list(range(i, i + half)) for i in (0, half)]
    (early,) = tied((expert_in[0],), arrived[-1])
    (late,) = tied((expert_out[0],), gathered_a[-1])
    ins = lax.all_gather(early, "tm", axis=0, tiled=True, axis_index_groups=groups)
    if half == 2:
        outs = [late, lax.ppermute(late, "tm", [(i, i ^ 1) for i in range(count)])]
    else:
        outs = [lax.all_gather(late, "tm", axis=0, tiled=True, axis_index_groups=groups)]

    taps = jnp.transpose(conv_taps.reshape(KERNEL, D // LANES, LANES), (1, 0, 2))
    slots = experts * capacity

    def chunks_of(split):
        if split:
            return (jax.ShapeDtypeStruct((capacity, D), BF16),) * experts
        return (jax.ShapeDtypeStruct((slots, D), BF16),)

    def route(arrays):
        if len(arrays) > 1:
            return trade(arrays, "dp")
        whole = arrays[0].reshape(experts, capacity, D)
        moved = lax.all_to_all(whole, "dp", split_axis=0, concat_axis=0, tiled=True)
        return [moved.reshape(slots, D)]

    def send_frames(windows, flip, split, block_routes):
        chunks = chunks_of(split)
        made = pl.pallas_call(
            functools.partial(frame_kernel, count, rows, experts, capacity, place, flip),
            out_shape=chunks
            + (
                jax.ShapeDtypeStruct((rows, LANES), F32),
                jax.ShapeDtypeStruct((D // LANES, rows, LANES), F32),
            ),
            in_specs=[SMEM, SMEM, SMEM] + [VMEM] * (5 + count),
            out_specs=(VMEM,) * (len(chunks) + 2),
            scratch_shapes=[
                pltpu.VMEM((D // LANES, window, LANES), F32),
                pltpu.VMEM((D // LANES, rows, LANES), F32),
                pltpu.VMEM((window, LANES), F32),
            ],
            compiler_params=params(24),
            cost_estimate=cost(10),
            name="frames",
        )(me, expert, lengths, out_proj, taps, router, block_routes, block_routes.T, *windows)
        return made[:-2], made[-2], made[-1]

    def run_expert(tokens):
        split = len(tokens) > 1
        chunks = chunks_of(split)
        produced = pl.pallas_call(
            functools.partial(expert_kernel, len(tokens)),
            out_shape=chunks,
            in_specs=[SMEM] + [VMEM] * (1 + len(tokens) + len(outs)),
            out_specs=(VMEM,) * len(chunks),
            compiler_params=params(24),
            cost_estimate=cost(8),
            name="experts",
        )(me, ins, *tokens, *outs)
        return produced

    outgoing_a, info_a, _ = send_frames(gathered_a, half, False, partner_routes)
    tokens_a = route(outgoing_a)
    gathered_b = tied(gathered_b, outgoing_a[0])
    outgoing_b, info_b, second = send_frames(gathered_b, 0, True, routes[0])
    tokens_b = route(outgoing_b)
    produced_a = run_expert(tokens_a)
    back_a = route(produced_a)
    tokens_b = tied(tokens_b, produced_a[0])
    back_b = route(run_expert(tokens_b))

    theirs = pl.pallas_call(
        theirs_kernel,
        out_shape=jax.ShapeDtypeStruct((rows, D), BF16),
        in_specs=[VMEM] * (1 + len(back_a)),
        out_specs=VMEM,
        compiler_params=params(16),
        cost_estimate=cost(1),
        name="theirs",
    )(info_a, *back_a)
    received = lax.ppermute(theirs, "tm", partner)
    out = pl.pallas_call(
        mine_kernel,
        out_shape=jax.ShapeDtypeStruct((rows, D), BF16),
        in_specs=[VMEM] * (3 + len(back_b)),
        out_specs=VMEM,
        compiler_params=params(16),
        cost_estimate=cost(1),
        name="mine",
    )(info_b, second, received, *back_b)
    return out[None]


def solution(mesh):
    return jax.shard_map(
        body,
        mesh=mesh,
        in_specs=(
            P("dp", "tm", None),
            P("dp", "tm", None),
            P("dp", "tm", None),
            P(),
            P(),
            P(),
            P(),
            P("dp", "tm", None),
            P("dp", "tm", None),
            P("dp", None),
            P("dp", "tm", None),
        ),
        out_specs=P("dp", "tm", None),
        check_vma=False,
    )
```

```python
import functools

import jax
import jax.numpy as jnp
from jax import lax
from jax.experimental import pallas as pl
from jax.experimental.pallas import tpu as pltpu
from jax.sharding import PartitionSpec as P

D = 1536
HEADS = 16
HEAD_DIM = 64
KERNEL = 31
TOPK = 2
RECS = 4
HALO = 16
LANES = 128
APART = 64.0
LOG2E = 1.4426950408889634
F32 = jnp.float32
BF16 = jnp.bfloat16
VMEM = pl.BlockSpec(memory_space=pltpu.VMEM)
SMEM = pl.BlockSpec(memory_space=pltpu.SMEM)


def params(mib):
    return pltpu.CompilerParams(vmem_limit_bytes=mib << 20)


def cost(micros):
    return pl.CostEstimate(flops=micros * 1_100_000_000, bytes_accessed=0, transcendentals=0)


def labels_of(frames, len_ref):
    first = len_ref[0, 0]
    second = first + len_ref[0, 1]
    third = second + len_ref[0, 2]
    return (
        (frames >= first).astype(F32)
        + (frames >= second).astype(F32)
        + (frames >= third).astype(F32)
    )


def unit_tile(tile, low):
    lifted = tile.astype(F32)
    square = lifted * lifted
    left = jnp.sum(jnp.where(low, square, 0.0), axis=1, keepdims=True)
    right = jnp.sum(jnp.where(low, 0.0, square), axis=1, keepdims=True)
    factor = jnp.where(low, lax.rsqrt(left + 1e-06), lax.rsqrt(right + 1e-06))
    return lifted * factor


def pack_kernel(place, me_ref, q_ref, k_ref, v_ref, *refs):
    o_refs, sem_ref = refs[:-1], refs[-1]
    width = o_refs[0].shape[2]
    copies = []
    for r in range(len(o_refs) - 1, -1, -1):
        target = place(me_ref[0], r)
        for which, ref in enumerate((q_ref, k_ref, v_ref)):
            if width % LANES == 0:
                columns = pl.ds(pl.multiple_of(target * width, LANES), width)
                copy = pltpu.make_async_copy(
                    ref.at[:, columns], o_refs[r].at[which], sem_ref.at[r * 3 + which]
                )
                copy.start()
                copies.append(copy)
            else:
                o_refs[r][which] = ref[:, target * width : (target + 1) * width]
    for copy in copies:
        copy.wait()


def attend_kernel(count, rows, heads, place, me_ref, scale_ref, len_ref, *refs):
    x_refs, oa_refs, ob_refs = refs[:count], refs[count : 2 * count], refs[2 * count : 3 * count]
    k_ref, v_ref, a_ref = refs[3 * count :]
    me = me_ref[0]
    width = heads * HEAD_DIM
    tiles = max(1, width // LANES)
    half = count // 2
    window = rows + 2 * HALO

    def tile_of(r, which, tile):
        if width >= LANES:
            return x_refs[r][which, :, tile * LANES : (tile + 1) * LANES]
        piece = x_refs[r][which]
        return jnp.concatenate([piece, jnp.zeros((rows, LANES - width), BF16)], axis=1)

    low = lax.broadcasted_iota(jnp.int32, (rows, LANES), 1) < HEAD_DIM
    lane = lax.broadcasted_iota(jnp.int32, (rows, LANES), 1).astype(F32)
    row = lax.broadcasted_iota(jnp.int32, (rows, LANES), 0)

    edge = jnp.zeros((HALO, width), BF16)
    a_ref[0:HALO, :] = edge
    a_ref[HALO + count * rows :, :] = edge
    for r in range(count):
        at = slice(r * rows, (r + 1) * rows)
        label = labels_of(row + place(me, r) * rows, len_ref)
        other = jnp.where((lane >= 1.0) & (lane <= 4.0) & (lane != label + 1.0), -APART, 0.0)
        extra = jnp.where(lane == 0.0, -1.0, other).astype(BF16)
        for tile in range(tiles):
            k_ref[tile, at, 0:LANES] = unit_tile(tile_of(r, 1, tile), low).astype(BF16)
            k_ref[tile, at, LANES:] = extra
            v_ref[tile, at, 0:LANES] = tile_of(r, 2, tile)
            v_ref[tile, at, LANES:] = jnp.ones((rows, LANES), BF16)

    for r in range(count):
        block = place(me, r)
        label = labels_of(row + block * rows, len_ref)
        extra = jnp.where((lane == 0.0) | (lane == label + 1.0), 1.0, 0.0).astype(BF16)
        for tile in range(tiles):
            unit = unit_tile(tile_of(r, 0, tile), low)
            parts = []
            for side in range(min(2, heads)):
                head = tile * 2 + side
                kept = jnp.where(low if side == 0 else ~low, unit, 0.0).astype(BF16)
                query = jnp.concatenate([kept, extra], axis=1)
                scores = lax.dot_general(
                    query, k_ref[tile], (((1,), (1,)), ((), ())), preferred_element_type=F32
                )
                weights = jnp.exp2(scores * (scale_ref[head] * LOG2E)).astype(BF16)
                summed = jnp.dot(weights, v_ref[tile], preferred_element_type=F32)
                parts.append(summed[:, 0:LANES] / summed[:, LANES:])
            done = parts[0] if len(parts) == 1 else jnp.where(low, parts[0], parts[1])
            start = pl.multiple_of(HALO + block * rows, HALO)
            wide = min(LANES, width)
            a_ref[pl.ds(start, rows), tile * LANES : tile * LANES + wide] = done[:, 0:wide].astype(BF16)

    for r in range(count):
        target = place(me, r)
        for o_ref, block in ((oa_refs[r], target ^ half), (ob_refs[r], target)):
            o_ref[...] = a_ref[pl.ds(pl.multiple_of(block * rows, HALO), window), :]


def normalize(values):
    average = jnp.mean(values, axis=-1, keepdims=True)
    centered = values - average
    spread = jnp.mean(centered * centered, axis=-1, keepdims=True)
    return centered * lax.rsqrt(spread + 1e-05)


def frame_kernel(
    count,
    rows,
    experts,
    capacity,
    place,
    flip,
    me_ref,
    expert_ref,
    len_ref,
    proj_ref,
    taps_ref,
    router_ref,
    routes_ref,
    turned_ref,
    *refs,
):
    att_refs, out_refs = refs[:count], refs[count:-5]
    info_ref, second_ref, x_ref, first_ref, lab_ref = refs[-5:]
    me = me_ref[0]
    turn = expert_ref[0] if len(out_refs) > 1 else 0
    width = att_refs[0].shape[1]
    window = rows + 2 * HALO
    half = (KERNEL - 1) // 2
    tiles = D // LANES
    step = 56
    first = jnp.zeros((window, D), F32)
    for r in range(count):
        begin = pl.multiple_of(place(me, r) * width, HEAD_DIM)
        first = first + jnp.dot(
            att_refs[r][...], proj_ref[pl.ds(begin, width), :], preferred_element_type=F32
        )
    normed = normalize(first).astype(BF16).astype(F32)
    origin = (me ^ flip) * rows
    frames = lax.broadcasted_iota(jnp.int32, (window, LANES), 0) + (origin - HALO)
    lab_ref[...] = labels_of(frames, len_ref)
    for tile in range(tiles):
        at = slice(tile * LANES, (tile + 1) * LANES)
        x_ref[tile] = normed[:, at]
        first_ref[tile] = first[HALO : HALO + rows, at]

    starts = [len_ref[0, 0], len_ref[0, 0] + len_ref[0, 1]]
    starts.append(starts[1] + len_ref[0, 2])
    for begin in range(0, rows, step):
        low = origin + begin - half
        high = low + step + 2 * half
        crossed = functools.reduce(
            jnp.logical_or, [(low < start) & (start < high) for start in starts]
        )

        def columns(tile, masked):
            total = jnp.zeros((step, LANES), F32)
            own = lab_ref[HALO + begin : HALO + begin + step, :] if masked else None
            for tap in range(KERNEL):
                source = HALO - half + begin + tap
                term = taps_ref[tile, tap : tap + 1, :] * x_ref[tile, source : source + step, :]
                if masked:
                    term = jnp.where(lab_ref[source : source + step, :] == own, term, 0.0)
                total = total + term
            gated = total / (1.0 + jnp.exp(-total))
            second_ref[tile, begin : begin + step, :] = (
                first_ref[tile, begin : begin + step, :] + gated
            )

        @pl.when(crossed)
        def _():
            lax.fori_loop(0, tiles, lambda tile, c: (columns(tile, True), c)[1], 0)

        @pl.when(jnp.logical_not(crossed))
        def _():
            lax.fori_loop(0, tiles, lambda tile, c: (columns(tile, False), c)[1], 0)

    second = jnp.concatenate([second_ref[tile] for tile in range(tiles)], axis=1)
    mixed = normalize(second).astype(BF16)

    logits = jnp.dot(mixed, router_ref[...], preferred_element_type=F32)
    lane = lax.broadcasted_iota(jnp.int32, (rows, experts), 1)
    named = [lane == routes_ref[:, pick : pick + 1] for pick in range(TOPK)]
    picked = [jnp.sum(jnp.where(one, logits, 0.0), axis=1, keepdims=True) for one in named]
    top = jnp.maximum(picked[0], picked[1])
    raised = [jnp.exp(one - top) for one in picked]
    mass = raised[0] + raised[1]
    down = lax.broadcasted_iota(jnp.int32, (rows, rows), 0)
    across = lax.broadcasted_iota(jnp.int32, (rows, rows), 1)
    picks = jnp.where(named[0] | named[1], 1.0, 0.0).astype(BF16)
    earlier = jnp.where(across < down, 1.0, 0.0).astype(BF16)
    ranks = jnp.dot(earlier, picks, preferred_element_type=F32)
    column = lax.broadcasted_iota(jnp.int32, (rows, LANES), 1)
    info = jnp.zeros((rows, LANES), F32)
    for pick in range(TOPK):
        rank = jnp.sum(jnp.where(named[pick], ranks, 0.0), axis=1, keepdims=True)
        place_of = routes_ref[:, pick : pick + 1] ^ turn
        slot = rank + (place_of * capacity).astype(F32)
        info = jnp.where(column == pick, slot, info)
        info = jnp.where(column == TOPK + pick, raised[pick] / mass, info)
    info_ref[...] = info

    expert = lax.broadcasted_iota(jnp.int32, (experts, rows), 0) ^ turn
    chosen = (expert == turned_ref[0:1, :]) | (expert == turned_ref[1:2, :])
    later = jnp.where(down < across, 1.0, 0.0).astype(BF16)
    order = jnp.dot(jnp.where(chosen, 1.0, 0.0).astype(BF16), later, preferred_element_type=F32)
    order = jnp.where(chosen, order, -1.0)
    slot = lax.broadcasted_iota(jnp.int32, (capacity, rows), 0).astype(F32)
    select = jnp.concatenate(
        [jnp.where(slot == order[e : e + 1, :], 1.0, 0.0) for e in range(experts)], axis=0
    ).astype(BF16)
    scatter(out_refs, jnp.dot(select, mixed, preferred_element_type=F32))


def joined(refs):
    if len(refs) == 1:
        return refs[0][...]
    return jnp.concatenate([ref[...].astype(F32) for ref in refs], axis=0).astype(BF16)


def scatter(refs, values):
    tall = values.shape[0] // len(refs)
    for e, ref in enumerate(refs):
        ref[...] = values[e * tall : (e + 1) * tall].astype(BF16)


def expert_kernel(chunks, pieces, *refs):
    x_refs, o_refs = refs[:chunks], refs[-chunks:]
    in_refs, out_refs = refs[chunks : chunks + pieces], refs[chunks + pieces : chunks + 2 * pieces]
    tokens = joined(x_refs)
    total = jnp.zeros((tokens.shape[0], D), F32)
    for in_ref, out_ref in zip(in_refs, out_refs):
        raw = lax.dot_general(
            tokens, in_ref[...], (((1,), (1,)), ((), ())), preferred_element_type=F32
        )
        hidden = (raw / (1.0 + jnp.exp(-raw))).astype(BF16)
        total = total + jnp.dot(hidden, out_ref[...], preferred_element_type=F32)
    scatter(o_refs, total)


def mixture_of(info, back_refs):
    back = joined(back_refs)
    column = lax.broadcasted_iota(jnp.int32, (info.shape[0], back.shape[0]), 1).astype(F32)
    spread = jnp.where(column == info[:, 0:1], info[:, 2:3], 0.0)
    spread = jnp.where(column == info[:, 1:2], info[:, 3:4], spread).astype(BF16)
    return jnp.dot(spread, back, preferred_element_type=F32)


def theirs_kernel(info_ref, *refs):
    refs[-1][...] = mixture_of(info_ref[...], refs[:-1]).astype(BF16)


def mine_kernel(info_ref, second_ref, part_ref, *refs):
    o_ref = refs[-1]
    mixture = mixture_of(info_ref[...], refs[:-1])
    for tile in range(D // LANES):
        at = slice(tile * LANES, (tile + 1) * LANES)
        both = mixture[:, at] + part_ref[:, at].astype(F32)
        o_ref[:, at] = (second_ref[tile] + 0.5 * both).astype(BF16)


def crossed(count, direct, me, r):
    return me ^ r if direct else r


def trade(arrays, axis, direct=True):
    count = len(arrays)
    if not direct:
        mixed = lax.all_to_all(jnp.stack(arrays), axis, split_axis=0, concat_axis=0, tiled=True)
        return [mixed[r] for r in range(count)]
    moved = {
        r: lax.ppermute(arrays[r], axis, [(i, i ^ r) for i in range(count)])
        for r in range(count - 1, 0, -1)
    }
    return [arrays[0]] + [moved[r] for r in range(1, count)]


def after(arrays, markers):
    return lax.optimization_barrier((*arrays, *markers))[: len(arrays)]


def body(
    query_rows,
    key_rows,
    value_rows,
    head_scale,
    out_proj,
    conv_taps,
    router,
    expert_in,
    expert_out,
    lengths,
    routes,
):
    rows = query_rows.shape[1]
    experts = lax.axis_size("dp")
    count = lax.axis_size("tm")
    half = count // 2
    heads = HEADS // count
    width = heads * HEAD_DIM
    window = rows + 2 * HALO
    capacity = -(-(3 * rows // experts) // 8) * 8
    direct = width % LANES == 0
    me = lax.axis_index("tm").astype(jnp.int32).reshape(1)
    expert = lax.axis_index("dp").astype(jnp.int32).reshape(1)
    partner = [(i, i ^ half) for i in range(count)]
    place = functools.partial(crossed, count, direct)

    packed = pl.pallas_call(
        functools.partial(pack_kernel, place),
        out_shape=(jax.ShapeDtypeStruct((3, rows, width), BF16),) * count,
        in_specs=[SMEM] + [pl.BlockSpec(memory_space=pltpu.HBM) if direct else VMEM] * 3,
        out_specs=(VMEM,) * count,
        scratch_shapes=[pltpu.SemaphoreType.DMA((3 * count,))],
        compiler_params=params(60),
        cost_estimate=cost(1),
        name="pack",
    )(me, query_rows[0], key_rows[0], value_rows[0])
    arrived = trade(packed, "tm", direct)
    scales = lax.dynamic_slice_in_dim(head_scale, me[0] * heads, heads)
    partner_routes = lax.ppermute(routes[0], "tm", partner)

    tiles = max(1, width // LANES)
    total = count * rows
    sent = jax.ShapeDtypeStruct((window, width), BF16)
    attended = pl.pallas_call(
        functools.partial(attend_kernel, count, rows, heads, place),
        out_shape=(sent,) * (2 * count),
        in_specs=[SMEM, SMEM, SMEM] + [VMEM] * count,
        out_specs=(VMEM,) * (2 * count),
        scratch_shapes=[
            pltpu.VMEM((tiles, total, 2 * LANES), BF16),
            pltpu.VMEM((tiles, total, 2 * LANES), BF16),
            pltpu.VMEM((total + 2 * HALO, width), BF16),
        ],
        compiler_params=params(10),
        cost_estimate=cost(6),
        name="attend",
    )(me, scales, lengths, *arrived)
    gathered_a = trade(attended[:count], "tm", direct)
    gathered_b = trade(attended[count:], "tm", direct)

    early, late = after((expert_in[0], expert_out[0]), gathered_b)
    if half == 2:
        swap = [(i, i ^ 1) for i in range(count)]
        ins = [early, lax.ppermute(early, "tm", swap)]
        outs = [late, lax.ppermute(late, "tm", swap)]
    else:
        groups = [list(range(i, i + half)) for i in (0, half)]
        ins = [lax.all_gather(early, "tm", axis=0, tiled=True, axis_index_groups=groups)]
        outs = [lax.all_gather(late, "tm", axis=0, tiled=True, axis_index_groups=groups)]

    taps = jnp.transpose(conv_taps.reshape(KERNEL, D // LANES, LANES), (1, 0, 2))
    slots = experts * capacity

    def chunks_of(split):
        if split:
            return (jax.ShapeDtypeStruct((capacity, D), BF16),) * experts
        return (jax.ShapeDtypeStruct((slots, D), BF16),)

    def route(arrays):
        if len(arrays) > 1:
            return trade(arrays, "dp")
        whole = arrays[0].reshape(experts, capacity, D)
        moved = lax.all_to_all(whole, "dp", split_axis=0, concat_axis=0, tiled=True)
        return [moved.reshape(slots, D)]

    def send_frames(windows, flip, split, block_routes):
        chunks = chunks_of(split)
        made = pl.pallas_call(
            functools.partial(frame_kernel, count, rows, experts, capacity, place, flip),
            out_shape=chunks
            + (
                jax.ShapeDtypeStruct((rows, LANES), F32),
                jax.ShapeDtypeStruct((D // LANES, rows, LANES), F32),
            ),
            in_specs=[SMEM, SMEM, SMEM] + [VMEM] * (5 + count),
            out_specs=(VMEM,) * (len(chunks) + 2),
            scratch_shapes=[
                pltpu.VMEM((D // LANES, window, LANES), F32),
                pltpu.VMEM((D // LANES, rows, LANES), F32),
                pltpu.VMEM((window, LANES), F32),
            ],
            compiler_params=params(16),
            cost_estimate=cost(10),
            name="frames",
        )(me, expert, lengths, out_proj, taps, router, block_routes, block_routes.T, *windows)
        return made[:-2], made[-2], made[-1]

    def run_expert(tokens):
        split = len(tokens) > 1
        chunks = chunks_of(split)
        produced = pl.pallas_call(
            functools.partial(expert_kernel, len(tokens), len(ins)),
            out_shape=chunks,
            in_specs=[VMEM] * (len(tokens) + len(ins) + len(outs)),
            out_specs=(VMEM,) * len(chunks),
            compiler_params=params(20),
            cost_estimate=cost(8),
            name="experts",
        )(*tokens, *ins, *outs)
        return produced

    outgoing_a, info_a, _ = send_frames(gathered_a, half, False, partner_routes)
    tokens_a = route(after(outgoing_a, gathered_b))
    gathered_b = after(gathered_b, (outgoing_a[0], ins[-1]))
    outgoing_b, info_b, second = send_frames(gathered_b, 0, True, routes[0])
    tokens_b = route(outgoing_b)
    produced_a = run_expert(after(tokens_a, tokens_b))
    back_a = route(produced_a)
    produced_b = run_expert(after(tokens_b, produced_a))
    back_b = route(produced_b)
    back_a = after(back_a, back_b[1:2])

    theirs = pl.pallas_call(
        theirs_kernel,
        out_shape=jax.ShapeDtypeStruct((rows, D), BF16),
        in_specs=[VMEM] * (1 + len(back_a)),
        out_specs=VMEM,
        compiler_params=params(8),
        cost_estimate=cost(1),
        name="theirs",
    )(info_a, *back_a)
    received = lax.ppermute(theirs, "tm", partner)
    out = pl.pallas_call(
        mine_kernel,
        out_shape=jax.ShapeDtypeStruct((rows, D), BF16),
        in_specs=[VMEM] * (3 + len(back_b)),
        out_specs=VMEM,
        compiler_params=params(12),
        cost_estimate=cost(1),
        name="mine",
    )(info_b, second, received, *back_b)
    return out[None]


def solution(mesh):
    return jax.shard_map(
        body,
        mesh=mesh,
        in_specs=(
            P("dp", "tm", None),
            P("dp", "tm", None),
            P("dp", "tm", None),
            P(),
            P(),
            P(),
            P(),
            P("dp", "tm", None),
            P("dp", "tm", None),
            P("dp", None),
            P("dp", "tm", None),
        ),
        out_specs=P("dp", "tm", None),
        check_vma=False,
    )
```

```python
import functools

import jax
import jax.numpy as jnp
from jax import lax
from jax.experimental import pallas as pl
from jax.experimental.pallas import tpu as pltpu
from jax.sharding import PartitionSpec as P

D = 1536
HEADS = 16
HEAD_DIM = 64
KERNEL = 31
TOPK = 2
RECS = 4
HALO = 16
LANES = 128
APART = 64.0
LOG2E = 1.4426950408889634
F32 = jnp.float32
BF16 = jnp.bfloat16
VMEM = pl.BlockSpec(memory_space=pltpu.VMEM)
SMEM = pl.BlockSpec(memory_space=pltpu.SMEM)


def params(mib):
    return pltpu.CompilerParams(vmem_limit_bytes=mib << 20)


def cost(micros):
    return pl.CostEstimate(flops=micros * 1_100_000_000, bytes_accessed=0, transcendentals=0)


def labels_of(frames, len_ref):
    first = len_ref[0, 0]
    second = first + len_ref[0, 1]
    third = second + len_ref[0, 2]
    return (
        (frames >= first).astype(F32)
        + (frames >= second).astype(F32)
        + (frames >= third).astype(F32)
    )


def unit_tile(tile, low):
    lifted = tile.astype(F32)
    square = lifted * lifted
    left = jnp.sum(jnp.where(low, square, 0.0), axis=1, keepdims=True)
    right = jnp.sum(jnp.where(low, 0.0, square), axis=1, keepdims=True)
    factor = jnp.where(low, lax.rsqrt(left + 1e-06), lax.rsqrt(right + 1e-06))
    return lifted * factor


def pack_kernel(place, me_ref, q_ref, k_ref, v_ref, *refs):
    o_refs, sem_ref = refs[:-1], refs[-1]
    width = o_refs[0].shape[2]
    copies = []
    for r in range(len(o_refs) - 1, -1, -1):
        target = place(me_ref[0], r)
        for which, ref in enumerate((q_ref, k_ref, v_ref)):
            if width % LANES == 0:
                columns = pl.ds(pl.multiple_of(target * width, LANES), width)
                copy = pltpu.make_async_copy(
                    ref.at[:, columns], o_refs[r].at[which], sem_ref.at[r * 3 + which]
                )
                copy.start()
                copies.append(copy)
            else:
                o_refs[r][which] = ref[:, target * width : (target + 1) * width]
    for copy in copies:
        copy.wait()


def attend_kernel(count, rows, heads, place, me_ref, scale_ref, len_ref, *refs):
    x_refs, oa_refs, ob_refs = refs[:count], refs[count : 2 * count], refs[2 * count : 3 * count]
    k_ref, v_ref, a_ref = refs[3 * count :]
    me = me_ref[0]
    width = heads * HEAD_DIM
    tiles = max(1, width // LANES)
    half = count // 2
    window = rows + 2 * HALO

    def tile_of(r, which, tile):
        if width >= LANES:
            return x_refs[r][which, :, tile * LANES : (tile + 1) * LANES]
        piece = x_refs[r][which]
        return jnp.concatenate([piece, jnp.zeros((rows, LANES - width), BF16)], axis=1)

    low = lax.broadcasted_iota(jnp.int32, (rows, LANES), 1) < HEAD_DIM
    lane = lax.broadcasted_iota(jnp.int32, (rows, LANES), 1).astype(F32)
    row = lax.broadcasted_iota(jnp.int32, (rows, LANES), 0)

    edge = jnp.zeros((HALO, width), BF16)
    a_ref[0:HALO, :] = edge
    a_ref[HALO + count * rows :, :] = edge
    for r in range(count):
        at = slice(r * rows, (r + 1) * rows)
        label = labels_of(row + place(me, r) * rows, len_ref)
        other = jnp.where((lane >= 1.0) & (lane <= 4.0) & (lane != label + 1.0), -APART, 0.0)
        extra = jnp.where(lane == 0.0, -1.0, other).astype(BF16)
        for tile in range(tiles):
            k_ref[tile, at, 0:LANES] = unit_tile(tile_of(r, 1, tile), low).astype(BF16)
            k_ref[tile, at, LANES:] = extra
            v_ref[tile, at, 0:LANES] = tile_of(r, 2, tile)
            v_ref[tile, at, LANES:] = jnp.ones((rows, LANES), BF16)

    for r in range(count):
        block = place(me, r)
        label = labels_of(row + block * rows, len_ref)
        extra = jnp.where((lane == 0.0) | (lane == label + 1.0), 1.0, 0.0).astype(BF16)
        for tile in range(tiles):
            unit = unit_tile(tile_of(r, 0, tile), low)
            parts = []
            for side in range(min(2, heads)):
                head = tile * 2 + side
                kept = jnp.where(low if side == 0 else ~low, unit, 0.0).astype(BF16)
                query = jnp.concatenate([kept, extra], axis=1)
                scores = lax.dot_general(
                    query, k_ref[tile], (((1,), (1,)), ((), ())), preferred_element_type=F32
                )
                weights = jnp.exp2(scores * (scale_ref[head] * LOG2E)).astype(BF16)
                summed = jnp.dot(weights, v_ref[tile], preferred_element_type=F32)
                parts.append(summed[:, 0:LANES] / summed[:, LANES:])
            done = parts[0] if len(parts) == 1 else jnp.where(low, parts[0], parts[1])
            start = pl.multiple_of(HALO + block * rows, HALO)
            wide = min(LANES, width)
            a_ref[pl.ds(start, rows), tile * LANES : tile * LANES + wide] = done[:, 0:wide].astype(BF16)

    for r in range(count):
        target = place(me, r)
        for o_ref, block in ((oa_refs[r], target ^ half), (ob_refs[r], target)):
            o_ref[...] = a_ref[pl.ds(pl.multiple_of(block * rows, HALO), window), :]


def normalize(values):
    average = jnp.mean(values, axis=-1, keepdims=True)
    centered = values - average
    spread = jnp.mean(centered * centered, axis=-1, keepdims=True)
    return centered * lax.rsqrt(spread + 1e-05)


def frame_kernel(
    count,
    rows,
    experts,
    capacity,
    place,
    flip,
    me_ref,
    expert_ref,
    len_ref,
    proj_ref,
    taps_ref,
    router_ref,
    routes_ref,
    turned_ref,
    *refs,
):
    att_refs, out_refs = refs[:count], refs[count:-5]
    info_ref, second_ref, x_ref, first_ref, lab_ref = refs[-5:]
    me = me_ref[0]
    turn = expert_ref[0] if len(out_refs) > 1 else 0
    width = att_refs[0].shape[1]
    window = rows + 2 * HALO
    half = (KERNEL - 1) // 2
    tiles = D // LANES
    step = 56
    first = jnp.zeros((window, D), F32)
    for r in range(count):
        begin = pl.multiple_of(place(me, r) * width, HEAD_DIM)
        first = first + jnp.dot(
            att_refs[r][...], proj_ref[pl.ds(begin, width), :], preferred_element_type=F32
        )
    normed = normalize(first).astype(BF16).astype(F32)
    origin = (me ^ flip) * rows
    frames = lax.broadcasted_iota(jnp.int32, (window, LANES), 0) + (origin - HALO)
    lab_ref[...] = labels_of(frames, len_ref)
    for tile in range(tiles):
        at = slice(tile * LANES, (tile + 1) * LANES)
        x_ref[tile] = normed[:, at]
        first_ref[tile] = first[HALO : HALO + rows, at]

    starts = [len_ref[0, 0], len_ref[0, 0] + len_ref[0, 1]]
    starts.append(starts[1] + len_ref[0, 2])
    for begin in range(0, rows, step):
        low = origin + begin - half
        high = low + step + 2 * half
        crossed = functools.reduce(
            jnp.logical_or, [(low < start) & (start < high) for start in starts]
        )

        def columns(tile, masked):
            total = jnp.zeros((step, LANES), F32)
            own = lab_ref[HALO + begin : HALO + begin + step, :] if masked else None
            for tap in range(KERNEL):
                source = HALO - half + begin + tap
                term = taps_ref[tile, tap : tap + 1, :] * x_ref[tile, source : source + step, :]
                if masked:
                    term = jnp.where(lab_ref[source : source + step, :] == own, term, 0.0)
                total = total + term
            gated = total / (1.0 + jnp.exp(-total))
            second_ref[tile, begin : begin + step, :] = (
                first_ref[tile, begin : begin + step, :] + gated
            )

        @pl.when(crossed)
        def _():
            lax.fori_loop(0, tiles, lambda tile, c: (columns(tile, True), c)[1], 0)

        @pl.when(jnp.logical_not(crossed))
        def _():
            lax.fori_loop(0, tiles, lambda tile, c: (columns(tile, False), c)[1], 0)

    second = jnp.concatenate([second_ref[tile] for tile in range(tiles)], axis=1)
    mixed = normalize(second).astype(BF16)

    logits = jnp.dot(mixed, router_ref[...], preferred_element_type=F32)
    lane = lax.broadcasted_iota(jnp.int32, (rows, experts), 1)
    named = [lane == routes_ref[:, pick : pick + 1] for pick in range(TOPK)]
    picked = [jnp.sum(jnp.where(one, logits, 0.0), axis=1, keepdims=True) for one in named]
    top = jnp.maximum(picked[0], picked[1])
    raised = [jnp.exp(one - top) for one in picked]
    mass = raised[0] + raised[1]
    down = lax.broadcasted_iota(jnp.int32, (rows, rows), 0)
    across = lax.broadcasted_iota(jnp.int32, (rows, rows), 1)
    picks = jnp.where(named[0] | named[1], 1.0, 0.0).astype(BF16)
    earlier = jnp.where(across < down, 1.0, 0.0).astype(BF16)
    ranks = jnp.dot(earlier, picks, preferred_element_type=F32)
    column = lax.broadcasted_iota(jnp.int32, (rows, LANES), 1)
    info = jnp.zeros((rows, LANES), F32)
    for pick in range(TOPK):
        rank = jnp.sum(jnp.where(named[pick], ranks, 0.0), axis=1, keepdims=True)
        place_of = routes_ref[:, pick : pick + 1] ^ turn
        slot = rank + (place_of * capacity).astype(F32)
        info = jnp.where(column == pick, slot, info)
        info = jnp.where(column == TOPK + pick, raised[pick] / mass, info)
    info_ref[...] = info

    expert = lax.broadcasted_iota(jnp.int32, (experts, rows), 0) ^ turn
    chosen = (expert == turned_ref[0:1, :]) | (expert == turned_ref[1:2, :])
    later = jnp.where(down < across, 1.0, 0.0).astype(BF16)
    order = jnp.dot(jnp.where(chosen, 1.0, 0.0).astype(BF16), later, preferred_element_type=F32)
    order = jnp.where(chosen, order, -1.0)
    slot = lax.broadcasted_iota(jnp.int32, (capacity, rows), 0).astype(F32)
    select = jnp.concatenate(
        [jnp.where(slot == order[e : e + 1, :], 1.0, 0.0) for e in range(experts)], axis=0
    ).astype(BF16)
    scatter(out_refs, jnp.dot(select, mixed, preferred_element_type=F32))


def joined(refs):
    if len(refs) == 1:
        return refs[0][...]
    return jnp.concatenate([ref[...].astype(F32) for ref in refs], axis=0).astype(BF16)


def scatter(refs, values):
    tall = values.shape[0] // len(refs)
    for e, ref in enumerate(refs):
        ref[...] = values[e * tall : (e + 1) * tall].astype(BF16)


def expert_kernel(chunks, spans, *refs):
    x_refs, o_refs = refs[:chunks], refs[-chunks:]
    in_refs, out_refs = refs[chunks : chunks + len(spans)], refs[chunks + len(spans) : -chunks]
    tokens = joined(x_refs)
    total = jnp.zeros((tokens.shape[0], D), F32)
    for in_ref, (place, begin) in zip(in_refs, spans):
        raw = lax.dot_general(
            tokens, in_ref[...], (((1,), (1,)), ((), ())), preferred_element_type=F32
        )
        hidden = (raw / (1.0 + jnp.exp(-raw))).astype(BF16)
        matching = out_refs[place][begin : begin + in_ref.shape[0], :]
        total = total + jnp.dot(hidden, matching, preferred_element_type=F32)
    scatter(o_refs, total)


def mixture_of(info, back_refs):
    back = joined(back_refs)
    column = lax.broadcasted_iota(jnp.int32, (info.shape[0], back.shape[0]), 1).astype(F32)
    spread = jnp.where(column == info[:, 0:1], info[:, 2:3], 0.0)
    spread = jnp.where(column == info[:, 1:2], info[:, 3:4], spread).astype(BF16)
    return jnp.dot(spread, back, preferred_element_type=F32)


def theirs_kernel(info_ref, *refs):
    refs[-1][...] = mixture_of(info_ref[...], refs[:-1]).astype(BF16)


def mine_kernel(info_ref, second_ref, part_ref, *refs):
    o_ref = refs[-1]
    mixture = mixture_of(info_ref[...], refs[:-1])
    for tile in range(D // LANES):
        at = slice(tile * LANES, (tile + 1) * LANES)
        both = mixture[:, at] + part_ref[:, at].astype(F32)
        o_ref[:, at] = (second_ref[tile] + 0.5 * both).astype(BF16)


def crossed(count, direct, me, r):
    return me ^ r if direct else r


def trade(arrays, axis, direct=True):
    count = len(arrays)
    if not direct:
        mixed = lax.all_to_all(jnp.stack(arrays), axis, split_axis=0, concat_axis=0, tiled=True)
        return [mixed[r] for r in range(count)]
    moved = {
        r: lax.ppermute(arrays[r], axis, [(i, i ^ r) for i in range(count)])
        for r in range(count - 1, 0, -1)
    }
    return [arrays[0]] + [moved[r] for r in range(1, count)]


def after(arrays, markers):
    return lax.optimization_barrier((*arrays, *markers))[: len(arrays)]


def body(
    query_rows,
    key_rows,
    value_rows,
    head_scale,
    out_proj,
    conv_taps,
    router,
    expert_in,
    expert_out,
    lengths,
    routes,
):
    rows = query_rows.shape[1]
    experts = lax.axis_size("dp")
    count = lax.axis_size("tm")
    half = count // 2
    heads = HEADS // count
    width = heads * HEAD_DIM
    window = rows + 2 * HALO
    capacity = -(-(3 * rows // experts) // 8) * 8
    direct = width % LANES == 0
    me = lax.axis_index("tm").astype(jnp.int32).reshape(1)
    expert = lax.axis_index("dp").astype(jnp.int32).reshape(1)
    partner = [(i, i ^ half) for i in range(count)]
    place = functools.partial(crossed, count, direct)

    packed = pl.pallas_call(
        functools.partial(pack_kernel, place),
        out_shape=(jax.ShapeDtypeStruct((3, rows, width), BF16),) * count,
        in_specs=[SMEM] + [pl.BlockSpec(memory_space=pltpu.HBM) if direct else VMEM] * 3,
        out_specs=(VMEM,) * count,
        scratch_shapes=[pltpu.SemaphoreType.DMA((3 * count,))],
        compiler_params=params(60),
        cost_estimate=cost(1),
        name="pack",
    )(me, query_rows[0], key_rows[0], value_rows[0])
    arrived = trade(packed, "tm", direct)
    scales = lax.dynamic_slice_in_dim(head_scale, me[0] * heads, heads)
    partner_routes = lax.ppermute(routes[0], "tm", partner)

    tiles = max(1, width // LANES)
    total = count * rows
    sent = jax.ShapeDtypeStruct((window, width), BF16)
    attended = pl.pallas_call(
        functools.partial(attend_kernel, count, rows, heads, place),
        out_shape=(sent,) * (2 * count),
        in_specs=[SMEM, SMEM, SMEM] + [VMEM] * count,
        out_specs=(VMEM,) * (2 * count),
        scratch_shapes=[
            pltpu.VMEM((tiles, total, 2 * LANES), BF16),
            pltpu.VMEM((tiles, total, 2 * LANES), BF16),
            pltpu.VMEM((total + 2 * HALO, width), BF16),
        ],
        compiler_params=params(10),
        cost_estimate=cost(6),
        name="attend",
    )(me, scales, lengths, *arrived)
    gathered_a = trade(attended[:count], "tm", direct)
    gathered_b = trade(attended[count:], "tm", direct)

    shards = after((expert_in[0], expert_out[0]), gathered_a + gathered_b)
    if half == 2:
        swap = [(i, i ^ 1) for i in range(count)]
        cut = expert_in.shape[1] // 2
        pieces = (shards[0][:cut], shards[0][cut:], shards[1])
        moved = [lax.ppermute(one, "tm", swap) for one in pieces]
        ins, outs = [shards[0], moved[0], moved[1]], [shards[1], moved[2]]
        spans = ((0, 0), (1, 0), (1, cut))
    else:
        groups = [list(range(i, i + half)) for i in (0, half)]
        moved = [
            lax.all_gather(one, "tm", axis=0, tiled=True, axis_index_groups=groups)
            for one in shards
        ]
        ins, outs, spans = moved[:1], moved[1:], ((0, 0),)

    taps = jnp.transpose(conv_taps.reshape(KERNEL, D // LANES, LANES), (1, 0, 2))
    slots = experts * capacity

    def chunks_of(split):
        if split:
            return (jax.ShapeDtypeStruct((capacity, D), BF16),) * experts
        return (jax.ShapeDtypeStruct((slots, D), BF16),)

    def route(arrays):
        if len(arrays) > 1:
            return trade(arrays, "dp")
        whole = arrays[0].reshape(experts, capacity, D)
        moved = lax.all_to_all(whole, "dp", split_axis=0, concat_axis=0, tiled=True)
        return [moved.reshape(slots, D)]

    def send_frames(windows, flip, split, block_routes):
        chunks = chunks_of(split)
        made = pl.pallas_call(
            functools.partial(frame_kernel, count, rows, experts, capacity, place, flip),
            out_shape=chunks
            + (
                jax.ShapeDtypeStruct((rows, LANES), F32),
                jax.ShapeDtypeStruct((D // LANES, rows, LANES), F32),
            ),
            in_specs=[SMEM, SMEM, SMEM] + [VMEM] * (5 + count),
            out_specs=(VMEM,) * (len(chunks) + 2),
            scratch_shapes=[
                pltpu.VMEM((D // LANES, window, LANES), F32),
                pltpu.VMEM((D // LANES, rows, LANES), F32),
                pltpu.VMEM((window, LANES), F32),
            ],
            compiler_params=params(16),
            cost_estimate=cost(10),
            name="frames",
        )(me, expert, lengths, out_proj, taps, router, block_routes, block_routes.T, *windows)
        return made[:-2], made[-2], made[-1]

    def run_expert(tokens):
        split = len(tokens) > 1
        chunks = chunks_of(split)
        produced = pl.pallas_call(
            functools.partial(expert_kernel, len(tokens), spans),
            out_shape=chunks,
            in_specs=[VMEM] * (len(tokens) + len(ins) + len(outs)),
            out_specs=(VMEM,) * len(chunks),
            compiler_params=params(20),
            cost_estimate=cost(8),
            name="experts",
        )(*tokens, *ins, *outs)
        return produced

    outgoing_a, info_a, _ = send_frames(gathered_a, half, False, partner_routes)
    tokens_a = route(after(outgoing_a, gathered_b))
    gathered_b = after(gathered_b, (outgoing_a[0], moved[0]))
    outgoing_b, info_b, second = send_frames(gathered_b, 0, False, routes[0])
    tokens_b = route(outgoing_b)
    produced_a = run_expert(tokens_a)
    back_a = route(after(produced_a, tokens_b))
    produced_b = run_expert(after(tokens_b, produced_a))
    back_a = after(back_a, produced_b)

    theirs = pl.pallas_call(
        theirs_kernel,
        out_shape=jax.ShapeDtypeStruct((rows, D), BF16),
        in_specs=[VMEM] * (1 + len(back_a)),
        out_specs=VMEM,
        compiler_params=params(8),
        cost_estimate=cost(1),
        name="theirs",
    )(info_a, *back_a)
    received = lax.ppermute(theirs, "tm", partner)
    back_b = route(after(produced_b, (theirs,)))
    out = pl.pallas_call(
        mine_kernel,
        out_shape=jax.ShapeDtypeStruct((rows, D), BF16),
        in_specs=[VMEM] * (3 + len(back_b)),
        out_specs=VMEM,
        compiler_params=params(12),
        cost_estimate=cost(1),
        name="mine",
    )(info_b, second, received, *back_b)
    return out[None]


def solution(mesh):
    return jax.shard_map(
        body,
        mesh=mesh,
        in_specs=(
            P("dp", "tm", None),
            P("dp", "tm", None),
            P("dp", "tm", None),
            P(),
            P(),
            P(),
            P(),
            P("dp", "tm", None),
            P("dp", "tm", None),
            P("dp", None),
            P("dp", "tm", None),
        ),
        out_specs=P("dp", "tm", None),
        check_vma=False,
    )
```

```python
import functools

import jax
import jax.numpy as jnp
from jax import lax
from jax.experimental import pallas as pl
from jax.experimental.pallas import tpu as pltpu
from jax.sharding import PartitionSpec as P

D = 1536
HEADS = 16
HEAD_DIM = 64
KERNEL = 31
TOPK = 2
RECS = 4
HALO = 16
LANES = 128
APART = 64.0
LOG2E = 1.4426950408889634
F32 = jnp.float32
BF16 = jnp.bfloat16
VMEM = pl.BlockSpec(memory_space=pltpu.VMEM)
SMEM = pl.BlockSpec(memory_space=pltpu.SMEM)


def params(mib):
    return pltpu.CompilerParams(vmem_limit_bytes=mib << 20)


def cost(micros):
    return pl.CostEstimate(flops=micros * 1_100_000_000, bytes_accessed=0, transcendentals=0)


def labels_of(frames, len_ref):
    first = len_ref[0, 0]
    second = first + len_ref[0, 1]
    third = second + len_ref[0, 2]
    return (
        (frames >= first).astype(F32)
        + (frames >= second).astype(F32)
        + (frames >= third).astype(F32)
    )


def unit_tile(tile, low):
    lifted = tile.astype(F32)
    square = lifted * lifted
    left = jnp.sum(jnp.where(low, square, 0.0), axis=1, keepdims=True)
    right = jnp.sum(jnp.where(low, 0.0, square), axis=1, keepdims=True)
    factor = jnp.where(low, lax.rsqrt(left + 1e-06), lax.rsqrt(right + 1e-06))
    return lifted * factor


def pack_kernel(place, me_ref, q_ref, k_ref, v_ref, *refs):
    o_refs, sem_ref = refs[:-1], refs[-1]
    width = o_refs[0].shape[2]
    copies = []
    for r in range(len(o_refs) - 1, -1, -1):
        target = place(me_ref[0], r)
        for which, ref in enumerate((q_ref, k_ref, v_ref)):
            if width % LANES == 0:
                columns = pl.ds(pl.multiple_of(target * width, LANES), width)
                copy = pltpu.make_async_copy(
                    ref.at[:, columns], o_refs[r].at[which], sem_ref.at[r * 3 + which]
                )
                copy.start()
                copies.append(copy)
            else:
                o_refs[r][which] = ref[:, target * width : (target + 1) * width]
    for copy in copies:
        copy.wait()


def attend_kernel(count, rows, heads, place, me_ref, scale_ref, len_ref, *refs):
    x_refs, (o_ref, k_ref, v_ref, a_ref) = refs[:count], refs[count:]
    me = me_ref[0]
    width = heads * HEAD_DIM
    tiles = max(1, width // LANES)
    half = count // 2
    window = rows + 2 * HALO

    def tile_of(r, which, tile):
        if width >= LANES:
            return x_refs[r][which, :, tile * LANES : (tile + 1) * LANES]
        piece = x_refs[r][which]
        return jnp.concatenate([piece, jnp.zeros((rows, LANES - width), BF16)], axis=1)

    low = lax.broadcasted_iota(jnp.int32, (rows, LANES), 1) < HEAD_DIM
    lane = lax.broadcasted_iota(jnp.int32, (rows, LANES), 1).astype(F32)
    row = lax.broadcasted_iota(jnp.int32, (rows, LANES), 0)

    edge = jnp.zeros((HALO, width), BF16)
    a_ref[0:HALO, :] = edge
    a_ref[HALO + count * rows :, :] = edge
    for r in range(count):
        at = slice(r * rows, (r + 1) * rows)
        label = labels_of(row + place(me, r) * rows, len_ref)
        other = jnp.where((lane >= 1.0) & (lane <= 4.0) & (lane != label + 1.0), -APART, 0.0)
        extra = jnp.where(lane == 0.0, -1.0, other).astype(BF16)
        for tile in range(tiles):
            k_ref[tile, at, 0:LANES] = unit_tile(tile_of(r, 1, tile), low).astype(BF16)
            k_ref[tile, at, LANES:] = extra
            v_ref[tile, at, 0:LANES] = tile_of(r, 2, tile)
            v_ref[tile, at, LANES:] = jnp.ones((rows, LANES), BF16)

    for r in range(count):
        block = place(me, r)
        label = labels_of(row + block * rows, len_ref)
        extra = jnp.where((lane == 0.0) | (lane == label + 1.0), 1.0, 0.0).astype(BF16)
        for tile in range(tiles):
            unit = unit_tile(tile_of(r, 0, tile), low)
            parts = []
            for side in range(min(2, heads)):
                head = tile * 2 + side
                kept = jnp.where(low if side == 0 else ~low, unit, 0.0).astype(BF16)
                query = jnp.concatenate([kept, extra], axis=1)
                scores = lax.dot_general(
                    query, k_ref[tile], (((1,), (1,)), ((), ())), preferred_element_type=F32
                )
                weights = jnp.exp2(scores * (scale_ref[head] * LOG2E)).astype(BF16)
                summed = jnp.dot(weights, v_ref[tile], preferred_element_type=F32)
                parts.append(summed[:, 0:LANES] / summed[:, LANES:])
            done = parts[0] if len(parts) == 1 else jnp.where(low, parts[0], parts[1])
            start = pl.multiple_of(HALO + block * rows, HALO)
            wide = min(LANES, width)
            a_ref[pl.ds(start, rows), tile * LANES : tile * LANES + wide] = done[:, 0:wide].astype(BF16)

    for target in range(count):
        for which, block in enumerate((target ^ half, target)):
            o_ref[target, which] = a_ref[block * rows : block * rows + window, :]


def normalize(values):
    average = jnp.mean(values, axis=-1, keepdims=True)
    centered = values - average
    spread = jnp.mean(centered * centered, axis=-1, keepdims=True)
    return centered * lax.rsqrt(spread + 1e-05)


def frame_kernel(
    count,
    rows,
    experts,
    capacity,
    flip,
    me_ref,
    expert_ref,
    len_ref,
    proj_ref,
    taps_ref,
    router_ref,
    routes_ref,
    turned_ref,
    *refs,
):
    att_ref, out_refs = refs[0], refs[1:-5]
    info_ref, second_ref, x_ref, first_ref, lab_ref = refs[-5:]
    me = me_ref[0]
    turn = expert_ref[0] if len(out_refs) > 1 else 0
    window = rows + 2 * HALO
    half = (KERNEL - 1) // 2
    tiles = D // LANES
    step = 56
    which = 0 if flip else 1
    attended = jnp.concatenate([att_ref[source, which] for source in range(count)], axis=1)
    first = jnp.dot(attended, proj_ref[...], preferred_element_type=F32)
    normed = normalize(first).astype(BF16).astype(F32)
    origin = (me ^ flip) * rows
    frames = lax.broadcasted_iota(jnp.int32, (window, LANES), 0) + (origin - HALO)
    lab_ref[...] = labels_of(frames, len_ref)
    for tile in range(tiles):
        at = slice(tile * LANES, (tile + 1) * LANES)
        x_ref[tile] = normed[:, at]
        first_ref[tile] = first[HALO : HALO + rows, at]

    starts = [len_ref[0, 0], len_ref[0, 0] + len_ref[0, 1]]
    starts.append(starts[1] + len_ref[0, 2])
    for begin in range(0, rows, step):
        low = origin + begin - half
        high = low + step + 2 * half
        crossed = functools.reduce(
            jnp.logical_or, [(low < start) & (start < high) for start in starts]
        )

        def columns(tile, masked):
            total = jnp.zeros((step, LANES), F32)
            own = lab_ref[HALO + begin : HALO + begin + step, :] if masked else None
            for tap in range(KERNEL):
                source = HALO - half + begin + tap
                term = taps_ref[tile, tap : tap + 1, :] * x_ref[tile, source : source + step, :]
                if masked:
                    term = jnp.where(lab_ref[source : source + step, :] == own, term, 0.0)
                total = total + term
            gated = total / (1.0 + jnp.exp(-total))
            second_ref[tile, begin : begin + step, :] = (
                first_ref[tile, begin : begin + step, :] + gated
            )

        @pl.when(crossed)
        def _():
            lax.fori_loop(0, tiles, lambda tile, c: (columns(tile, True), c)[1], 0)

        @pl.when(jnp.logical_not(crossed))
        def _():
            lax.fori_loop(0, tiles, lambda tile, c: (columns(tile, False), c)[1], 0)

    second = jnp.concatenate([second_ref[tile] for tile in range(tiles)], axis=1)
    mixed = normalize(second).astype(BF16)

    logits = jnp.dot(mixed, router_ref[...], preferred_element_type=F32)
    lane = lax.broadcasted_iota(jnp.int32, (rows, experts), 1)
    named = [lane == routes_ref[:, pick : pick + 1] for pick in range(TOPK)]
    picked = [jnp.sum(jnp.where(one, logits, 0.0), axis=1, keepdims=True) for one in named]
    top = jnp.maximum(picked[0], picked[1])
    raised = [jnp.exp(one - top) for one in picked]
    mass = raised[0] + raised[1]
    down = lax.broadcasted_iota(jnp.int32, (rows, rows), 0)
    across = lax.broadcasted_iota(jnp.int32, (rows, rows), 1)
    picks = jnp.where(named[0] | named[1], 1.0, 0.0).astype(BF16)
    earlier = jnp.where(across < down, 1.0, 0.0).astype(BF16)
    ranks = jnp.dot(earlier, picks, preferred_element_type=F32)
    column = lax.broadcasted_iota(jnp.int32, (rows, LANES), 1)
    info = jnp.zeros((rows, LANES), F32)
    for pick in range(TOPK):
        rank = jnp.sum(jnp.where(named[pick], ranks, 0.0), axis=1, keepdims=True)
        place_of = routes_ref[:, pick : pick + 1] ^ turn
        slot = rank + (place_of * capacity).astype(F32)
        info = jnp.where(column == pick, slot, info)
        info = jnp.where(column == TOPK + pick, raised[pick] / mass, info)
    info_ref[...] = info

    expert = lax.broadcasted_iota(jnp.int32, (experts, rows), 0) ^ turn
    chosen = (expert == turned_ref[0:1, :]) | (expert == turned_ref[1:2, :])
    later = jnp.where(down < across, 1.0, 0.0).astype(BF16)
    order = jnp.dot(jnp.where(chosen, 1.0, 0.0).astype(BF16), later, preferred_element_type=F32)
    order = jnp.where(chosen, order, -1.0)
    slot = lax.broadcasted_iota(jnp.int32, (capacity, rows), 0).astype(F32)
    select = jnp.concatenate(
        [jnp.where(slot == order[e : e + 1, :], 1.0, 0.0) for e in range(experts)], axis=0
    ).astype(BF16)
    scatter(out_refs, jnp.dot(select, mixed, preferred_element_type=F32))


def joined(refs):
    if len(refs) == 1:
        return refs[0][...]
    return jnp.concatenate([ref[...].astype(F32) for ref in refs], axis=0).astype(BF16)


def scatter(refs, values):
    tall = values.shape[0] // len(refs)
    for e, ref in enumerate(refs):
        ref[...] = values[e * tall : (e + 1) * tall].astype(BF16)


def expert_kernel(chunks, units, spans, *refs):
    x_refs, w_refs, o_refs = refs[:chunks], refs[chunks:-chunks], refs[-chunks:]
    tokens = joined(x_refs)
    total = None
    for (into, first), (out, second) in spans:
        raw = lax.dot_general(
            tokens,
            w_refs[into][first : first + units, :],
            (((1,), (1,)), ((), ())),
            preferred_element_type=F32,
        )
        hidden = (raw / (1.0 + jnp.exp(-raw))).astype(BF16)
        product = jnp.dot(
            hidden, w_refs[out][second : second + units, :], preferred_element_type=F32
        )
        total = product if total is None else total + product
    scatter(o_refs, total)


def mixture_of(info, back_refs):
    back = joined(back_refs)
    column = lax.broadcasted_iota(jnp.int32, (info.shape[0], back.shape[0]), 1).astype(F32)
    spread = jnp.where(column == info[:, 0:1], info[:, 2:3], 0.0)
    spread = jnp.where(column == info[:, 1:2], info[:, 3:4], spread).astype(BF16)
    return jnp.dot(spread, back, preferred_element_type=F32)


def theirs_kernel(info_ref, *refs):
    refs[-1][...] = mixture_of(info_ref[...], refs[:-1]).astype(BF16)


def mine_kernel(info_ref, second_ref, part_ref, *refs):
    o_ref = refs[-1]
    mixture = mixture_of(info_ref[...], refs[:-1])
    for tile in range(D // LANES):
        at = slice(tile * LANES, (tile + 1) * LANES)
        both = mixture[:, at] + part_ref[:, at].astype(F32)
        o_ref[:, at] = (second_ref[tile] + 0.5 * both).astype(BF16)


def crossed(count, direct, me, r):
    return me ^ r if direct else r


def trade(arrays, axis, direct=True):
    count = len(arrays)
    if not direct:
        mixed = lax.all_to_all(jnp.stack(arrays), axis, split_axis=0, concat_axis=0, tiled=True)
        return [mixed[r] for r in range(count)]
    moved = {
        r: lax.ppermute(arrays[r], axis, [(i, i ^ r) for i in range(count)])
        for r in range(count - 1, 0, -1)
    }
    return [arrays[0]] + [moved[r] for r in range(1, count)]


def after(arrays, markers):
    return lax.optimization_barrier((*arrays, *markers))[: len(arrays)]


def body(
    query_rows,
    key_rows,
    value_rows,
    head_scale,
    out_proj,
    conv_taps,
    router,
    expert_in,
    expert_out,
    lengths,
    routes,
):
    rows = query_rows.shape[1]
    experts = lax.axis_size("dp")
    count = lax.axis_size("tm")
    half = count // 2
    heads = HEADS // count
    width = heads * HEAD_DIM
    window = rows + 2 * HALO
    capacity = -(-(3 * rows // experts) // 8) * 8
    direct = width % LANES == 0
    me = lax.axis_index("tm").astype(jnp.int32).reshape(1)
    expert = lax.axis_index("dp").astype(jnp.int32).reshape(1)
    partner = [(i, i ^ half) for i in range(count)]
    place = functools.partial(crossed, count, direct)

    packed = pl.pallas_call(
        functools.partial(pack_kernel, place),
        out_shape=(jax.ShapeDtypeStruct((3, rows, width), BF16),) * count,
        in_specs=[SMEM] + [pl.BlockSpec(memory_space=pltpu.HBM) if direct else VMEM] * 3,
        out_specs=(VMEM,) * count,
        scratch_shapes=[pltpu.SemaphoreType.DMA((3 * count,))],
        compiler_params=params(60),
        cost_estimate=cost(1),
        name="pack",
    )(me, query_rows[0], key_rows[0], value_rows[0])
    arrived = trade(packed, "tm", direct)
    scales = lax.dynamic_slice_in_dim(head_scale, me[0] * heads, heads)
    partner_routes = lax.ppermute(routes[0], "tm", partner)

    tiles = max(1, width // LANES)
    total = count * rows
    attended = pl.pallas_call(
        functools.partial(attend_kernel, count, rows, heads, place),
        out_shape=jax.ShapeDtypeStruct((count, 2, window, width), BF16),
        in_specs=[SMEM, SMEM, SMEM] + [VMEM] * count,
        out_specs=VMEM,
        scratch_shapes=[
            pltpu.VMEM((tiles, total, 2 * LANES), BF16),
            pltpu.VMEM((tiles, total, 2 * LANES), BF16),
            pltpu.VMEM((total + 2 * HALO, width), BF16),
        ],
        compiler_params=params(16),
        cost_estimate=cost(6),
        name="attend",
    )(me, scales, lengths, *arrived)
    windows = lax.all_to_all(attended, "tm", split_axis=0, concat_axis=0, tiled=True)

    units = expert_in.shape[1]
    (shard,) = after((jnp.concatenate([expert_in[0], expert_out[0]]),), (attended,))
    if half == 2:
        moved = lax.ppermute(shard, "tm", [(i, i ^ 1) for i in range(count)])
        weights = [expert_in[0], expert_out[0], moved]
        spans = (((0, 0), (1, 0)), ((2, 0), (2, units)))
    else:
        groups = [list(range(i, i + half)) for i in (0, half)]
        weights = [
            lax.all_gather(one, "tm", axis=0, tiled=True, axis_index_groups=groups)
            for one in (shard[:units], shard[units:])
        ]
        units = units * half
        spans = (((0, 0), (1, 0)),)

    taps = jnp.transpose(conv_taps.reshape(KERNEL, D // LANES, LANES), (1, 0, 2))
    slots = experts * capacity

    def chunks_of(split):
        if split:
            return (jax.ShapeDtypeStruct((capacity, D), BF16),) * experts
        return (jax.ShapeDtypeStruct((slots, D), BF16),)

    def route(arrays):
        if len(arrays) > 1:
            return trade(arrays, "dp")
        whole = arrays[0].reshape(experts, capacity, D)
        moved = lax.all_to_all(whole, "dp", split_axis=0, concat_axis=0, tiled=True)
        return [moved.reshape(slots, D)]

    def send_frames(windows, flip, split, block_routes):
        chunks = chunks_of(split)
        made = pl.pallas_call(
            functools.partial(frame_kernel, count, rows, experts, capacity, flip),
            out_shape=chunks
            + (
                jax.ShapeDtypeStruct((rows, LANES), F32),
                jax.ShapeDtypeStruct((D // LANES, rows, LANES), F32),
            ),
            in_specs=[SMEM, SMEM, SMEM] + [VMEM] * 6,
            out_specs=(VMEM,) * (len(chunks) + 2),
            scratch_shapes=[
                pltpu.VMEM((D // LANES, window, LANES), F32),
                pltpu.VMEM((D // LANES, rows, LANES), F32),
                pltpu.VMEM((window, LANES), F32),
            ],
            compiler_params=params(56),
            cost_estimate=cost(10),
            name="frames",
        )(me, expert, lengths, out_proj, taps, router, block_routes, block_routes.T, windows)
        return made[:-2], made[-2], made[-1]

    def run_expert(tokens):
        split = len(tokens) > 1
        chunks = chunks_of(split)
        produced = pl.pallas_call(
            functools.partial(expert_kernel, len(tokens), units, spans),
            out_shape=chunks,
            in_specs=[VMEM] * (len(tokens) + len(weights)),
            out_specs=(VMEM,) * len(chunks),
            compiler_params=params(56),
            cost_estimate=cost(8),
            name="experts",
        )(*tokens, *weights)
        return produced

    outgoing_a, info_a, _ = send_frames(windows, half, False, partner_routes)
    tokens_a = route(outgoing_a)
    (windows,) = after((windows,), outgoing_a)
    outgoing_b, info_b, second = send_frames(windows, 0, False, routes[0])
    tokens_b = route(after(outgoing_b, tokens_a))
    produced_a = run_expert(tokens_a)
    back_a = route(after(produced_a, tokens_b))
    produced_b = run_expert(after(tokens_b, produced_a))
    back_a = after(back_a, produced_b)

    theirs = pl.pallas_call(
        theirs_kernel,
        out_shape=jax.ShapeDtypeStruct((rows, D), BF16),
        in_specs=[VMEM] * (1 + len(back_a)),
        out_specs=VMEM,
        compiler_params=params(56),
        cost_estimate=cost(1),
        name="theirs",
    )(info_a, *back_a)
    received = lax.ppermute(theirs, "tm", partner)
    back_b = route(after(produced_b, (theirs,)))
    out = pl.pallas_call(
        mine_kernel,
        out_shape=jax.ShapeDtypeStruct((rows, D), BF16),
        in_specs=[VMEM] * (3 + len(back_b)),
        out_specs=VMEM,
        compiler_params=params(56),
        cost_estimate=cost(1),
        name="mine",
    )(info_b, second, received, *back_b)
    return out[None]


def solution(mesh):
    return jax.shard_map(
        body,
        mesh=mesh,
        in_specs=(
            P("dp", "tm", None),
            P("dp", "tm", None),
            P("dp", "tm", None),
            P(),
            P(),
            P(),
            P(),
            P("dp", "tm", None),
            P("dp", "tm", None),
            P("dp", None),
            P("dp", "tm", None),
        ),
        out_specs=P("dp", "tm", None),
        check_vma=False,
    )
```

```python
import functools

import jax
import jax.numpy as jnp
from jax import lax
from jax.experimental import pallas as pl
from jax.experimental.pallas import tpu as pltpu
from jax.sharding import PartitionSpec as P

D = 1536
HEADS = 16
HEAD_DIM = 64
KERNEL = 31
TOPK = 2
RECS = 4
HALO = 16
LANES = 128
APART = 64.0
LOG2E = 1.4426950408889634
F32 = jnp.float32
BF16 = jnp.bfloat16
VMEM = pl.BlockSpec(memory_space=pltpu.VMEM)
SMEM = pl.BlockSpec(memory_space=pltpu.SMEM)


def params(mib):
    return pltpu.CompilerParams(vmem_limit_bytes=mib << 20)


def cost(micros):
    return pl.CostEstimate(flops=micros * 1_100_000_000, bytes_accessed=0, transcendentals=0)


def labels_of(frames, len_ref):
    first = len_ref[0, 0]
    second = first + len_ref[0, 1]
    third = second + len_ref[0, 2]
    return (
        (frames >= first).astype(F32)
        + (frames >= second).astype(F32)
        + (frames >= third).astype(F32)
    )


def unit_tile(tile, low):
    lifted = tile.astype(F32)
    square = lifted * lifted
    left = jnp.sum(jnp.where(low, square, 0.0), axis=1, keepdims=True)
    right = jnp.sum(jnp.where(low, 0.0, square), axis=1, keepdims=True)
    factor = jnp.where(low, lax.rsqrt(left + 1e-06), lax.rsqrt(right + 1e-06))
    return lifted * factor


def pack_kernel(place, me_ref, q_ref, k_ref, v_ref, *refs):
    o_refs, sem_ref = refs[:-1], refs[-1]
    width = o_refs[0].shape[2]
    copies = []
    for r in range(len(o_refs) - 1, -1, -1):
        target = place(me_ref[0], r)
        for which, ref in enumerate((q_ref, k_ref, v_ref)):
            if width % LANES == 0:
                columns = pl.ds(pl.multiple_of(target * width, LANES), width)
                copy = pltpu.make_async_copy(
                    ref.at[:, columns], o_refs[r].at[which], sem_ref.at[r * 3 + which]
                )
                copy.start()
                copies.append(copy)
            else:
                o_refs[r][which] = ref[:, target * width : (target + 1) * width]
    for copy in copies:
        copy.wait()


def attend_kernel(count, rows, heads, place, me_ref, scale_ref, len_ref, *refs):
    x_refs, o_refs = refs[:count], refs[count : 2 * count]
    k_ref, v_ref, a_ref = refs[2 * count :]
    me = me_ref[0]
    width = heads * HEAD_DIM
    tiles = max(1, width // LANES)
    half = count // 2
    window = rows + 2 * HALO

    def tile_of(r, which, tile):
        if width >= LANES:
            return x_refs[r][which, :, tile * LANES : (tile + 1) * LANES]
        piece = x_refs[r][which]
        return jnp.concatenate([piece, jnp.zeros((rows, LANES - width), BF16)], axis=1)

    low = lax.broadcasted_iota(jnp.int32, (rows, LANES), 1) < HEAD_DIM
    lane = lax.broadcasted_iota(jnp.int32, (rows, LANES), 1).astype(F32)
    row = lax.broadcasted_iota(jnp.int32, (rows, LANES), 0)

    edge = jnp.zeros((HALO, width), BF16)
    a_ref[0:HALO, :] = edge
    a_ref[HALO + count * rows :, :] = edge
    for r in range(count):
        at = slice(r * rows, (r + 1) * rows)
        label = labels_of(row + place(me, r) * rows, len_ref)
        other = jnp.where((lane >= 1.0) & (lane <= 4.0) & (lane != label + 1.0), -APART, 0.0)
        extra = jnp.where(lane == 0.0, -1.0, other).astype(BF16)
        for tile in range(tiles):
            k_ref[tile, at, 0:LANES] = unit_tile(tile_of(r, 1, tile), low).astype(BF16)
            k_ref[tile, at, LANES:] = extra
            v_ref[tile, at, 0:LANES] = tile_of(r, 2, tile)
            v_ref[tile, at, LANES:] = jnp.ones((rows, LANES), BF16)

    for r in range(count):
        block = place(me, r)
        label = labels_of(row + block * rows, len_ref)
        extra = jnp.where((lane == 0.0) | (lane == label + 1.0), 1.0, 0.0).astype(BF16)
        for tile in range(tiles):
            unit = unit_tile(tile_of(r, 0, tile), low)
            parts = []
            for side in range(min(2, heads)):
                head = tile * 2 + side
                kept = jnp.where(low if side == 0 else ~low, unit, 0.0).astype(BF16)
                query = jnp.concatenate([kept, extra], axis=1)
                scores = lax.dot_general(
                    query, k_ref[tile], (((1,), (1,)), ((), ())), preferred_element_type=F32
                )
                weights = jnp.exp2(scores * (scale_ref[head] * LOG2E)).astype(BF16)
                summed = jnp.dot(weights, v_ref[tile], preferred_element_type=F32)
                parts.append(summed[:, 0:LANES] / summed[:, LANES:])
            done = parts[0] if len(parts) == 1 else jnp.where(low, parts[0], parts[1])
            start = pl.multiple_of(HALO + block * rows, HALO)
            wide = min(LANES, width)
            a_ref[pl.ds(start, rows), tile * LANES : tile * LANES + wide] = done[:, 0:wide].astype(BF16)

    for r in range(count):
        target = place(me, r)
        for which, block in enumerate((target ^ half, target)):
            begin = pl.multiple_of(block * rows, HALO)
            o_refs[r][which] = a_ref[pl.ds(begin, window), :]


def normalize(values):
    average = jnp.mean(values, axis=-1, keepdims=True)
    centered = values - average
    spread = jnp.mean(centered * centered, axis=-1, keepdims=True)
    return centered * lax.rsqrt(spread + 1e-05)


def frame_kernel(
    count,
    rows,
    experts,
    capacity,
    place,
    flip,
    me_ref,
    expert_ref,
    len_ref,
    proj_ref,
    taps_ref,
    router_ref,
    routes_ref,
    turned_ref,
    *refs,
):
    att_refs, out_refs = refs[:count], refs[count:-5]
    info_ref, second_ref, x_ref, first_ref, lab_ref = refs[-5:]
    me = me_ref[0]
    turn = 0 if flip else expert_ref[0]
    window = rows + 2 * HALO
    half = (KERNEL - 1) // 2
    tiles = D // LANES
    step = 56
    which = 0 if flip else 1
    width = att_refs[0].shape[2]
    first = None
    for r in range(count):
        begin = pl.multiple_of(place(me, r) * width, HEAD_DIM)
        term = jnp.dot(
            att_refs[r][which], proj_ref[pl.ds(begin, width), :], preferred_element_type=F32
        )
        first = term if first is None else first + term
    normed = normalize(first).astype(BF16).astype(F32)
    origin = (me ^ flip) * rows
    frames = lax.broadcasted_iota(jnp.int32, (window, LANES), 0) + (origin - HALO)
    lab_ref[...] = labels_of(frames, len_ref)
    for tile in range(tiles):
        at = slice(tile * LANES, (tile + 1) * LANES)
        x_ref[tile] = normed[:, at]
        first_ref[tile] = first[HALO : HALO + rows, at]

    starts = [len_ref[0, 0], len_ref[0, 0] + len_ref[0, 1]]
    starts.append(starts[1] + len_ref[0, 2])
    for begin in range(0, rows, step):
        low = origin + begin - half
        high = low + step + 2 * half
        crossed = functools.reduce(
            jnp.logical_or, [(low < start) & (start < high) for start in starts]
        )

        def columns(tile, masked):
            total = jnp.zeros((step, LANES), F32)
            own = lab_ref[HALO + begin : HALO + begin + step, :] if masked else None
            for tap in range(KERNEL):
                source = HALO - half + begin + tap
                term = taps_ref[tile, tap : tap + 1, :] * x_ref[tile, source : source + step, :]
                if masked:
                    term = jnp.where(lab_ref[source : source + step, :] == own, term, 0.0)
                total = total + term
            gated = total / (1.0 + jnp.exp(-total))
            second_ref[tile, begin : begin + step, :] = (
                first_ref[tile, begin : begin + step, :] + gated
            )

        @pl.when(crossed)
        def _():
            lax.fori_loop(0, tiles, lambda tile, c: (columns(tile, True), c)[1], 0)

        @pl.when(jnp.logical_not(crossed))
        def _():
            lax.fori_loop(0, tiles, lambda tile, c: (columns(tile, False), c)[1], 0)

    second = jnp.concatenate([second_ref[tile] for tile in range(tiles)], axis=1)
    mixed = normalize(second).astype(BF16)

    logits = jnp.dot(mixed, router_ref[...], preferred_element_type=F32)
    lane = lax.broadcasted_iota(jnp.int32, (rows, experts), 1)
    named = [lane == routes_ref[:, pick : pick + 1] for pick in range(TOPK)]
    picked = [jnp.sum(jnp.where(one, logits, 0.0), axis=1, keepdims=True) for one in named]
    top = jnp.maximum(picked[0], picked[1])
    raised = [jnp.exp(one - top) for one in picked]
    mass = raised[0] + raised[1]
    down = lax.broadcasted_iota(jnp.int32, (rows, rows), 0)
    across = lax.broadcasted_iota(jnp.int32, (rows, rows), 1)
    picks = jnp.where(named[0] | named[1], 1.0, 0.0).astype(BF16)
    earlier = jnp.where(across < down, 1.0, 0.0).astype(BF16)
    ranks = jnp.dot(earlier, picks, preferred_element_type=F32)
    column = lax.broadcasted_iota(jnp.int32, (rows, LANES), 1)
    info = jnp.zeros((rows, LANES), F32)
    for pick in range(TOPK):
        rank = jnp.sum(jnp.where(named[pick], ranks, 0.0), axis=1, keepdims=True)
        place_of = routes_ref[:, pick : pick + 1] ^ turn
        slot = rank + (place_of * capacity).astype(F32)
        info = jnp.where(column == pick, slot, info)
        info = jnp.where(column == TOPK + pick, raised[pick] / mass, info)
    info_ref[...] = info

    expert = lax.broadcasted_iota(jnp.int32, (experts, rows), 0)
    chosen = (expert == turned_ref[0:1, :]) | (expert == turned_ref[1:2, :])
    later = jnp.where(down < across, 1.0, 0.0).astype(BF16)
    order = jnp.dot(jnp.where(chosen, 1.0, 0.0).astype(BF16), later, preferred_element_type=F32)
    order = jnp.where(chosen, order, -1.0)
    slot = lax.broadcasted_iota(jnp.int32, (capacity, rows), 0).astype(F32)
    select = jnp.concatenate(
        [jnp.where(slot == order[e : e + 1, :], 1.0, 0.0) for e in range(experts)], axis=0
    ).astype(BF16)
    out_refs[0][...] = jnp.dot(select, mixed, preferred_element_type=F32).astype(BF16)


def joined(refs):
    if len(refs) == 1:
        return refs[0][...]
    return jnp.concatenate([ref[...].astype(F32) for ref in refs], axis=0).astype(BF16)


def expert_kernel(chunks, units, spans, expert_ref, x_ref, *refs):
    pieces = len(refs) - chunks - (chunks > 1)
    w_refs, o_refs = refs[:pieces], refs[pieces : pieces + chunks]
    tokens = x_ref[...]
    total = None
    for (into, first), (out, second) in spans:
        raw = lax.dot_general(
            tokens,
            w_refs[into][first : first + units, :],
            (((1,), (1,)), ((), ())),
            preferred_element_type=F32,
        )
        hidden = (raw / (1.0 + jnp.exp(-raw))).astype(BF16)
        product = jnp.dot(
            hidden, w_refs[out][second : second + units, :], preferred_element_type=F32
        )
        total = product if total is None else total + product
    if chunks == 1:
        o_refs[0][...] = total.astype(BF16)
        return
    refs[-1][...] = total
    tall = o_refs[0].shape[0]
    for r, o_ref in enumerate(o_refs):
        begin = pl.multiple_of((expert_ref[0] ^ r) * tall, 8)
        o_ref[...] = refs[-1][pl.ds(begin, tall), :].astype(BF16)


def mixture_of(info, back_refs):
    back = joined(back_refs)
    column = lax.broadcasted_iota(jnp.int32, (info.shape[0], back.shape[0]), 1).astype(F32)
    spread = jnp.where(column == info[:, 0:1], info[:, 2:3], 0.0)
    spread = jnp.where(column == info[:, 1:2], info[:, 3:4], spread).astype(BF16)
    return jnp.dot(spread, back, preferred_element_type=F32)


def theirs_kernel(info_ref, *refs):
    refs[-1][...] = mixture_of(info_ref[...], refs[:-1]).astype(BF16)


def mine_kernel(info_ref, second_ref, part_ref, *refs):
    o_ref = refs[-1]
    mixture = mixture_of(info_ref[...], refs[:-1])
    for tile in range(D // LANES):
        at = slice(tile * LANES, (tile + 1) * LANES)
        both = mixture[:, at] + part_ref[:, at].astype(F32)
        o_ref[:, at] = (second_ref[tile] + 0.5 * both).astype(BF16)


def crossed(count, direct, me, r):
    return me ^ r if direct else r


def trade(arrays, axis, direct=True):
    count = len(arrays)
    if not direct:
        mixed = lax.all_to_all(jnp.stack(arrays), axis, split_axis=0, concat_axis=0, tiled=True)
        return [mixed[r] for r in range(count)]
    moved = {
        r: lax.ppermute(arrays[r], axis, [(i, i ^ r) for i in range(count)])
        for r in range(count - 1, 0, -1)
    }
    return [arrays[0]] + [moved[r] for r in range(1, count)]


def after(arrays, markers):
    return lax.optimization_barrier((*arrays, *markers))[: len(arrays)]


def body(
    query_rows,
    key_rows,
    value_rows,
    head_scale,
    out_proj,
    conv_taps,
    router,
    expert_in,
    expert_out,
    lengths,
    routes,
):
    rows = query_rows.shape[1]
    experts = lax.axis_size("dp")
    count = lax.axis_size("tm")
    half = count // 2
    heads = HEADS // count
    width = heads * HEAD_DIM
    window = rows + 2 * HALO
    capacity = -(-(3 * rows // experts) // 8) * 8
    direct = width % LANES == 0
    me = lax.axis_index("tm").astype(jnp.int32).reshape(1)
    expert = lax.axis_index("dp").astype(jnp.int32).reshape(1)
    partner = [(i, i ^ half) for i in range(count)]
    place = functools.partial(crossed, count, direct)

    packed = pl.pallas_call(
        functools.partial(pack_kernel, place),
        out_shape=(jax.ShapeDtypeStruct((3, rows, width), BF16),) * count,
        in_specs=[SMEM] + [pl.BlockSpec(memory_space=pltpu.HBM) if direct else VMEM] * 3,
        out_specs=(VMEM,) * count,
        scratch_shapes=[pltpu.SemaphoreType.DMA((3 * count,))],
        compiler_params=params(60),
        cost_estimate=cost(1),
        name="pack",
    )(me, query_rows[0], key_rows[0], value_rows[0])
    arrived = trade(packed, "tm", direct)
    scales = lax.dynamic_slice_in_dim(head_scale, me[0] * heads, heads)
    partner_routes = lax.ppermute(routes[0], "tm", partner)

    tiles = max(1, width // LANES)
    total = count * rows
    attended = pl.pallas_call(
        functools.partial(attend_kernel, count, rows, heads, place),
        out_shape=(jax.ShapeDtypeStruct((2, window, width), BF16),) * count,
        in_specs=[SMEM, SMEM, SMEM] + [VMEM] * count,
        out_specs=(VMEM,) * count,
        scratch_shapes=[
            pltpu.VMEM((tiles, total, 2 * LANES), BF16),
            pltpu.VMEM((tiles, total, 2 * LANES), BF16),
            pltpu.VMEM((total + 2 * HALO, width), BF16),
        ],
        compiler_params=params(16),
        cost_estimate=cost(6),
        name="attend",
    )(me, scales, lengths, *arrived)
    windows = trade(attended, "tm", direct)

    units = expert_in.shape[1]
    (shard,) = after((jnp.concatenate([expert_in[0], expert_out[0]]),), windows)
    if half == 2:
        moved = lax.ppermute(shard, "tm", [(i, i ^ 1) for i in range(count)])
        weights = [expert_in[0], expert_out[0], moved]
        spans = (((0, 0), (1, 0)), ((2, 0), (2, units)))
    else:
        groups = [list(range(i, i + half)) for i in (0, half)]
        weights = [
            lax.all_gather(one, "tm", axis=0, tiled=True, axis_index_groups=groups)
            for one in (shard[:units], shard[units:])
        ]
        units = units * half
        spans = (((0, 0), (1, 0)),)

    taps = jnp.transpose(conv_taps.reshape(KERNEL, D // LANES, LANES), (1, 0, 2))
    slots = experts * capacity

    def chunks_of(split):
        if split:
            return (jax.ShapeDtypeStruct((capacity, D), BF16),) * experts
        return (jax.ShapeDtypeStruct((slots, D), BF16),)

    def route(arrays):
        if len(arrays) > 1:
            return trade(arrays, "dp")
        whole = arrays[0].reshape(experts, capacity, D)
        moved = lax.all_to_all(whole, "dp", split_axis=0, concat_axis=0, tiled=True)
        return [moved.reshape(slots, D)]

    def send_frames(windows, flip, block_routes):
        chunks = chunks_of(False)
        made = pl.pallas_call(
            functools.partial(frame_kernel, count, rows, experts, capacity, place, flip),
            out_shape=chunks
            + (
                jax.ShapeDtypeStruct((rows, LANES), F32),
                jax.ShapeDtypeStruct((D // LANES, rows, LANES), F32),
            ),
            in_specs=[SMEM, SMEM, SMEM] + [VMEM] * (5 + count),
            out_specs=(VMEM,) * (len(chunks) + 2),
            scratch_shapes=[
                pltpu.VMEM((D // LANES, window, LANES), F32),
                pltpu.VMEM((D // LANES, rows, LANES), F32),
                pltpu.VMEM((window, LANES), F32),
            ],
            compiler_params=params(56),
            cost_estimate=cost(10),
            name="frames",
        )(me, expert, lengths, out_proj, taps, router, block_routes, block_routes.T, *windows)
        return made[:-2], made[-2], made[-1]

    def run_expert(tokens, split):
        chunks = chunks_of(split)
        produced = pl.pallas_call(
            functools.partial(expert_kernel, len(chunks), units, spans),
            out_shape=chunks,
            in_specs=[SMEM, VMEM] + [VMEM] * len(weights),
            out_specs=(VMEM,) * len(chunks),
            scratch_shapes=[pltpu.VMEM((slots, D), F32)] * split,
            compiler_params=params(56),
            cost_estimate=cost(8),
            name="experts",
        )(expert, *tokens, *weights)
        return produced

    outgoing_a, info_a, _ = send_frames(windows, half, partner_routes)
    tokens_a = route(outgoing_a)
    windows = after(windows, outgoing_a)
    outgoing_b, info_b, second = send_frames(windows, 0, routes[0])
    tokens_b = route(after(outgoing_b, tokens_a))
    produced_a = run_expert(tokens_a, False)
    back_a = route(after(produced_a, tokens_b))
    produced_b = run_expert(after(tokens_b, produced_a), True)
    back_b = route(produced_b)
    back_a = after(back_a, back_b[1:2])

    theirs = pl.pallas_call(
        theirs_kernel,
        out_shape=jax.ShapeDtypeStruct((rows, D), BF16),
        in_specs=[VMEM] * (1 + len(back_a)),
        out_specs=VMEM,
        compiler_params=params(16),
        cost_estimate=cost(1),
        name="theirs",
    )(info_a, *back_a)
    received = lax.ppermute(theirs, "tm", partner)
    out = pl.pallas_call(
        mine_kernel,
        out_shape=jax.ShapeDtypeStruct((rows, D), BF16),
        in_specs=[VMEM] * (3 + len(back_b)),
        out_specs=VMEM,
        compiler_params=params(16),
        cost_estimate=cost(1),
        name="mine",
    )(info_b, second, received, *back_b)
    return out[None]


def solution(mesh):
    return jax.shard_map(
        body,
        mesh=mesh,
        in_specs=(
            P("dp", "tm", None),
            P("dp", "tm", None),
            P("dp", "tm", None),
            P(),
            P(),
            P(),
            P(),
            P("dp", "tm", None),
            P("dp", "tm", None),
            P("dp", None),
            P("dp", "tm", None),
        ),
        out_specs=P("dp", "tm", None),
        check_vma=False,
    )
```

```python
import functools

import jax
import jax.numpy as jnp
from jax import lax
from jax.experimental import pallas as pl
from jax.experimental.pallas import tpu as pltpu
from jax.sharding import PartitionSpec as P

D = 1536
HEADS = 16
HEAD_DIM = 64
KERNEL = 31
TOPK = 2
RECS = 4
HALO = 16
LANES = 128
APART = 64.0
LOG2E = 1.4426950408889634
F32 = jnp.float32
BF16 = jnp.bfloat16
VMEM = pl.BlockSpec(memory_space=pltpu.VMEM)
SMEM = pl.BlockSpec(memory_space=pltpu.SMEM)


def params(mib):
    return pltpu.CompilerParams(vmem_limit_bytes=mib << 20)


def cost(micros):
    return pl.CostEstimate(flops=micros * 1_100_000_000, bytes_accessed=0, transcendentals=0)


def labels_of(frames, len_ref):
    first = len_ref[0, 0]
    second = first + len_ref[0, 1]
    third = second + len_ref[0, 2]
    return (
        (frames >= first).astype(F32)
        + (frames >= second).astype(F32)
        + (frames >= third).astype(F32)
    )


def unit_tile(tile, low):
    lifted = tile.astype(F32)
    square = lifted * lifted
    left = jnp.sum(jnp.where(low, square, 0.0), axis=1, keepdims=True)
    right = jnp.sum(jnp.where(low, 0.0, square), axis=1, keepdims=True)
    factor = jnp.where(low, lax.rsqrt(left + 1e-06), lax.rsqrt(right + 1e-06))
    return lifted * factor


def pack_kernel(place, me_ref, q_ref, k_ref, v_ref, *refs):
    o_refs, sem_ref = refs[:-1], refs[-1]
    width = o_refs[0].shape[2]
    copies = []
    for r in range(len(o_refs) - 1, -1, -1):
        target = place(me_ref[0], r)
        for which, ref in enumerate((q_ref, k_ref, v_ref)):
            if width % LANES == 0:
                columns = pl.ds(pl.multiple_of(target * width, LANES), width)
                copy = pltpu.make_async_copy(
                    ref.at[:, columns], o_refs[r].at[which], sem_ref.at[r * 3 + which]
                )
                copy.start()
                copies.append(copy)
            else:
                o_refs[r][which] = ref[:, target * width : (target + 1) * width]
    for copy in copies:
        copy.wait()


def attend_kernel(count, rows, heads, place, me_ref, scale_ref, len_ref, *refs):
    x_refs, o_refs = refs[:count], refs[count : 2 * count]
    k_ref, v_ref, a_ref = refs[2 * count :]
    me = me_ref[0]
    width = heads * HEAD_DIM
    tiles = max(1, width // LANES)
    half = count // 2
    window = rows + 2 * HALO

    def tile_of(r, which, tile):
        if width >= LANES:
            return x_refs[r][which, :, tile * LANES : (tile + 1) * LANES]
        piece = x_refs[r][which]
        return jnp.concatenate([piece, jnp.zeros((rows, LANES - width), BF16)], axis=1)

    low = lax.broadcasted_iota(jnp.int32, (rows, LANES), 1) < HEAD_DIM
    lane = lax.broadcasted_iota(jnp.int32, (rows, LANES), 1).astype(F32)
    row = lax.broadcasted_iota(jnp.int32, (rows, LANES), 0)

    edge = jnp.zeros((HALO, width), BF16)
    a_ref[0:HALO, :] = edge
    a_ref[HALO + count * rows :, :] = edge
    for r in range(count):
        at = slice(r * rows, (r + 1) * rows)
        label = labels_of(row + place(me, r) * rows, len_ref)
        other = jnp.where((lane >= 1.0) & (lane <= 4.0) & (lane != label + 1.0), -APART, 0.0)
        extra = jnp.where(lane == 0.0, -1.0, other).astype(BF16)
        for tile in range(tiles):
            k_ref[tile, at, 0:LANES] = unit_tile(tile_of(r, 1, tile), low).astype(BF16)
            k_ref[tile, at, LANES:] = extra
            v_ref[tile, at, 0:LANES] = tile_of(r, 2, tile)
            v_ref[tile, at, LANES:] = jnp.ones((rows, LANES), BF16)

    for r in range(count):
        block = place(me, r)
        label = labels_of(row + block * rows, len_ref)
        extra = jnp.where((lane == 0.0) | (lane == label + 1.0), 1.0, 0.0).astype(BF16)
        for tile in range(tiles):
            unit = unit_tile(tile_of(r, 0, tile), low)
            parts = []
            for side in range(min(2, heads)):
                head = tile * 2 + side
                kept = jnp.where(low if side == 0 else ~low, unit, 0.0).astype(BF16)
                query = jnp.concatenate([kept, extra], axis=1)
                scores = lax.dot_general(
                    query, k_ref[tile], (((1,), (1,)), ((), ())), preferred_element_type=F32
                )
                weights = jnp.exp2(scores * (scale_ref[head] * LOG2E)).astype(BF16)
                summed = jnp.dot(weights, v_ref[tile], preferred_element_type=F32)
                parts.append(summed[:, 0:LANES] / summed[:, LANES:])
            done = parts[0] if len(parts) == 1 else jnp.where(low, parts[0], parts[1])
            start = pl.multiple_of(HALO + block * rows, HALO)
            wide = min(LANES, width)
            a_ref[pl.ds(start, rows), tile * LANES : tile * LANES + wide] = done[:, 0:wide].astype(BF16)

    for r in range(count):
        target = place(me, r)
        for which, block in enumerate((target ^ half, target)):
            begin = pl.multiple_of(block * rows, HALO)
            o_refs[r][which] = a_ref[pl.ds(begin, window), :]


def normalize(values):
    average = jnp.mean(values, axis=-1, keepdims=True)
    centered = values - average
    spread = jnp.mean(centered * centered, axis=-1, keepdims=True)
    return centered * lax.rsqrt(spread + 1e-05)


def frame_kernel(
    count,
    rows,
    experts,
    capacity,
    place,
    flip,
    me_ref,
    expert_ref,
    len_ref,
    proj_ref,
    taps_ref,
    router_ref,
    routes_ref,
    turned_ref,
    *refs,
):
    att_refs, out_ref = refs[:count], refs[count]
    info_ref, second_ref, x_ref, first_ref, lab_ref = refs[-5:]
    me = me_ref[0]
    turn = expert_ref[0]
    window = rows + 2 * HALO
    half = (KERNEL - 1) // 2
    tiles = D // LANES
    step = 56
    which = 0 if flip else 1
    width = att_refs[0].shape[2]
    first = None
    for r in range(count):
        begin = pl.multiple_of(place(me, r) * width, HEAD_DIM)
        term = jnp.dot(
            att_refs[r][which], proj_ref[pl.ds(begin, width), :], preferred_element_type=F32
        )
        first = term if first is None else first + term
    normed = normalize(first).astype(BF16).astype(F32)
    origin = (me ^ flip) * rows
    frames = lax.broadcasted_iota(jnp.int32, (window, LANES), 0) + (origin - HALO)
    lab_ref[...] = labels_of(frames, len_ref)
    for tile in range(tiles):
        at = slice(tile * LANES, (tile + 1) * LANES)
        x_ref[tile] = normed[:, at]
        first_ref[tile] = first[HALO : HALO + rows, at]

    starts = [len_ref[0, 0], len_ref[0, 0] + len_ref[0, 1]]
    starts.append(starts[1] + len_ref[0, 2])
    for begin in range(0, rows, step):
        low = origin + begin - half
        high = low + step + 2 * half
        crossed = functools.reduce(
            jnp.logical_or, [(low < start) & (start < high) for start in starts]
        )

        def columns(tile, masked):
            total = jnp.zeros((step, LANES), F32)
            own = lab_ref[HALO + begin : HALO + begin + step, :] if masked else None
            for tap in range(KERNEL):
                source = HALO - half + begin + tap
                term = taps_ref[tile, tap : tap + 1, :] * x_ref[tile, source : source + step, :]
                if masked:
                    term = jnp.where(lab_ref[source : source + step, :] == own, term, 0.0)
                total = total + term
            gated = total / (1.0 + jnp.exp(-total))
            second_ref[tile, begin : begin + step, :] = (
                first_ref[tile, begin : begin + step, :] + gated
            )

        @pl.when(crossed)
        def _():
            lax.fori_loop(0, tiles, lambda tile, c: (columns(tile, True), c)[1], 0)

        @pl.when(jnp.logical_not(crossed))
        def _():
            lax.fori_loop(0, tiles, lambda tile, c: (columns(tile, False), c)[1], 0)

    second = jnp.concatenate([second_ref[tile] for tile in range(tiles)], axis=1)
    mixed = normalize(second).astype(BF16)

    logits = jnp.dot(mixed, router_ref[...], preferred_element_type=F32)
    lane = lax.broadcasted_iota(jnp.int32, (rows, experts), 1)
    named = [lane == routes_ref[:, pick : pick + 1] for pick in range(TOPK)]
    picked = [jnp.sum(jnp.where(one, logits, 0.0), axis=1, keepdims=True) for one in named]
    top = jnp.maximum(picked[0], picked[1])
    raised = [jnp.exp(one - top) for one in picked]
    mass = raised[0] + raised[1]
    down = lax.broadcasted_iota(jnp.int32, (rows, rows), 0)
    across = lax.broadcasted_iota(jnp.int32, (rows, rows), 1)
    picks = jnp.where(named[0] | named[1], 1.0, 0.0).astype(BF16)
    earlier = jnp.where(across < down, 1.0, 0.0).astype(BF16)
    ranks = jnp.dot(earlier, picks, preferred_element_type=F32)
    column = lax.broadcasted_iota(jnp.int32, (rows, LANES), 1)
    info = jnp.zeros((rows, LANES), F32)
    for pick in range(TOPK):
        rank = jnp.sum(jnp.where(named[pick], ranks, 0.0), axis=1, keepdims=True)
        place_of = routes_ref[:, pick : pick + 1] ^ turn
        slot = rank + (place_of * capacity).astype(F32)
        info = jnp.where(column == pick, slot, info)
        info = jnp.where(column == TOPK + pick, raised[pick] / mass, info)
    info_ref[...] = info

    expert = lax.broadcasted_iota(jnp.int32, (experts, rows), 0)
    chosen = (expert == turned_ref[0:1, :]) | (expert == turned_ref[1:2, :])
    later = jnp.where(down < across, 1.0, 0.0).astype(BF16)
    order = jnp.dot(jnp.where(chosen, 1.0, 0.0).astype(BF16), later, preferred_element_type=F32)
    order = jnp.where(chosen, order, -1.0)
    slot = lax.broadcasted_iota(jnp.int32, (capacity, rows), 0).astype(F32)
    select = jnp.concatenate(
        [jnp.where(slot == order[e : e + 1, :], 1.0, 0.0) for e in range(experts)], axis=0
    ).astype(BF16)
    out_ref[...] = jnp.dot(select, mixed, preferred_element_type=F32).astype(BF16)


def joined(refs):
    if len(refs) == 1:
        return refs[0][...]
    return jnp.concatenate([ref[...].astype(F32) for ref in refs], axis=0).astype(BF16)


def expert_kernel(experts, units, spans, expert_ref, *refs):
    count = (len(refs) - experts - 2) // 2
    sources, o_refs = refs[:count], refs[count : count + experts]
    held, (sum_ref, sem_ref) = refs[count + experts : -2], refs[-2:]
    copies = [
        pltpu.make_async_copy(sources[k], held[k], sem_ref.at[k]) for k in range(count)
    ]
    for copy in copies:
        copy.start()
    waiting = set(range(count))

    def ready(k):
        if k in waiting:
            waiting.remove(k)
            copies[k].wait()
        return held[k]

    tokens = ready(0)[...]
    total = None
    for (into, first), (out, second) in spans:
        raw = lax.dot_general(
            tokens,
            ready(1 + into)[first : first + units, :],
            (((1,), (1,)), ((), ())),
            preferred_element_type=F32,
        )
        hidden = (raw / (1.0 + jnp.exp(-raw))).astype(BF16)
        product = jnp.dot(
            hidden, ready(1 + out)[second : second + units, :], preferred_element_type=F32
        )
        total = product if total is None else total + product
    sum_ref[...] = total
    tall = o_refs[0].shape[0]
    for r, o_ref in enumerate(o_refs):
        begin = pl.multiple_of((expert_ref[0] ^ r) * tall, 8)
        o_ref[...] = sum_ref[pl.ds(begin, tall), :].astype(BF16)


def mixture_of(info, back_refs):
    back = joined(back_refs)
    column = lax.broadcasted_iota(jnp.int32, (info.shape[0], back.shape[0]), 1).astype(F32)
    spread = jnp.where(column == info[:, 0:1], info[:, 2:3], 0.0)
    spread = jnp.where(column == info[:, 1:2], info[:, 3:4], spread).astype(BF16)
    return jnp.dot(spread, back, preferred_element_type=F32)


def theirs_kernel(info_ref, *refs):
    refs[-1][...] = mixture_of(info_ref[...], refs[:-1]).astype(BF16)


def mine_kernel(info_ref, second_ref, part_ref, *refs):
    o_ref = refs[-1]
    mixture = mixture_of(info_ref[...], refs[:-1])
    for tile in range(D // LANES):
        at = slice(tile * LANES, (tile + 1) * LANES)
        both = mixture[:, at] + part_ref[:, at].astype(F32)
        o_ref[:, at] = (second_ref[tile] + 0.5 * both).astype(BF16)


def crossed(count, direct, me, r):
    return me ^ r if direct else r


def trade(arrays, axis, direct=True):
    count = len(arrays)
    if not direct:
        mixed = lax.all_to_all(jnp.stack(arrays), axis, split_axis=0, concat_axis=0, tiled=True)
        return [mixed[r] for r in range(count)]
    moved = {
        r: lax.ppermute(arrays[r], axis, [(i, i ^ r) for i in range(count)])
        for r in range(count - 1, 0, -1)
    }
    return [arrays[0]] + [moved[r] for r in range(1, count)]


def after(arrays, markers):
    return lax.optimization_barrier((*arrays, *markers))[: len(arrays)]


def body(
    query_rows,
    key_rows,
    value_rows,
    head_scale,
    out_proj,
    conv_taps,
    router,
    expert_in,
    expert_out,
    lengths,
    routes,
):
    rows = query_rows.shape[1]
    experts = lax.axis_size("dp")
    count = lax.axis_size("tm")
    half = count // 2
    heads = HEADS // count
    width = heads * HEAD_DIM
    window = rows + 2 * HALO
    capacity = -(-(3 * rows // experts) // 8) * 8
    direct = width % LANES == 0
    me = lax.axis_index("tm").astype(jnp.int32).reshape(1)
    expert = lax.axis_index("dp").astype(jnp.int32).reshape(1)
    partner = [(i, i ^ half) for i in range(count)]
    place = functools.partial(crossed, count, direct)

    packed = pl.pallas_call(
        functools.partial(pack_kernel, place),
        out_shape=(jax.ShapeDtypeStruct((3, rows, width), BF16),) * count,
        in_specs=[SMEM] + [pl.BlockSpec(memory_space=pltpu.HBM) if direct else VMEM] * 3,
        out_specs=(VMEM,) * count,
        scratch_shapes=[pltpu.SemaphoreType.DMA((3 * count,))],
        compiler_params=params(60),
        cost_estimate=cost(1),
        name="pack",
    )(me, query_rows[0], key_rows[0], value_rows[0])
    arrived = trade(packed, "tm", direct)
    scales = lax.dynamic_slice_in_dim(head_scale, me[0] * heads, heads)
    partner_routes = lax.ppermute(routes[0], "tm", partner)

    tiles = max(1, width // LANES)
    total = count * rows
    attended = pl.pallas_call(
        functools.partial(attend_kernel, count, rows, heads, place),
        out_shape=(jax.ShapeDtypeStruct((2, window, width), BF16),) * count,
        in_specs=[SMEM, SMEM, SMEM] + [VMEM] * count,
        out_specs=(VMEM,) * count,
        scratch_shapes=[
            pltpu.VMEM((tiles, total, 2 * LANES), BF16),
            pltpu.VMEM((tiles, total, 2 * LANES), BF16),
            pltpu.VMEM((total + 2 * HALO, width), BF16),
        ],
        compiler_params=params(16),
        cost_estimate=cost(6),
        name="attend",
    )(me, scales, lengths, *arrived)
    windows = trade(attended, "tm", direct)

    units = expert_in.shape[1]
    (shard,) = after((jnp.concatenate([expert_in[0], expert_out[0]]),), windows)
    if half == 2:
        moved = lax.ppermute(shard, "tm", [(i, i ^ 1) for i in range(count)])
        weights = [expert_in[0], expert_out[0], moved]
        spans = (((0, 0), (1, 0)), ((2, 0), (2, units)))
    else:
        groups = [list(range(i, i + half)) for i in (0, half)]
        weights = [
            lax.all_gather(one, "tm", axis=0, tiled=True, axis_index_groups=groups)
            for one in (shard[:units], shard[units:])
        ]
        units = units * half
        spans = (((0, 0), (1, 0)),)

    taps = jnp.transpose(conv_taps.reshape(KERNEL, D // LANES, LANES), (1, 0, 2))
    slots = experts * capacity

    def route(array):
        whole = array.reshape(experts, capacity, D)
        moved = lax.all_to_all(whole, "dp", split_axis=0, concat_axis=0, tiled=True)
        return (moved.reshape(slots, D),)

    def send_frames(windows, flip, block_routes):
        made = pl.pallas_call(
            functools.partial(frame_kernel, count, rows, experts, capacity, place, flip),
            out_shape=(
                jax.ShapeDtypeStruct((slots, D), BF16),
                jax.ShapeDtypeStruct((rows, LANES), F32),
                jax.ShapeDtypeStruct((D // LANES, rows, LANES), F32),
            ),
            in_specs=[SMEM, SMEM, SMEM] + [VMEM] * (5 + count),
            out_specs=(VMEM,) * 3,
            scratch_shapes=[
                pltpu.VMEM((D // LANES, window, LANES), F32),
                pltpu.VMEM((D // LANES, rows, LANES), F32),
                pltpu.VMEM((window, LANES), F32),
            ],
            compiler_params=params(56),
            cost_estimate=cost(10),
            name="frames",
        )(me, expert, lengths, out_proj, taps, router, block_routes, block_routes.T, *windows)
        return made

    def run_expert(tokens):
        operands = (*tokens, *weights)
        return pl.pallas_call(
            functools.partial(expert_kernel, experts, units, spans),
            out_shape=(jax.ShapeDtypeStruct((capacity, D), BF16),) * experts,
            in_specs=[SMEM] + [pl.BlockSpec(memory_space=pl.ANY)] * len(operands),
            out_specs=(VMEM,) * experts,
            scratch_shapes=[pltpu.VMEM(one.shape, BF16) for one in operands]
            + [pltpu.VMEM((slots, D), F32), pltpu.SemaphoreType.DMA((len(operands),))],
            compiler_params=params(56),
            cost_estimate=cost(8),
            name="experts",
        )(expert, *operands)

    outgoing_a, info_a, _ = send_frames(windows, half, partner_routes)
    tokens_a = route(outgoing_a)
    windows = after(windows, (outgoing_a,))
    outgoing_b, info_b, second = send_frames(windows, 0, routes[0])
    tokens_b = route(after((outgoing_b,), tokens_a)[0])
    produced_a = run_expert(tokens_a)
    back_a = trade(after(produced_a, tokens_b), "dp")
    produced_b = run_expert(after(tokens_b, produced_a))
    back_b = trade(produced_b, "dp")
    back_a = after(back_a, back_b[1:2])

    theirs = pl.pallas_call(
        theirs_kernel,
        out_shape=jax.ShapeDtypeStruct((rows, D), BF16),
        in_specs=[VMEM] * (1 + len(back_a)),
        out_specs=VMEM,
        compiler_params=params(16),
        cost_estimate=cost(1),
        name="theirs",
    )(info_a, *back_a)
    received = lax.ppermute(theirs, "tm", partner)
    out = pl.pallas_call(
        mine_kernel,
        out_shape=jax.ShapeDtypeStruct((rows, D), BF16),
        in_specs=[VMEM] * (3 + len(back_b)),
        out_specs=VMEM,
        compiler_params=params(16),
        cost_estimate=cost(1),
        name="mine",
    )(info_b, second, received, *back_b)
    return out[None]


def solution(mesh):
    return jax.shard_map(
        body,
        mesh=mesh,
        in_specs=(
            P("dp", "tm", None),
            P("dp", "tm", None),
            P("dp", "tm", None),
            P(),
            P(),
            P(),
            P(),
            P("dp", "tm", None),
            P("dp", "tm", None),
            P("dp", None),
            P("dp", "tm", None),
        ),
        out_specs=P("dp", "tm", None),
        check_vma=False,
    )
```

```python
import functools

import jax
import jax.numpy as jnp
from jax import lax
from jax.experimental import pallas as pl
from jax.experimental.pallas import tpu as pltpu
from jax.sharding import PartitionSpec as P

D = 1536
HEADS = 16
HEAD_DIM = 64
KERNEL = 31
TOPK = 2
RECS = 4
HALO = 16
LANES = 128
APART = 64.0
LOG2E = 1.4426950408889634
F32 = jnp.float32
BF16 = jnp.bfloat16
VMEM = pl.BlockSpec(memory_space=pltpu.VMEM)
SMEM = pl.BlockSpec(memory_space=pltpu.SMEM)


def params(mib):
    return pltpu.CompilerParams(vmem_limit_bytes=mib << 20)


def cost(micros):
    return pl.CostEstimate(flops=micros * 1_100_000_000, bytes_accessed=0, transcendentals=0)


def labels_of(frames, len_ref):
    first = len_ref[0, 0]
    second = first + len_ref[0, 1]
    third = second + len_ref[0, 2]
    return (
        (frames >= first).astype(F32)
        + (frames >= second).astype(F32)
        + (frames >= third).astype(F32)
    )


def unit_tile(tile, low):
    lifted = tile.astype(F32)
    square = lifted * lifted
    left = jnp.sum(jnp.where(low, square, 0.0), axis=1, keepdims=True)
    right = jnp.sum(jnp.where(low, 0.0, square), axis=1, keepdims=True)
    factor = jnp.where(low, lax.rsqrt(left + 1e-06), lax.rsqrt(right + 1e-06))
    return lifted * factor


def pack_kernel(place, me_ref, q_ref, k_ref, v_ref, *refs):
    o_refs, sem_ref = refs[:-1], refs[-1]
    width = o_refs[0].shape[2]
    copies = []
    for r in range(len(o_refs) - 1, -1, -1):
        target = place(me_ref[0], r)
        for which, ref in enumerate((q_ref, k_ref, v_ref)):
            if width % LANES == 0:
                columns = pl.ds(pl.multiple_of(target * width, LANES), width)
                copy = pltpu.make_async_copy(
                    ref.at[:, columns], o_refs[r].at[which], sem_ref.at[r * 3 + which]
                )
                copy.start()
                copies.append(copy)
            else:
                o_refs[r][which] = ref[:, target * width : (target + 1) * width]
    for copy in copies:
        copy.wait()


def attend_kernel(count, rows, heads, place, me_ref, scale_ref, len_ref, *refs):
    x_refs, o_refs = refs[:count], refs[count : 2 * count]
    k_ref, v_ref, a_ref = refs[2 * count :]
    me = me_ref[0]
    width = heads * HEAD_DIM
    tiles = max(1, width // LANES)
    half = count // 2
    window = rows + 2 * HALO

    def tile_of(r, which, tile):
        if width >= LANES:
            return x_refs[r][which, :, tile * LANES : (tile + 1) * LANES]
        piece = x_refs[r][which]
        return jnp.concatenate([piece, jnp.zeros((rows, LANES - width), BF16)], axis=1)

    low = lax.broadcasted_iota(jnp.int32, (rows, LANES), 1) < HEAD_DIM
    lane = lax.broadcasted_iota(jnp.int32, (rows, LANES), 1).astype(F32)
    row = lax.broadcasted_iota(jnp.int32, (rows, LANES), 0)

    edge = jnp.zeros((HALO, width), BF16)
    a_ref[0:HALO, :] = edge
    a_ref[HALO + count * rows :, :] = edge
    for r in range(count):
        at = slice(r * rows, (r + 1) * rows)
        label = labels_of(row + place(me, r) * rows, len_ref)
        other = jnp.where((lane >= 1.0) & (lane <= 4.0) & (lane != label + 1.0), -APART, 0.0)
        extra = jnp.where(lane == 0.0, -1.0, other).astype(BF16)
        for tile in range(tiles):
            k_ref[tile, at, 0:LANES] = unit_tile(tile_of(r, 1, tile), low).astype(BF16)
            k_ref[tile, at, LANES:] = extra
            v_ref[tile, at, 0:LANES] = tile_of(r, 2, tile)
            v_ref[tile, at, LANES:] = jnp.ones((rows, LANES), BF16)

    for r in range(count):
        block = place(me, r)
        label = labels_of(row + block * rows, len_ref)
        extra = jnp.where((lane == 0.0) | (lane == label + 1.0), 1.0, 0.0).astype(BF16)
        for tile in range(tiles):
            unit = unit_tile(tile_of(r, 0, tile), low)
            parts = []
            for side in range(min(2, heads)):
                head = tile * 2 + side
                kept = jnp.where(low if side == 0 else ~low, unit, 0.0).astype(BF16)
                query = jnp.concatenate([kept, extra], axis=1)
                scores = lax.dot_general(
                    query, k_ref[tile], (((1,), (1,)), ((), ())), preferred_element_type=F32
                )
                weights = jnp.exp2(scores * (scale_ref[head] * LOG2E)).astype(BF16)
                summed = jnp.dot(weights, v_ref[tile], preferred_element_type=F32)
                parts.append(summed[:, 0:LANES] / summed[:, LANES:])
            done = parts[0] if len(parts) == 1 else jnp.where(low, parts[0], parts[1])
            start = pl.multiple_of(HALO + block * rows, HALO)
            wide = min(LANES, width)
            a_ref[pl.ds(start, rows), tile * LANES : tile * LANES + wide] = done[:, 0:wide].astype(BF16)

    for r in range(count):
        target = place(me, r)
        for which, block in enumerate((target ^ half, target)):
            begin = pl.multiple_of(block * rows, HALO)
            o_refs[r][which] = a_ref[pl.ds(begin, window), :]


def normalize(values):
    average = jnp.mean(values, axis=-1, keepdims=True)
    centered = values - average
    spread = jnp.mean(centered * centered, axis=-1, keepdims=True)
    return centered * lax.rsqrt(spread + 1e-05)


def frame_kernel(
    count,
    rows,
    experts,
    capacity,
    place,
    flip,
    me_ref,
    expert_ref,
    len_ref,
    proj_ref,
    taps_ref,
    router_ref,
    routes_ref,
    turned_ref,
    *refs,
):
    att_refs, out_ref = refs[:count], refs[count]
    info_ref, second_ref, x_ref, first_ref, lab_ref = refs[-5:]
    me = me_ref[0]
    turn = expert_ref[0]
    window = rows + 2 * HALO
    half = (KERNEL - 1) // 2
    tiles = D // LANES
    step = 56
    which = 0 if flip else 1
    width = att_refs[0].shape[2]
    first = None
    for r in range(count):
        begin = pl.multiple_of(place(me, r) * width, HEAD_DIM)
        term = jnp.dot(
            att_refs[r][which], proj_ref[pl.ds(begin, width), :], preferred_element_type=F32
        )
        first = term if first is None else first + term
    normed = normalize(first).astype(BF16).astype(F32)
    origin = (me ^ flip) * rows
    frames = lax.broadcasted_iota(jnp.int32, (window, LANES), 0) + (origin - HALO)
    lab_ref[...] = labels_of(frames, len_ref)
    for tile in range(tiles):
        at = slice(tile * LANES, (tile + 1) * LANES)
        x_ref[tile] = normed[:, at]
        first_ref[tile] = first[HALO : HALO + rows, at]

    starts = [len_ref[0, 0], len_ref[0, 0] + len_ref[0, 1]]
    starts.append(starts[1] + len_ref[0, 2])
    for begin in range(0, rows, step):
        low = origin + begin - half
        high = low + step + 2 * half
        crossed = functools.reduce(
            jnp.logical_or, [(low < start) & (start < high) for start in starts]
        )

        def columns(tile, masked):
            total = jnp.zeros((step, LANES), F32)
            own = lab_ref[HALO + begin : HALO + begin + step, :] if masked else None
            for tap in range(KERNEL):
                source = HALO - half + begin + tap
                term = taps_ref[tile, tap : tap + 1, :] * x_ref[tile, source : source + step, :]
                if masked:
                    term = jnp.where(lab_ref[source : source + step, :] == own, term, 0.0)
                total = total + term
            gated = total / (1.0 + jnp.exp(-total))
            second_ref[tile, begin : begin + step, :] = (
                first_ref[tile, begin : begin + step, :] + gated
            )

        @pl.when(crossed)
        def _():
            lax.fori_loop(0, tiles, lambda tile, c: (columns(tile, True), c)[1], 0)

        @pl.when(jnp.logical_not(crossed))
        def _():
            lax.fori_loop(0, tiles, lambda tile, c: (columns(tile, False), c)[1], 0)

    second = jnp.concatenate([second_ref[tile] for tile in range(tiles)], axis=1)
    mixed = normalize(second).astype(BF16)

    logits = jnp.dot(mixed, router_ref[...], preferred_element_type=F32)
    lane = lax.broadcasted_iota(jnp.int32, (rows, experts), 1)
    named = [lane == routes_ref[:, pick : pick + 1] for pick in range(TOPK)]
    picked = [jnp.sum(jnp.where(one, logits, 0.0), axis=1, keepdims=True) for one in named]
    top = jnp.maximum(picked[0], picked[1])
    raised = [jnp.exp(one - top) for one in picked]
    mass = raised[0] + raised[1]
    down = lax.broadcasted_iota(jnp.int32, (rows, rows), 0)
    across = lax.broadcasted_iota(jnp.int32, (rows, rows), 1)
    picks = jnp.where(named[0] | named[1], 1.0, 0.0).astype(BF16)
    earlier = jnp.where(across < down, 1.0, 0.0).astype(BF16)
    ranks = jnp.dot(earlier, picks, preferred_element_type=F32)
    column = lax.broadcasted_iota(jnp.int32, (rows, LANES), 1)
    info = jnp.zeros((rows, LANES), F32)
    for pick in range(TOPK):
        rank = jnp.sum(jnp.where(named[pick], ranks, 0.0), axis=1, keepdims=True)
        place_of = routes_ref[:, pick : pick + 1] ^ turn
        slot = rank + (place_of * capacity).astype(F32)
        info = jnp.where(column == pick, slot, info)
        info = jnp.where(column == TOPK + pick, raised[pick] / mass, info)
    info_ref[...] = info

    expert = lax.broadcasted_iota(jnp.int32, (experts, rows), 0)
    chosen = (expert == turned_ref[0:1, :]) | (expert == turned_ref[1:2, :])
    later = jnp.where(down < across, 1.0, 0.0).astype(BF16)
    order = jnp.dot(jnp.where(chosen, 1.0, 0.0).astype(BF16), later, preferred_element_type=F32)
    order = jnp.where(chosen, order, -1.0)
    slot = lax.broadcasted_iota(jnp.int32, (capacity, rows), 0).astype(F32)
    select = jnp.concatenate(
        [jnp.where(slot == order[e : e + 1, :], 1.0, 0.0) for e in range(experts)], axis=0
    ).astype(BF16)
    out_ref[...] = jnp.dot(select, mixed, preferred_element_type=F32).astype(BF16)


def joined(refs):
    order = far_first(len(refs))
    parts = [refs[order.index(r)][...].astype(F32) for r in range(len(refs))]
    return jnp.concatenate(parts, axis=0).astype(BF16)


def expert_kernel(experts, units, spans, begun, expert_ref, *refs):
    results = max(1, experts)
    count = (len(refs) - results - 2) // 2
    sources, o_refs = refs[:count], refs[count : count + results]
    held, (sum_ref, sem_ref) = refs[count + results : -2], refs[-2:]
    copies = [
        pltpu.make_async_copy(sources[k], held[k], sem_ref.at[k]) for k in range(count)
    ]
    for copy in copies:
        copy.start()
    waiting = set(range(count))

    def ready(k):
        if k in waiting:
            waiting.remove(k)
            copies[k].wait()
        return held[k]

    tokens = ready(0)[...]
    products = []
    for (into, first), (out, second) in spans:
        raw = lax.dot_general(
            tokens,
            ready(1 + into)[first : first + units, :],
            (((1,), (1,)), ((), ())),
            preferred_element_type=F32,
        )
        hidden = (raw / (1.0 + jnp.exp(-raw))).astype(BF16)
        products.append(
            jnp.dot(hidden, ready(1 + out)[second : second + units, :], preferred_element_type=F32)
        )
    if begun:
        products.append(ready(count - 1)[...])
    total = functools.reduce(jnp.add, products)
    if experts == 0:
        o_refs[0][...] = total
        return
    sum_ref[...] = total
    tall = o_refs[0].shape[0]
    for r, o_ref in enumerate(o_refs):
        begin = pl.multiple_of((expert_ref[0] ^ r) * tall, 8)
        o_ref[...] = sum_ref[pl.ds(begin, tall), :].astype(BF16)


def mixture_of(info, back_refs):
    back = joined(back_refs)
    column = lax.broadcasted_iota(jnp.int32, (info.shape[0], back.shape[0]), 1).astype(F32)
    spread = jnp.where(column == info[:, 0:1], info[:, 2:3], 0.0)
    spread = jnp.where(column == info[:, 1:2], info[:, 3:4], spread).astype(BF16)
    return jnp.dot(spread, back, preferred_element_type=F32)


def theirs_kernel(info_ref, *refs):
    refs[-1][...] = mixture_of(info_ref[...], refs[:-1]).astype(BF16)


def mine_kernel(info_ref, second_ref, part_ref, *refs):
    o_ref = refs[-1]
    mixture = mixture_of(info_ref[...], refs[:-1])
    for tile in range(D // LANES):
        at = slice(tile * LANES, (tile + 1) * LANES)
        both = mixture[:, at] + part_ref[:, at].astype(F32)
        o_ref[:, at] = (second_ref[tile] + 0.5 * both).astype(BF16)


def crossed(count, direct, me, r):
    return me ^ r if direct else r


def trade(arrays, axis, direct=True):
    count = len(arrays)
    if not direct:
        mixed = lax.all_to_all(jnp.stack(arrays), axis, split_axis=0, concat_axis=0, tiled=True)
        return [mixed[r] for r in range(count)]
    moved = {
        r: lax.ppermute(arrays[r], axis, [(i, i ^ r) for i in range(count)])
        for r in range(count - 1, 0, -1)
    }
    return [arrays[0]] + [moved[r] for r in range(1, count)]


def far_first(count):
    return sorted(range(count), key=lambda r: (r == 0, -bin(r >> 1).count("1"), r))


def after(arrays, markers):
    return lax.optimization_barrier((*arrays, *markers))[: len(arrays)]


def body(
    query_rows,
    key_rows,
    value_rows,
    head_scale,
    out_proj,
    conv_taps,
    router,
    expert_in,
    expert_out,
    lengths,
    routes,
):
    rows = query_rows.shape[1]
    experts = lax.axis_size("dp")
    count = lax.axis_size("tm")
    half = count // 2
    heads = HEADS // count
    width = heads * HEAD_DIM
    window = rows + 2 * HALO
    capacity = -(-(3 * rows // experts) // 8) * 8
    direct = width % LANES == 0
    me = lax.axis_index("tm").astype(jnp.int32).reshape(1)
    expert = lax.axis_index("dp").astype(jnp.int32).reshape(1)
    partner = [(i, i ^ half) for i in range(count)]
    place = functools.partial(crossed, count, direct)

    packed = pl.pallas_call(
        functools.partial(pack_kernel, place),
        out_shape=(jax.ShapeDtypeStruct((3, rows, width), BF16),) * count,
        in_specs=[SMEM] + [pl.BlockSpec(memory_space=pltpu.HBM) if direct else VMEM] * 3,
        out_specs=(VMEM,) * count,
        scratch_shapes=[pltpu.SemaphoreType.DMA((3 * count,))],
        compiler_params=params(60),
        cost_estimate=cost(1),
        name="pack",
    )(me, query_rows[0], key_rows[0], value_rows[0])
    arrived = trade(packed, "tm", direct)
    scales = lax.dynamic_slice_in_dim(head_scale, me[0] * heads, heads)
    partner_routes = lax.ppermute(routes[0], "tm", partner)

    tiles = max(1, width // LANES)
    total = count * rows
    attended = pl.pallas_call(
        functools.partial(attend_kernel, count, rows, heads, place),
        out_shape=(jax.ShapeDtypeStruct((2, window, width), BF16),) * count,
        in_specs=[SMEM, SMEM, SMEM] + [VMEM] * count,
        out_specs=(VMEM,) * count,
        scratch_shapes=[
            pltpu.VMEM((tiles, total, 2 * LANES), BF16),
            pltpu.VMEM((tiles, total, 2 * LANES), BF16),
            pltpu.VMEM((total + 2 * HALO, width), BF16),
        ],
        compiler_params=params(16),
        cost_estimate=cost(6),
        name="attend",
    )(me, scales, lengths, *arrived)
    windows = trade(attended, "tm", direct)

    units = expert_in.shape[1]
    (shard,) = after((jnp.concatenate([expert_in[0], expert_out[0]]),), windows)
    if half == 2:
        moved = lax.ppermute(shard, "tm", [(i, i ^ 1) for i in range(count)])
        weights = [expert_in[0], expert_out[0], moved]
        spans = (((0, 0), (1, 0)), ((2, 0), (2, units)))
    else:
        groups = [list(range(i, i + half)) for i in (0, half)]
        weights = [
            lax.all_gather(one, "tm", axis=0, tiled=True, axis_index_groups=groups)
            for one in (shard[:units], shard[units:])
        ]
        units = units * half
        spans = (((0, 0), (1, 0)),)

    taps = jnp.transpose(conv_taps.reshape(KERNEL, D // LANES, LANES), (1, 0, 2))
    slots = experts * capacity

    def route(array):
        whole = array.reshape(experts, capacity, D)
        moved = lax.all_to_all(whole, "dp", split_axis=0, concat_axis=0, tiled=True)
        return (moved.reshape(slots, D),)

    def send_frames(windows, flip, block_routes):
        made = pl.pallas_call(
            functools.partial(frame_kernel, count, rows, experts, capacity, place, flip),
            out_shape=(
                jax.ShapeDtypeStruct((slots, D), BF16),
                jax.ShapeDtypeStruct((rows, LANES), F32),
                jax.ShapeDtypeStruct((D // LANES, rows, LANES), F32),
            ),
            in_specs=[SMEM, SMEM, SMEM] + [VMEM] * (5 + count),
            out_specs=(VMEM,) * 3,
            scratch_shapes=[
                pltpu.VMEM((D // LANES, window, LANES), F32),
                pltpu.VMEM((D // LANES, rows, LANES), F32),
                pltpu.VMEM((window, LANES), F32),
            ],
            compiler_params=params(56),
            cost_estimate=cost(10),
            name="frames",
        )(me, expert, lengths, out_proj, taps, router, block_routes, block_routes.T, *windows)
        return made

    def run_expert(tokens, matrices, parts, partial=(), last=True):
        operands = (*tokens, *matrices, *partial)
        if last:
            made = (jax.ShapeDtypeStruct((capacity, D), BF16),) * experts
        else:
            made = (jax.ShapeDtypeStruct((slots, D), F32),)
        kernel = functools.partial(
            expert_kernel, experts if last else 0, units, parts, len(partial) > 0
        )
        return pl.pallas_call(
            kernel,
            out_shape=made,
            in_specs=[SMEM] + [pl.BlockSpec(memory_space=pl.ANY)] * len(operands),
            out_specs=(VMEM,) * len(made),
            scratch_shapes=[pltpu.VMEM(one.shape, one.dtype) for one in operands]
            + [
                pltpu.VMEM((slots, D) if last else (8, LANES), F32),
                pltpu.SemaphoreType.DMA((len(operands),)),
            ],
            compiler_params=params(56),
            cost_estimate=cost(8 if len(parts) > 1 else 5),
            name="experts",
        )(expert, *operands)

    outgoing_a, info_a, _ = send_frames(windows, half, partner_routes)
    tokens_a = route(outgoing_a)
    windows = after(windows, (outgoing_a,))
    outgoing_b, info_b, second = send_frames(windows, 0, routes[0])
    tokens_b = route(after((outgoing_b,), tokens_a)[0])
    if half == 2:
        begun = run_expert(tokens_a, weights[:2], spans[:1], last=False)
        rest = (((0, 0), (0, units)),)
        produced_a = run_expert(tokens_a, weights[2:], rest, begun)
    else:
        produced_a = run_expert(tokens_a, weights, spans)
    back_a = trade(after(produced_a, tokens_b), "dp")
    produced_b = run_expert(after(tokens_b, produced_a), weights, spans)
    back_b = trade(produced_b, "dp")
    order = far_first(experts)
    back_a = after([back_a[r] for r in order], back_b[1:2])
    back_b = [back_b[r] for r in order]

    theirs = pl.pallas_call(
        theirs_kernel,
        out_shape=jax.ShapeDtypeStruct((rows, D), BF16),
        in_specs=[VMEM] * (1 + len(back_a)),
        out_specs=VMEM,
        compiler_params=params(16),
        cost_estimate=cost(1),
        name="theirs",
    )(info_a, *back_a)
    received = lax.ppermute(theirs, "tm", partner)
    out = pl.pallas_call(
        mine_kernel,
        out_shape=jax.ShapeDtypeStruct((rows, D), BF16),
        in_specs=[VMEM] * (3 + len(back_b)),
        out_specs=VMEM,
        compiler_params=params(16),
        cost_estimate=cost(1),
        name="mine",
    )(info_b, second, received, *back_b)
    return out[None]


def solution(mesh):
    return jax.shard_map(
        body,
        mesh=mesh,
        in_specs=(
            P("dp", "tm", None),
            P("dp", "tm", None),
            P("dp", "tm", None),
            P(),
            P(),
            P(),
            P(),
            P("dp", "tm", None),
            P("dp", "tm", None),
            P("dp", None),
            P("dp", "tm", None),
        ),
        out_specs=P("dp", "tm", None),
        check_vma=False,
    )
```

```python
import functools

import jax
import jax.numpy as jnp
from jax import lax
from jax.experimental import pallas as pl
from jax.experimental.pallas import tpu as pltpu
from jax.sharding import PartitionSpec as P

D = 1536
HEADS = 16
HEAD_DIM = 64
KERNEL = 31
TOPK = 2
RECS = 4
HALO = 16
LANES = 128
APART = 64.0
LOG2E = 1.4426950408889634
F32 = jnp.float32
BF16 = jnp.bfloat16
VMEM = pl.BlockSpec(memory_space=pltpu.VMEM)
SMEM = pl.BlockSpec(memory_space=pltpu.SMEM)


def params(mib):
    return pltpu.CompilerParams(vmem_limit_bytes=mib << 20)


def cost(micros):
    return pl.CostEstimate(flops=micros * 1_100_000_000, bytes_accessed=0, transcendentals=0)


def labels_of(frames, len_ref):
    first = len_ref[0, 0]
    second = first + len_ref[0, 1]
    third = second + len_ref[0, 2]
    return (
        (frames >= first).astype(F32)
        + (frames >= second).astype(F32)
        + (frames >= third).astype(F32)
    )


def unit_tile(tile, low):
    lifted = tile.astype(F32)
    square = lifted * lifted
    left = jnp.sum(jnp.where(low, square, 0.0), axis=1, keepdims=True)
    right = jnp.sum(jnp.where(low, 0.0, square), axis=1, keepdims=True)
    factor = jnp.where(low, lax.rsqrt(left + 1e-06), lax.rsqrt(right + 1e-06))
    return lifted * factor


def pack_kernel(place, me_ref, q_ref, k_ref, v_ref, *refs):
    o_refs, sem_ref = refs[:-1], refs[-1]
    width = o_refs[0].shape[2]
    copies = []
    for r in range(len(o_refs) - 1, -1, -1):
        target = place(me_ref[0], r)
        for which, ref in enumerate((q_ref, k_ref, v_ref)):
            if width % LANES == 0:
                columns = pl.ds(pl.multiple_of(target * width, LANES), width)
                copy = pltpu.make_async_copy(
                    ref.at[:, columns], o_refs[r].at[which], sem_ref.at[r * 3 + which]
                )
                copy.start()
                copies.append(copy)
            else:
                o_refs[r][which] = ref[:, target * width : (target + 1) * width]
    for copy in copies:
        copy.wait()


def attend_kernel(count, rows, heads, place, me_ref, scale_ref, len_ref, *refs):
    x_refs, o_refs = refs[:count], refs[count : 2 * count]
    k_ref, v_ref, a_ref = refs[2 * count :]
    me = me_ref[0]
    width = heads * HEAD_DIM
    tiles = max(1, width // LANES)
    half = count // 2
    window = rows + 2 * HALO

    def tile_of(r, which, tile):
        if width >= LANES:
            return x_refs[r][which, :, tile * LANES : (tile + 1) * LANES]
        piece = x_refs[r][which]
        return jnp.concatenate([piece, jnp.zeros((rows, LANES - width), BF16)], axis=1)

    low = lax.broadcasted_iota(jnp.int32, (rows, LANES), 1) < HEAD_DIM
    lane = lax.broadcasted_iota(jnp.int32, (rows, LANES), 1).astype(F32)
    row = lax.broadcasted_iota(jnp.int32, (rows, LANES), 0)

    edge = jnp.zeros((HALO, width), BF16)
    a_ref[0:HALO, :] = edge
    a_ref[HALO + count * rows :, :] = edge
    for r in range(count):
        at = slice(r * rows, (r + 1) * rows)
        label = labels_of(row + place(me, r) * rows, len_ref)
        other = jnp.where((lane >= 1.0) & (lane <= 4.0) & (lane != label + 1.0), -APART, 0.0)
        extra = jnp.where(lane == 0.0, -1.0, other).astype(BF16)
        for tile in range(tiles):
            k_ref[tile, at, 0:LANES] = unit_tile(tile_of(r, 1, tile), low).astype(BF16)
            k_ref[tile, at, LANES:] = extra
            v_ref[tile, at, 0:LANES] = tile_of(r, 2, tile)
            v_ref[tile, at, LANES:] = jnp.ones((rows, LANES), BF16)

    for r in range(count):
        block = place(me, r)
        label = labels_of(row + block * rows, len_ref)
        extra = jnp.where((lane == 0.0) | (lane == label + 1.0), 1.0, 0.0).astype(BF16)
        for tile in range(tiles):
            unit = unit_tile(tile_of(r, 0, tile), low)
            parts = []
            for side in range(min(2, heads)):
                head = tile * 2 + side
                kept = jnp.where(low if side == 0 else ~low, unit, 0.0).astype(BF16)
                query = jnp.concatenate([kept, extra], axis=1)
                scores = lax.dot_general(
                    query, k_ref[tile], (((1,), (1,)), ((), ())), preferred_element_type=F32
                )
                weights = jnp.exp2(scores * (scale_ref[head] * LOG2E)).astype(BF16)
                summed = jnp.dot(weights, v_ref[tile], preferred_element_type=F32)
                parts.append(summed[:, 0:LANES] / summed[:, LANES:])
            done = parts[0] if len(parts) == 1 else jnp.where(low, parts[0], parts[1])
            start = pl.multiple_of(HALO + block * rows, HALO)
            wide = min(LANES, width)
            a_ref[pl.ds(start, rows), tile * LANES : tile * LANES + wide] = done[:, 0:wide].astype(BF16)

    for r in range(count):
        target = place(me, r)
        for which, block in enumerate((target ^ half, target)):
            begin = pl.multiple_of(block * rows, HALO)
            o_refs[r][which] = a_ref[pl.ds(begin, window), :]


def normalize(values):
    average = jnp.mean(values, axis=-1, keepdims=True)
    centered = values - average
    spread = jnp.mean(centered * centered, axis=-1, keepdims=True)
    return centered * lax.rsqrt(spread + 1e-05)


def frame_kernel(
    count,
    rows,
    experts,
    capacity,
    place,
    flip,
    me_ref,
    expert_ref,
    len_ref,
    proj_ref,
    taps_ref,
    router_ref,
    routes_ref,
    turned_ref,
    *refs,
):
    att_refs, out_ref = refs[:count], refs[count]
    info_ref, second_ref, x_ref, first_ref, lab_ref = refs[-5:]
    me = me_ref[0]
    turn = expert_ref[0]
    window = rows + 2 * HALO
    half = (KERNEL - 1) // 2
    tiles = D // LANES
    step = 56
    which = 0 if flip else 1
    width = att_refs[0].shape[2]
    first = None
    for r in range(count):
        begin = pl.multiple_of(place(me, r) * width, HEAD_DIM)
        term = jnp.dot(
            att_refs[r][which], proj_ref[pl.ds(begin, width), :], preferred_element_type=F32
        )
        first = term if first is None else first + term
    normed = normalize(first).astype(BF16).astype(F32)
    origin = (me ^ flip) * rows
    frames = lax.broadcasted_iota(jnp.int32, (window, LANES), 0) + (origin - HALO)
    lab_ref[...] = labels_of(frames, len_ref)
    for tile in range(tiles):
        at = slice(tile * LANES, (tile + 1) * LANES)
        x_ref[tile] = normed[:, at]
        first_ref[tile] = first[HALO : HALO + rows, at]

    starts = [len_ref[0, 0], len_ref[0, 0] + len_ref[0, 1]]
    starts.append(starts[1] + len_ref[0, 2])
    for begin in range(0, rows, step):
        low = origin + begin - half
        high = low + step + 2 * half
        crossed = functools.reduce(
            jnp.logical_or, [(low < start) & (start < high) for start in starts]
        )

        def columns(tile, masked):
            total = jnp.zeros((step, LANES), F32)
            own = lab_ref[HALO + begin : HALO + begin + step, :] if masked else None
            for tap in range(KERNEL):
                source = HALO - half + begin + tap
                term = taps_ref[tile, tap : tap + 1, :] * x_ref[tile, source : source + step, :]
                if masked:
                    term = jnp.where(lab_ref[source : source + step, :] == own, term, 0.0)
                total = total + term
            gated = total / (1.0 + jnp.exp(-total))
            second_ref[tile, begin : begin + step, :] = (
                first_ref[tile, begin : begin + step, :] + gated
            )

        @pl.when(crossed)
        def _():
            lax.fori_loop(0, tiles, lambda tile, c: (columns(tile, True), c)[1], 0)

        @pl.when(jnp.logical_not(crossed))
        def _():
            lax.fori_loop(0, tiles, lambda tile, c: (columns(tile, False), c)[1], 0)

    second = jnp.concatenate([second_ref[tile] for tile in range(tiles)], axis=1)
    mixed = normalize(second).astype(BF16)

    logits = jnp.dot(mixed, router_ref[...], preferred_element_type=F32)
    lane = lax.broadcasted_iota(jnp.int32, (rows, experts), 1)
    named = [lane == routes_ref[:, pick : pick + 1] for pick in range(TOPK)]
    picked = [jnp.sum(jnp.where(one, logits, 0.0), axis=1, keepdims=True) for one in named]
    top = jnp.maximum(picked[0], picked[1])
    raised = [jnp.exp(one - top) for one in picked]
    mass = raised[0] + raised[1]
    down = lax.broadcasted_iota(jnp.int32, (rows, rows), 0)
    across = lax.broadcasted_iota(jnp.int32, (rows, rows), 1)
    picks = jnp.where(named[0] | named[1], 1.0, 0.0).astype(BF16)
    earlier = jnp.where(across < down, 1.0, 0.0).astype(BF16)
    ranks = jnp.dot(earlier, picks, preferred_element_type=F32)
    column = lax.broadcasted_iota(jnp.int32, (rows, LANES), 1)
    info = jnp.zeros((rows, LANES), F32)
    for pick in range(TOPK):
        rank = jnp.sum(jnp.where(named[pick], ranks, 0.0), axis=1, keepdims=True)
        place_of = routes_ref[:, pick : pick + 1] ^ turn
        slot = rank + (place_of * capacity).astype(F32)
        info = jnp.where(column == pick, slot, info)
        info = jnp.where(column == TOPK + pick, raised[pick] / mass, info)
    info_ref[...] = info

    expert = lax.broadcasted_iota(jnp.int32, (experts, rows), 0)
    chosen = (expert == turned_ref[0:1, :]) | (expert == turned_ref[1:2, :])
    later = jnp.where(down < across, 1.0, 0.0).astype(BF16)
    order = jnp.dot(jnp.where(chosen, 1.0, 0.0).astype(BF16), later, preferred_element_type=F32)
    order = jnp.where(chosen, order, -1.0)
    slot = lax.broadcasted_iota(jnp.int32, (capacity, rows), 0).astype(F32)
    select = jnp.concatenate(
        [jnp.where(slot == order[e : e + 1, :], 1.0, 0.0) for e in range(experts)], axis=0
    ).astype(BF16)
    out_ref[...] = jnp.dot(select, mixed, preferred_element_type=F32).astype(BF16)


def joined(refs):
    order = far_first(len(refs))
    parts = [refs[order.index(r)][...].astype(F32) for r in range(len(refs))]
    return jnp.concatenate(parts, axis=0).astype(BF16)


def expert_kernel(experts, units, spans, begun, expert_ref, *refs):
    results = max(1, experts)
    count = (len(refs) - results - 2) // 2
    sources, o_refs = refs[:count], refs[count : count + results]
    held, (sum_ref, sem_ref) = refs[count + results : -2], refs[-2:]
    copies = [
        pltpu.make_async_copy(sources[k], held[k], sem_ref.at[k]) for k in range(count)
    ]
    for copy in copies:
        copy.start()
    waiting = set(range(count))

    def ready(k):
        if k in waiting:
            waiting.remove(k)
            copies[k].wait()
        return held[k]

    tokens = ready(0)[...]
    products = []
    for (into, first), (out, second) in spans:
        raw = lax.dot_general(
            tokens,
            ready(1 + into)[first : first + units, :],
            (((1,), (1,)), ((), ())),
            preferred_element_type=F32,
        )
        hidden = (raw / (1.0 + jnp.exp(-raw))).astype(BF16)
        products.append(
            jnp.dot(hidden, ready(1 + out)[second : second + units, :], preferred_element_type=F32)
        )
    if begun:
        products.append(ready(count - 1)[...])
    total = functools.reduce(jnp.add, products)
    if experts == 0:
        o_refs[0][...] = total
        return
    sum_ref[...] = total
    tall = o_refs[0].shape[0]
    for r, o_ref in enumerate(o_refs):
        begin = pl.multiple_of((expert_ref[0] ^ r) * tall, 8)
        o_ref[...] = sum_ref[pl.ds(begin, tall), :].astype(BF16)


def mixture_of(info, back_refs):
    back = joined(back_refs)
    column = lax.broadcasted_iota(jnp.int32, (info.shape[0], back.shape[0]), 1).astype(F32)
    spread = jnp.where(column == info[:, 0:1], info[:, 2:3], 0.0)
    spread = jnp.where(column == info[:, 1:2], info[:, 3:4], spread).astype(BF16)
    return jnp.dot(spread, back, preferred_element_type=F32)


def theirs_kernel(info_ref, *refs):
    refs[-1][...] = mixture_of(info_ref[...], refs[:-1]).astype(BF16)


def mine_kernel(info_ref, second_ref, part_ref, *refs):
    o_ref = refs[-1]
    mixture = mixture_of(info_ref[...], refs[:-1])
    for tile in range(D // LANES):
        at = slice(tile * LANES, (tile + 1) * LANES)
        both = mixture[:, at] + part_ref[:, at].astype(F32)
        o_ref[:, at] = (second_ref[tile] + 0.5 * both).astype(BF16)


def crossed(count, direct, me, r):
    return me ^ r if direct else r


def trade(arrays, axis, direct=True):
    count = len(arrays)
    if not direct:
        mixed = lax.all_to_all(jnp.stack(arrays), axis, split_axis=0, concat_axis=0, tiled=True)
        return [mixed[r] for r in range(count)]
    moved = {
        r: lax.ppermute(arrays[r], axis, [(i, i ^ r) for i in range(count)])
        for r in range(count - 1, 0, -1)
    }
    return [arrays[0]] + [moved[r] for r in range(1, count)]


def far_first(count):
    return sorted(range(count), key=lambda r: (r == 0, -bin(r >> 1).count("1"), r))


def after(arrays, markers):
    return lax.optimization_barrier((*arrays, *markers))[: len(arrays)]


def body(
    query_rows,
    key_rows,
    value_rows,
    head_scale,
    out_proj,
    conv_taps,
    router,
    expert_in,
    expert_out,
    lengths,
    routes,
):
    rows = query_rows.shape[1]
    experts = lax.axis_size("dp")
    count = lax.axis_size("tm")
    half = count // 2
    heads = HEADS // count
    width = heads * HEAD_DIM
    window = rows + 2 * HALO
    capacity = -(-(3 * rows // experts) // 8) * 8
    direct = width % LANES == 0
    me = lax.axis_index("tm").astype(jnp.int32).reshape(1)
    expert = lax.axis_index("dp").astype(jnp.int32).reshape(1)
    partner = [(i, i ^ half) for i in range(count)]
    place = functools.partial(crossed, count, direct)

    packed = pl.pallas_call(
        functools.partial(pack_kernel, place),
        out_shape=(jax.ShapeDtypeStruct((3, rows, width), BF16),) * count,
        in_specs=[SMEM] + [pl.BlockSpec(memory_space=pltpu.HBM) if direct else VMEM] * 3,
        out_specs=(VMEM,) * count,
        scratch_shapes=[pltpu.SemaphoreType.DMA((3 * count,))],
        compiler_params=params(60),
        cost_estimate=cost(1),
        name="pack",
    )(me, query_rows[0], key_rows[0], value_rows[0])
    arrived = trade(packed, "tm", direct)
    scales = lax.dynamic_slice_in_dim(head_scale, me[0] * heads, heads)
    partner_routes = lax.ppermute(routes[0], "tm", partner)

    tiles = max(1, width // LANES)
    total = count * rows
    attended = pl.pallas_call(
        functools.partial(attend_kernel, count, rows, heads, place),
        out_shape=(jax.ShapeDtypeStruct((2, window, width), BF16),) * count,
        in_specs=[SMEM, SMEM, SMEM] + [VMEM] * count,
        out_specs=(VMEM,) * count,
        scratch_shapes=[
            pltpu.VMEM((tiles, total, 2 * LANES), BF16),
            pltpu.VMEM((tiles, total, 2 * LANES), BF16),
            pltpu.VMEM((total + 2 * HALO, width), BF16),
        ],
        compiler_params=params(16),
        cost_estimate=cost(6),
        name="attend",
    )(me, scales, lengths, *arrived)
    windows = trade(attended, "tm", direct)

    units = expert_in.shape[1]
    (shard,) = after((jnp.concatenate([expert_in[0], expert_out[0]]),), windows)
    if half == 2:
        moved = lax.ppermute(shard, "tm", [(i, i ^ 1) for i in range(count)])
        weights = [expert_in[0], expert_out[0], moved]
        spans = (((0, 0), (1, 0)), ((2, 0), (2, units)))
    else:
        groups = [list(range(i, i + half)) for i in (0, half)]
        weights = [
            lax.all_gather(one, "tm", axis=0, tiled=True, axis_index_groups=groups)
            for one in (shard[:units], shard[units:])
        ]
        units = units * half
        spans = (((0, 0), (1, 0)),)

    taps = jnp.transpose(conv_taps.reshape(KERNEL, D // LANES, LANES), (1, 0, 2))
    slots = experts * capacity

    def route(array):
        whole = array.reshape(experts, capacity, D)
        moved = lax.all_to_all(whole, "dp", split_axis=0, concat_axis=0, tiled=True)
        return (moved.reshape(slots, D),)

    def send_frames(windows, flip, block_routes):
        made = pl.pallas_call(
            functools.partial(frame_kernel, count, rows, experts, capacity, place, flip),
            out_shape=(
                jax.ShapeDtypeStruct((slots, D), BF16),
                jax.ShapeDtypeStruct((rows, LANES), F32),
                jax.ShapeDtypeStruct((D // LANES, rows, LANES), F32),
            ),
            in_specs=[SMEM, SMEM, SMEM] + [VMEM] * (5 + count),
            out_specs=(VMEM,) * 3,
            scratch_shapes=[
                pltpu.VMEM((D // LANES, window, LANES), F32),
                pltpu.VMEM((D // LANES, rows, LANES), F32),
                pltpu.VMEM((window, LANES), F32),
            ],
            compiler_params=params(56),
            cost_estimate=cost(7),
            name="frames",
        )(me, expert, lengths, out_proj, taps, router, block_routes, block_routes.T, *windows)
        return made

    def run_expert(tokens, matrices, parts, partial=(), last=True):
        operands = (*tokens, *matrices, *partial)
        if last:
            made = (jax.ShapeDtypeStruct((capacity, D), BF16),) * experts
        else:
            made = (jax.ShapeDtypeStruct((slots, D), F32),)
        kernel = functools.partial(
            expert_kernel, experts if last else 0, units, parts, len(partial) > 0
        )
        return pl.pallas_call(
            kernel,
            out_shape=made,
            in_specs=[SMEM] + [pl.BlockSpec(memory_space=pl.ANY)] * len(operands),
            out_specs=(VMEM,) * len(made),
            scratch_shapes=[pltpu.VMEM(one.shape, one.dtype) for one in operands]
            + [
                pltpu.VMEM((slots, D) if last else (8, LANES), F32),
                pltpu.SemaphoreType.DMA((len(operands),)),
            ],
            compiler_params=params(56),
            cost_estimate=cost(8 if last else 0),
            name="experts",
        )(expert, *operands)

    outgoing_a, info_a, _ = send_frames(windows, half, partner_routes)
    tokens_a = route(outgoing_a)
    windows = after(windows, (outgoing_a,))
    outgoing_b, info_b, second = send_frames(windows, 0, routes[0])
    tokens_b = route(after((outgoing_b,), tokens_a)[0])
    if half == 2:
        begun = run_expert(tokens_a, weights[:2], spans[:1], last=False)
        rest = (((0, 0), (0, units)),)
        produced_a = run_expert(tokens_a, weights[2:], rest, begun)
    else:
        produced_a = run_expert(tokens_a, weights, spans)
    back_a = trade(after(produced_a, tokens_b), "dp")
    produced_b = run_expert(after(tokens_b, produced_a), weights, spans)
    back_b = trade(produced_b, "dp")
    order = far_first(experts)
    back_a = after([back_a[r] for r in order], back_b[1:2])
    back_b = [back_b[r] for r in order]

    theirs = pl.pallas_call(
        theirs_kernel,
        out_shape=jax.ShapeDtypeStruct((rows, D), BF16),
        in_specs=[VMEM] * (1 + len(back_a)),
        out_specs=VMEM,
        compiler_params=params(16),
        cost_estimate=cost(1),
        name="theirs",
    )(info_a, *back_a)
    received = lax.ppermute(theirs, "tm", partner)
    out = pl.pallas_call(
        mine_kernel,
        out_shape=jax.ShapeDtypeStruct((rows, D), BF16),
        in_specs=[VMEM] * (3 + len(back_b)),
        out_specs=VMEM,
        compiler_params=params(16),
        cost_estimate=cost(1),
        name="mine",
    )(info_b, second, received, *back_b)
    return out[None]


def solution(mesh):
    return jax.shard_map(
        body,
        mesh=mesh,
        in_specs=(
            P("dp", "tm", None),
            P("dp", "tm", None),
            P("dp", "tm", None),
            P(),
            P(),
            P(),
            P(),
            P("dp", "tm", None),
            P("dp", "tm", None),
            P("dp", None),
            P("dp", "tm", None),
        ),
        out_specs=P("dp", "tm", None),
        check_vma=False,
    )
```

```python
import functools

import jax
import jax.numpy as jnp
from jax import lax
from jax.experimental import pallas as pl
from jax.experimental.pallas import tpu as pltpu
from jax.sharding import PartitionSpec as P

D = 1536
HEADS = 16
HEAD_DIM = 64
KERNEL = 31
TOPK = 2
RECS = 4
HALO = 16
LANES = 128
APART = 64.0
LOG2E = 1.4426950408889634
F32 = jnp.float32
BF16 = jnp.bfloat16
VMEM = pl.BlockSpec(memory_space=pltpu.VMEM)
SMEM = pl.BlockSpec(memory_space=pltpu.SMEM)


def params(mib):
    return pltpu.CompilerParams(vmem_limit_bytes=mib << 20)


def cost(micros):
    return pl.CostEstimate(flops=micros * 1_100_000_000, bytes_accessed=0, transcendentals=0)


def labels_of(frames, len_ref):
    first = len_ref[0, 0]
    second = first + len_ref[0, 1]
    third = second + len_ref[0, 2]
    return (
        (frames >= first).astype(F32)
        + (frames >= second).astype(F32)
        + (frames >= third).astype(F32)
    )


def unit_tile(tile, low):
    lifted = tile.astype(F32)
    square = lifted * lifted
    left = jnp.sum(jnp.where(low, square, 0.0), axis=1, keepdims=True)
    right = jnp.sum(jnp.where(low, 0.0, square), axis=1, keepdims=True)
    factor = jnp.where(low, lax.rsqrt(left + 1e-06), lax.rsqrt(right + 1e-06))
    return lifted * factor


def pack_kernel(place, me_ref, q_ref, k_ref, v_ref, *refs):
    o_refs, sem_ref = refs[:-1], refs[-1]
    width = o_refs[0].shape[2]
    copies = []
    for r in range(len(o_refs) - 1, -1, -1):
        target = place(me_ref[0], r)
        for which, ref in enumerate((q_ref, k_ref, v_ref)):
            if width % LANES == 0:
                columns = pl.ds(pl.multiple_of(target * width, LANES), width)
                copy = pltpu.make_async_copy(
                    ref.at[:, columns], o_refs[r].at[which], sem_ref.at[r * 3 + which]
                )
                copy.start()
                copies.append(copy)
            else:
                o_refs[r][which] = ref[:, target * width : (target + 1) * width]
    for copy in copies:
        copy.wait()


def attend_kernel(count, rows, heads, place, me_ref, scale_ref, len_ref, *refs):
    x_refs, o_refs = refs[:count][::-1], refs[count : 2 * count]
    k_ref, v_ref, a_ref = refs[2 * count :]
    me = me_ref[0]
    width = heads * HEAD_DIM
    tiles = max(1, width // LANES)
    half = count // 2
    window = rows + 2 * HALO

    def tile_of(r, which, tile):
        if width >= LANES:
            return x_refs[r][which, :, tile * LANES : (tile + 1) * LANES]
        piece = x_refs[r][which]
        return jnp.concatenate([piece, jnp.zeros((rows, LANES - width), BF16)], axis=1)

    low = lax.broadcasted_iota(jnp.int32, (rows, LANES), 1) < HEAD_DIM
    lane = lax.broadcasted_iota(jnp.int32, (rows, LANES), 1).astype(F32)
    row = lax.broadcasted_iota(jnp.int32, (rows, LANES), 0)

    edge = jnp.zeros((HALO, width), BF16)
    a_ref[0:HALO, :] = edge
    a_ref[HALO + count * rows :, :] = edge
    for r in range(count):
        at = slice(r * rows, (r + 1) * rows)
        label = labels_of(row + place(me, r) * rows, len_ref)
        other = jnp.where((lane >= 1.0) & (lane <= 4.0) & (lane != label + 1.0), -APART, 0.0)
        extra = jnp.where(lane == 0.0, -1.0, other).astype(BF16)
        for tile in range(tiles):
            k_ref[tile, at, 0:LANES] = unit_tile(tile_of(r, 1, tile), low).astype(BF16)
            k_ref[tile, at, LANES:] = extra
            v_ref[tile, at, 0:LANES] = tile_of(r, 2, tile)
            v_ref[tile, at, LANES:] = jnp.ones((rows, LANES), BF16)

    for r in range(count):
        block = place(me, r)
        label = labels_of(row + block * rows, len_ref)
        extra = jnp.where((lane == 0.0) | (lane == label + 1.0), 1.0, 0.0).astype(BF16)
        for tile in range(tiles):
            unit = unit_tile(tile_of(r, 0, tile), low)
            parts = []
            for side in range(min(2, heads)):
                head = tile * 2 + side
                kept = jnp.where(low if side == 0 else ~low, unit, 0.0).astype(BF16)
                query = jnp.concatenate([kept, extra], axis=1)
                scores = lax.dot_general(
                    query, k_ref[tile], (((1,), (1,)), ((), ())), preferred_element_type=F32
                )
                weights = jnp.exp2(scores * (scale_ref[head] * LOG2E)).astype(BF16)
                summed = jnp.dot(weights, v_ref[tile], preferred_element_type=F32)
                parts.append(summed[:, 0:LANES] / summed[:, LANES:])
            done = parts[0] if len(parts) == 1 else jnp.where(low, parts[0], parts[1])
            start = pl.multiple_of(HALO + block * rows, HALO)
            wide = min(LANES, width)
            a_ref[pl.ds(start, rows), tile * LANES : tile * LANES + wide] = done[:, 0:wide].astype(BF16)

    for r in range(count):
        target = place(me, r)
        for which, block in enumerate((target ^ half, target)):
            begin = pl.multiple_of(block * rows, HALO)
            o_refs[r][which] = a_ref[pl.ds(begin, window), :]


def normalize(values):
    average = jnp.mean(values, axis=-1, keepdims=True)
    centered = values - average
    spread = jnp.mean(centered * centered, axis=-1, keepdims=True)
    return centered * lax.rsqrt(spread + 1e-05)


def frame_kernel(
    count,
    rows,
    experts,
    capacity,
    place,
    flip,
    me_ref,
    expert_ref,
    len_ref,
    proj_ref,
    taps_ref,
    router_ref,
    routes_ref,
    turned_ref,
    *refs,
):
    att_refs, out_ref = refs[:count][::-1], refs[count]
    info_ref, second_ref, x_ref, first_ref, lab_ref = refs[-5:]
    me = me_ref[0]
    turn = expert_ref[0]
    window = rows + 2 * HALO
    half = (KERNEL - 1) // 2
    tiles = D // LANES
    step = 56
    which = 0 if flip else 1
    width = att_refs[0].shape[2]
    first = None
    for r in range(count):
        begin = pl.multiple_of(place(me, r) * width, HEAD_DIM)
        term = jnp.dot(
            att_refs[r][which], proj_ref[pl.ds(begin, width), :], preferred_element_type=F32
        )
        first = term if first is None else first + term
    normed = normalize(first).astype(BF16).astype(F32)
    origin = (me ^ flip) * rows
    frames = lax.broadcasted_iota(jnp.int32, (window, LANES), 0) + (origin - HALO)
    lab_ref[...] = labels_of(frames, len_ref)
    for tile in range(tiles):
        at = slice(tile * LANES, (tile + 1) * LANES)
        x_ref[tile] = normed[:, at]
        first_ref[tile] = first[HALO : HALO + rows, at]

    starts = [len_ref[0, 0], len_ref[0, 0] + len_ref[0, 1]]
    starts.append(starts[1] + len_ref[0, 2])
    for begin in range(0, rows, step):
        low = origin + begin - half
        high = low + step + 2 * half
        crossed = functools.reduce(
            jnp.logical_or, [(low < start) & (start < high) for start in starts]
        )

        def columns(tile, masked):
            total = jnp.zeros((step, LANES), F32)
            own = lab_ref[HALO + begin : HALO + begin + step, :] if masked else None
            for tap in range(KERNEL):
                source = HALO - half + begin + tap
                term = taps_ref[tile, tap : tap + 1, :] * x_ref[tile, source : source + step, :]
                if masked:
                    term = jnp.where(lab_ref[source : source + step, :] == own, term, 0.0)
                total = total + term
            gated = total / (1.0 + jnp.exp(-total))
            second_ref[tile, begin : begin + step, :] = (
                first_ref[tile, begin : begin + step, :] + gated
            )

        @pl.when(crossed)
        def _():
            lax.fori_loop(0, tiles, lambda tile, c: (columns(tile, True), c)[1], 0)

        @pl.when(jnp.logical_not(crossed))
        def _():
            lax.fori_loop(0, tiles, lambda tile, c: (columns(tile, False), c)[1], 0)

    second = jnp.concatenate([second_ref[tile] for tile in range(tiles)], axis=1)
    mixed = normalize(second).astype(BF16)

    logits = jnp.dot(mixed, router_ref[...], preferred_element_type=F32)
    lane = lax.broadcasted_iota(jnp.int32, (rows, experts), 1)
    named = [lane == routes_ref[:, pick : pick + 1] for pick in range(TOPK)]
    picked = [jnp.sum(jnp.where(one, logits, 0.0), axis=1, keepdims=True) for one in named]
    top = jnp.maximum(picked[0], picked[1])
    raised = [jnp.exp(one - top) for one in picked]
    mass = raised[0] + raised[1]
    down = lax.broadcasted_iota(jnp.int32, (rows, rows), 0)
    across = lax.broadcasted_iota(jnp.int32, (rows, rows), 1)
    picks = jnp.where(named[0] | named[1], 1.0, 0.0).astype(BF16)
    earlier = jnp.where(across < down, 1.0, 0.0).astype(BF16)
    ranks = jnp.dot(earlier, picks, preferred_element_type=F32)
    column = lax.broadcasted_iota(jnp.int32, (rows, LANES), 1)
    info = jnp.zeros((rows, LANES), F32)
    for pick in range(TOPK):
        rank = jnp.sum(jnp.where(named[pick], ranks, 0.0), axis=1, keepdims=True)
        place_of = routes_ref[:, pick : pick + 1] ^ turn
        slot = rank + (place_of * capacity).astype(F32)
        info = jnp.where(column == pick, slot, info)
        info = jnp.where(column == TOPK + pick, raised[pick] / mass, info)
    info_ref[...] = info

    expert = lax.broadcasted_iota(jnp.int32, (experts, rows), 0)
    chosen = (expert == turned_ref[0:1, :]) | (expert == turned_ref[1:2, :])
    later = jnp.where(down < across, 1.0, 0.0).astype(BF16)
    order = jnp.dot(jnp.where(chosen, 1.0, 0.0).astype(BF16), later, preferred_element_type=F32)
    order = jnp.where(chosen, order, -1.0)
    slot = lax.broadcasted_iota(jnp.int32, (capacity, rows), 0).astype(F32)
    select = jnp.concatenate(
        [jnp.where(slot == order[e : e + 1, :], 1.0, 0.0) for e in range(experts)], axis=0
    ).astype(BF16)
    out_ref[...] = jnp.dot(select, mixed, preferred_element_type=F32).astype(BF16)


def joined(refs):
    order = far_first(len(refs))
    parts = [refs[order.index(r)][...].astype(F32) for r in range(len(refs))]
    return jnp.concatenate(parts, axis=0).astype(BF16)


def expert_kernel(experts, units, spans, begun, expert_ref, *refs):
    results = max(1, experts)
    count = (len(refs) - results - 2) // 2
    sources, o_refs = refs[:count], refs[count : count + results]
    held, (sum_ref, sem_ref) = refs[count + results : -2], refs[-2:]
    copies = [
        pltpu.make_async_copy(sources[k], held[k], sem_ref.at[k]) for k in range(count)
    ]
    for copy in copies:
        copy.start()
    waiting = set(range(count))

    def ready(k):
        if k in waiting:
            waiting.remove(k)
            copies[k].wait()
        return held[k]

    tokens = ready(0)[...]
    products = []
    for (into, first), (out, second) in spans:
        raw = lax.dot_general(
            tokens,
            ready(1 + into)[first : first + units, :],
            (((1,), (1,)), ((), ())),
            preferred_element_type=F32,
        )
        hidden = (raw / (1.0 + jnp.exp(-raw))).astype(BF16)
        products.append(
            jnp.dot(hidden, ready(1 + out)[second : second + units, :], preferred_element_type=F32)
        )
    if begun:
        products.append(ready(count - 1)[...])
    total = functools.reduce(jnp.add, products)
    if experts == 0:
        o_refs[0][...] = total
        return
    sum_ref[...] = total
    tall = o_refs[0].shape[0]
    for r, o_ref in enumerate(o_refs):
        begin = pl.multiple_of((expert_ref[0] ^ r) * tall, 8)
        o_ref[...] = sum_ref[pl.ds(begin, tall), :].astype(BF16)


def mixture_of(info, back_refs):
    back = joined(back_refs)
    column = lax.broadcasted_iota(jnp.int32, (info.shape[0], back.shape[0]), 1).astype(F32)
    spread = jnp.where(column == info[:, 0:1], info[:, 2:3], 0.0)
    spread = jnp.where(column == info[:, 1:2], info[:, 3:4], spread).astype(BF16)
    return jnp.dot(spread, back, preferred_element_type=F32)


def theirs_kernel(info_ref, *refs):
    refs[-1][...] = mixture_of(info_ref[...], refs[:-1]).astype(BF16)


def mine_kernel(info_ref, second_ref, part_ref, *refs):
    o_ref = refs[-1]
    mixture = mixture_of(info_ref[...], refs[:-1])
    for tile in range(D // LANES):
        at = slice(tile * LANES, (tile + 1) * LANES)
        both = mixture[:, at] + part_ref[:, at].astype(F32)
        o_ref[:, at] = (second_ref[tile] + 0.5 * both).astype(BF16)


def crossed(count, direct, me, r):
    return me ^ r if direct else r


def trade(arrays, axis, direct=True):
    count = len(arrays)
    if not direct:
        mixed = lax.all_to_all(jnp.stack(arrays), axis, split_axis=0, concat_axis=0, tiled=True)
        return [mixed[r] for r in range(count)]
    moved = {
        r: lax.ppermute(arrays[r], axis, [(i, i ^ r) for i in range(count)])
        for r in range(count - 1, 0, -1)
    }
    return [arrays[0]] + [moved[r] for r in range(1, count)]


def far_first(count):
    return sorted(range(count), key=lambda r: (r == 0, -bin(r >> 1).count("1"), r))


def after(arrays, markers):
    return lax.optimization_barrier((*arrays, *markers))[: len(arrays)]


def body(
    query_rows,
    key_rows,
    value_rows,
    head_scale,
    out_proj,
    conv_taps,
    router,
    expert_in,
    expert_out,
    lengths,
    routes,
):
    rows = query_rows.shape[1]
    experts = lax.axis_size("dp")
    count = lax.axis_size("tm")
    half = count // 2
    heads = HEADS // count
    width = heads * HEAD_DIM
    window = rows + 2 * HALO
    capacity = -(-(3 * rows // experts) // 8) * 8
    direct = width % LANES == 0
    me = lax.axis_index("tm").astype(jnp.int32).reshape(1)
    expert = lax.axis_index("dp").astype(jnp.int32).reshape(1)
    partner = [(i, i ^ half) for i in range(count)]
    place = functools.partial(crossed, count, direct)

    packed = pl.pallas_call(
        functools.partial(pack_kernel, place),
        out_shape=(jax.ShapeDtypeStruct((3, rows, width), BF16),) * count,
        in_specs=[SMEM] + [pl.BlockSpec(memory_space=pltpu.HBM) if direct else VMEM] * 3,
        out_specs=(VMEM,) * count,
        scratch_shapes=[pltpu.SemaphoreType.DMA((3 * count,))],
        compiler_params=params(60),
        cost_estimate=cost(1),
        name="pack",
    )(me, query_rows[0], key_rows[0], value_rows[0])
    arrived = trade(packed, "tm", direct)
    scales = lax.dynamic_slice_in_dim(head_scale, me[0] * heads, heads)
    partner_routes = lax.ppermute(routes[0], "tm", partner)

    tiles = max(1, width // LANES)
    total = count * rows
    attended = pl.pallas_call(
        functools.partial(attend_kernel, count, rows, heads, place),
        out_shape=(jax.ShapeDtypeStruct((2, window, width), BF16),) * count,
        in_specs=[SMEM, SMEM, SMEM] + [VMEM] * count,
        out_specs=(VMEM,) * count,
        scratch_shapes=[
            pltpu.VMEM((tiles, total, 2 * LANES), BF16),
            pltpu.VMEM((tiles, total, 2 * LANES), BF16),
            pltpu.VMEM((total + 2 * HALO, width), BF16),
        ],
        compiler_params=params(16),
        cost_estimate=cost(6),
        name="attend",
    )(me, scales, lengths, *arrived[::-1])
    windows = trade(attended, "tm", direct)

    units = expert_in.shape[1]
    (shard,) = after((jnp.concatenate([expert_in[0], expert_out[0]]),), windows[::-1])
    if half == 2:
        moved = lax.ppermute(shard, "tm", [(i, i ^ 1) for i in range(count)])
        weights = [expert_in[0], expert_out[0], moved]
        spans = (((0, 0), (1, 0)), ((2, 0), (2, units)))
    else:
        groups = [list(range(i, i + half)) for i in (0, half)]
        weights = [
            lax.all_gather(one, "tm", axis=0, tiled=True, axis_index_groups=groups)
            for one in (shard[:units], shard[units:])
        ]
        units = units * half
        spans = (((0, 0), (1, 0)),)

    taps = jnp.transpose(conv_taps.reshape(KERNEL, D // LANES, LANES), (1, 0, 2))
    slots = experts * capacity

    def route(array):
        whole = array.reshape(experts, capacity, D)
        moved = lax.all_to_all(whole, "dp", split_axis=0, concat_axis=0, tiled=True)
        return (moved.reshape(slots, D),)

    def send_frames(windows, flip, block_routes):
        made = pl.pallas_call(
            functools.partial(frame_kernel, count, rows, experts, capacity, place, flip),
            out_shape=(
                jax.ShapeDtypeStruct((slots, D), BF16),
                jax.ShapeDtypeStruct((rows, LANES), F32),
                jax.ShapeDtypeStruct((D // LANES, rows, LANES), F32),
            ),
            in_specs=[SMEM, SMEM, SMEM] + [VMEM] * (5 + count),
            out_specs=(VMEM,) * 3,
            scratch_shapes=[
                pltpu.VMEM((D // LANES, window, LANES), F32),
                pltpu.VMEM((D // LANES, rows, LANES), F32),
                pltpu.VMEM((window, LANES), F32),
            ],
            compiler_params=params(56),
            cost_estimate=cost(7),
            name="frames",
        )(me, expert, lengths, out_proj, taps, router, block_routes, block_routes.T, *windows[::-1])
        return made

    def run_expert(tokens, matrices, parts, partial=(), last=True):
        operands = (*tokens, *matrices, *partial)
        if last:
            made = (jax.ShapeDtypeStruct((capacity, D), BF16),) * experts
        else:
            made = (jax.ShapeDtypeStruct((slots, D), F32),)
        kernel = functools.partial(
            expert_kernel, experts if last else 0, units, parts, len(partial) > 0
        )
        return pl.pallas_call(
            kernel,
            out_shape=made,
            in_specs=[SMEM] + [pl.BlockSpec(memory_space=pl.ANY)] * len(operands),
            out_specs=(VMEM,) * len(made),
            scratch_shapes=[pltpu.VMEM(one.shape, one.dtype) for one in operands]
            + [
                pltpu.VMEM((slots, D) if last else (8, LANES), F32),
                pltpu.SemaphoreType.DMA((len(operands),)),
            ],
            compiler_params=params(56),
            cost_estimate=cost(8 if last else 0),
            name="experts",
        )(expert, *operands)

    outgoing_a, info_a, _ = send_frames(windows, half, partner_routes)
    tokens_a = route(outgoing_a)
    windows = after(windows[::-1], (outgoing_a,))[::-1]
    outgoing_b, info_b, second = send_frames(windows, 0, routes[0])
    tokens_b = route(after((outgoing_b,), tokens_a)[0])
    if half == 2:
        begun = run_expert(tokens_a, weights[:2], spans[:1], last=False)
        rest = (((0, 0), (0, units)),)
        produced_a = run_expert(tokens_a, weights[2:], rest, begun)
    else:
        produced_a = run_expert(tokens_a, weights, spans)
    back_a = trade(after(produced_a, tokens_b), "dp")
    produced_b = run_expert(after(tokens_b, produced_a), weights, spans)
    back_b = trade(produced_b, "dp")
    order = far_first(experts)
    back_a = after([back_a[r] for r in order], back_b[1:2])
    back_b = [back_b[r] for r in order]

    theirs = pl.pallas_call(
        theirs_kernel,
        out_shape=jax.ShapeDtypeStruct((rows, D), BF16),
        in_specs=[VMEM] * (1 + len(back_a)),
        out_specs=VMEM,
        compiler_params=params(16),
        cost_estimate=cost(1),
        name="theirs",
    )(info_a, *back_a)
    received = lax.ppermute(theirs, "tm", partner)
    out = pl.pallas_call(
        mine_kernel,
        out_shape=jax.ShapeDtypeStruct((rows, D), BF16),
        in_specs=[VMEM] * (3 + len(back_b)),
        out_specs=VMEM,
        compiler_params=params(16),
        cost_estimate=cost(1),
        name="mine",
    )(info_b, second, received, *back_b)
    return out[None]


def solution(mesh):
    return jax.shard_map(
        body,
        mesh=mesh,
        in_specs=(
            P("dp", "tm", None),
            P("dp", "tm", None),
            P("dp", "tm", None),
            P(),
            P(),
            P(),
            P(),
            P("dp", "tm", None),
            P("dp", "tm", None),
            P("dp", None),
            P("dp", "tm", None),
        ),
        out_specs=P("dp", "tm", None),
        check_vma=False,
    )
```

```python
import functools

import jax
import jax.numpy as jnp
from jax import lax
from jax.experimental import pallas as pl
from jax.experimental.pallas import tpu as pltpu
from jax.sharding import PartitionSpec as P

D = 1536
HEADS = 16
HEAD_DIM = 64
KERNEL = 31
TOPK = 2
RECS = 4
HALO = 16
LANES = 128
APART = 64.0
LOG2E = 1.4426950408889634
F32 = jnp.float32
BF16 = jnp.bfloat16
VMEM = pl.BlockSpec(memory_space=pltpu.VMEM)
SMEM = pl.BlockSpec(memory_space=pltpu.SMEM)


def params(mib):
    return pltpu.CompilerParams(vmem_limit_bytes=mib << 20)


def cost(micros):
    return pl.CostEstimate(flops=micros * 1_100_000_000, bytes_accessed=0, transcendentals=0)


def labels_of(frames, len_ref):
    first = len_ref[0, 0]
    second = first + len_ref[0, 1]
    third = second + len_ref[0, 2]
    return (
        (frames >= first).astype(F32)
        + (frames >= second).astype(F32)
        + (frames >= third).astype(F32)
    )


def unit_tile(tile, low):
    lifted = tile.astype(F32)
    square = lifted * lifted
    left = jnp.sum(jnp.where(low, square, 0.0), axis=1, keepdims=True)
    right = jnp.sum(jnp.where(low, 0.0, square), axis=1, keepdims=True)
    factor = jnp.where(low, lax.rsqrt(left + 1e-06), lax.rsqrt(right + 1e-06))
    return lifted * factor


def pack_kernel(place, me_ref, q_ref, k_ref, v_ref, *refs):
    o_refs, sem_ref = refs[:-1], refs[-1]
    width = o_refs[0].shape[2]
    copies = []
    for r in range(len(o_refs) - 1, -1, -1):
        target = place(me_ref[0], r)
        for which, ref in enumerate((q_ref, k_ref, v_ref)):
            if width % LANES == 0:
                columns = pl.ds(pl.multiple_of(target * width, LANES), width)
                copy = pltpu.make_async_copy(
                    ref.at[:, columns], o_refs[r].at[which], sem_ref.at[r * 3 + which]
                )
                copy.start()
                copies.append(copy)
            else:
                o_refs[r][which] = ref[:, target * width : (target + 1) * width]
    for copy in copies:
        copy.wait()


def attend_kernel(count, rows, heads, place, me_ref, scale_ref, len_ref, *refs):
    x_refs, o_refs = refs[:count][::-1], refs[count : 2 * count]
    k_ref, v_ref, a_ref = refs[2 * count :]
    me = me_ref[0]
    width = heads * HEAD_DIM
    tiles = max(1, width // LANES)
    half = count // 2
    window = rows + 2 * HALO

    def tile_of(r, which, tile):
        if width >= LANES:
            return x_refs[r][which, :, tile * LANES : (tile + 1) * LANES]
        piece = x_refs[r][which]
        return jnp.concatenate([piece, jnp.zeros((rows, LANES - width), BF16)], axis=1)

    low = lax.broadcasted_iota(jnp.int32, (rows, LANES), 1) < HEAD_DIM
    lane = lax.broadcasted_iota(jnp.int32, (rows, LANES), 1).astype(F32)
    row = lax.broadcasted_iota(jnp.int32, (rows, LANES), 0)

    edge = jnp.zeros((HALO, width), BF16)
    a_ref[0:HALO, :] = edge
    a_ref[HALO + count * rows :, :] = edge
    for r in range(count):
        at = slice(r * rows, (r + 1) * rows)
        label = labels_of(row + place(me, r) * rows, len_ref)
        other = jnp.where((lane >= 1.0) & (lane <= 4.0) & (lane != label + 1.0), -APART, 0.0)
        extra = jnp.where(lane == 0.0, -1.0, other).astype(BF16)
        for tile in range(tiles):
            k_ref[tile, at, 0:LANES] = unit_tile(tile_of(r, 1, tile), low).astype(BF16)
            k_ref[tile, at, LANES:] = extra
            v_ref[tile, at, 0:LANES] = tile_of(r, 2, tile)
            v_ref[tile, at, LANES:] = jnp.ones((rows, LANES), BF16)

    for r in range(count):
        block = place(me, r)
        label = labels_of(row + block * rows, len_ref)
        extra = jnp.where((lane == 0.0) | (lane == label + 1.0), 1.0, 0.0).astype(BF16)
        for tile in range(tiles):
            unit = unit_tile(tile_of(r, 0, tile), low)
            parts = []
            for side in range(min(2, heads)):
                head = tile * 2 + side
                kept = jnp.where(low if side == 0 else ~low, unit, 0.0).astype(BF16)
                query = jnp.concatenate([kept, extra], axis=1)
                scores = lax.dot_general(
                    query, k_ref[tile], (((1,), (1,)), ((), ())), preferred_element_type=F32
                )
                weights = jnp.exp2(scores * (scale_ref[head] * LOG2E)).astype(BF16)
                summed = jnp.dot(weights, v_ref[tile], preferred_element_type=F32)
                parts.append(summed[:, 0:LANES] / summed[:, LANES:])
            done = parts[0] if len(parts) == 1 else jnp.where(low, parts[0], parts[1])
            start = pl.multiple_of(HALO + block * rows, HALO)
            wide = min(LANES, width)
            a_ref[pl.ds(start, rows), tile * LANES : tile * LANES + wide] = done[:, 0:wide].astype(BF16)

    for r in range(count):
        target = place(me, r)
        for which, block in enumerate((target ^ half, target)):
            begin = pl.multiple_of(block * rows, HALO)
            o_refs[r][which] = a_ref[pl.ds(begin, window), :]


def normalize(values):
    average = jnp.mean(values, axis=-1, keepdims=True)
    centered = values - average
    spread = jnp.mean(centered * centered, axis=-1, keepdims=True)
    return centered * lax.rsqrt(spread + 1e-05)


def frame_kernel(
    count,
    rows,
    experts,
    capacity,
    place,
    flip,
    me_ref,
    expert_ref,
    len_ref,
    proj_ref,
    taps_ref,
    router_ref,
    routes_ref,
    turned_ref,
    *refs,
):
    att_refs, out_ref = refs[:count][::-1], refs[count]
    info_ref, second_ref, x_ref, first_ref, lab_ref = refs[-5:]
    me = me_ref[0]
    turn = expert_ref[0]
    window = rows + 2 * HALO
    half = (KERNEL - 1) // 2
    tiles = D // LANES
    step = 56
    which = 0 if flip else 1
    width = att_refs[0].shape[2]
    first = None
    for r in range(count):
        begin = pl.multiple_of(place(me, r) * width, HEAD_DIM)
        term = jnp.dot(
            att_refs[r][which], proj_ref[pl.ds(begin, width), :], preferred_element_type=F32
        )
        first = term if first is None else first + term
    normed = normalize(first).astype(BF16).astype(F32)
    origin = (me ^ flip) * rows
    frames = lax.broadcasted_iota(jnp.int32, (window, LANES), 0) + (origin - HALO)
    lab_ref[...] = labels_of(frames, len_ref)
    for tile in range(tiles):
        at = slice(tile * LANES, (tile + 1) * LANES)
        x_ref[tile] = normed[:, at]
        first_ref[tile] = first[HALO : HALO + rows, at]

    starts = [len_ref[0, 0], len_ref[0, 0] + len_ref[0, 1]]
    starts.append(starts[1] + len_ref[0, 2])
    for begin in range(0, rows, step):
        low = origin + begin - half
        high = low + step + 2 * half
        crossed = functools.reduce(
            jnp.logical_or, [(low < start) & (start < high) for start in starts]
        )

        def columns(tile, masked):
            total = jnp.zeros((step, LANES), F32)
            own = lab_ref[HALO + begin : HALO + begin + step, :] if masked else None
            for tap in range(KERNEL):
                source = HALO - half + begin + tap
                term = taps_ref[tile, tap : tap + 1, :] * x_ref[tile, source : source + step, :]
                if masked:
                    term = jnp.where(lab_ref[source : source + step, :] == own, term, 0.0)
                total = total + term
            gated = total / (1.0 + jnp.exp(-total))
            second_ref[tile, begin : begin + step, :] = (
                first_ref[tile, begin : begin + step, :] + gated
            )

        @pl.when(crossed)
        def _():
            lax.fori_loop(0, tiles, lambda tile, c: (columns(tile, True), c)[1], 0)

        @pl.when(jnp.logical_not(crossed))
        def _():
            lax.fori_loop(0, tiles, lambda tile, c: (columns(tile, False), c)[1], 0)

    second = jnp.concatenate([second_ref[tile] for tile in range(tiles)], axis=1)
    mixed = normalize(second).astype(BF16)

    logits = jnp.dot(mixed, router_ref[...], preferred_element_type=F32)
    lane = lax.broadcasted_iota(jnp.int32, (rows, experts), 1)
    named = [lane == routes_ref[:, pick : pick + 1] for pick in range(TOPK)]
    picked = [jnp.sum(jnp.where(one, logits, 0.0), axis=1, keepdims=True) for one in named]
    top = jnp.maximum(picked[0], picked[1])
    raised = [jnp.exp(one - top) for one in picked]
    mass = raised[0] + raised[1]
    down = lax.broadcasted_iota(jnp.int32, (rows, rows), 0)
    across = lax.broadcasted_iota(jnp.int32, (rows, rows), 1)
    picks = jnp.where(named[0] | named[1], 1.0, 0.0).astype(BF16)
    earlier = jnp.where(across < down, 1.0, 0.0).astype(BF16)
    ranks = jnp.dot(earlier, picks, preferred_element_type=F32)
    column = lax.broadcasted_iota(jnp.int32, (rows, LANES), 1)
    info = jnp.zeros((rows, LANES), F32)
    for pick in range(TOPK):
        rank = jnp.sum(jnp.where(named[pick], ranks, 0.0), axis=1, keepdims=True)
        place_of = routes_ref[:, pick : pick + 1] ^ turn
        slot = rank + (place_of * capacity).astype(F32)
        info = jnp.where(column == pick, slot, info)
        info = jnp.where(column == TOPK + pick, raised[pick] / mass, info)
    info_ref[...] = info

    expert = lax.broadcasted_iota(jnp.int32, (experts, rows), 0)
    chosen = (expert == turned_ref[0:1, :]) | (expert == turned_ref[1:2, :])
    later = jnp.where(down < across, 1.0, 0.0).astype(BF16)
    order = jnp.dot(jnp.where(chosen, 1.0, 0.0).astype(BF16), later, preferred_element_type=F32)
    order = jnp.where(chosen, order, -1.0)
    slot = lax.broadcasted_iota(jnp.int32, (capacity, rows), 0).astype(F32)
    select = jnp.concatenate(
        [jnp.where(slot == order[e : e + 1, :], 1.0, 0.0) for e in range(experts)], axis=0
    ).astype(BF16)
    out_ref[...] = jnp.dot(select, mixed, preferred_element_type=F32).astype(BF16)


def joined(refs):
    order = far_first(len(refs))
    parts = [refs[order.index(r)][...].astype(F32) for r in range(len(refs))]
    return jnp.concatenate(parts, axis=0).astype(BF16)


def expert_kernel(experts, units, spans, begun, expert_ref, *refs):
    results = max(1, experts)
    count = (len(refs) - results - 2) // 2
    sources, o_refs = refs[:count], refs[count : count + results]
    held, (sum_ref, sem_ref) = refs[count + results : -2], refs[-2:]
    copies = [
        pltpu.make_async_copy(sources[k], held[k], sem_ref.at[k]) for k in range(count)
    ]
    for copy in copies:
        copy.start()
    waiting = set(range(count))

    def ready(k):
        if k in waiting:
            waiting.remove(k)
            copies[k].wait()
        return held[k]

    tokens = ready(0)[...]
    products = []
    for (into, first), (out, second) in spans:
        raw = lax.dot_general(
            tokens,
            ready(1 + into)[first : first + units, :],
            (((1,), (1,)), ((), ())),
            preferred_element_type=F32,
        )
        hidden = (raw / (1.0 + jnp.exp(-raw))).astype(BF16)
        products.append(
            jnp.dot(hidden, ready(1 + out)[second : second + units, :], preferred_element_type=F32)
        )
    if begun:
        products.append(ready(count - 1)[...])
    total = functools.reduce(jnp.add, products)
    if experts == 0:
        o_refs[0][...] = total
        return
    sum_ref[...] = total
    tall = o_refs[0].shape[0]
    for r, o_ref in enumerate(o_refs):
        begin = pl.multiple_of((expert_ref[0] ^ r) * tall, 8)
        o_ref[...] = sum_ref[pl.ds(begin, tall), :].astype(BF16)


def mixture_of(info, back_refs):
    back = joined(back_refs)
    column = lax.broadcasted_iota(jnp.int32, (info.shape[0], back.shape[0]), 1).astype(F32)
    spread = jnp.where(column == info[:, 0:1], info[:, 2:3], 0.0)
    spread = jnp.where(column == info[:, 1:2], info[:, 3:4], spread).astype(BF16)
    return jnp.dot(spread, back, preferred_element_type=F32)


def theirs_kernel(info_ref, *refs):
    refs[-1][...] = mixture_of(info_ref[...], refs[:-1]).astype(BF16)


def mine_kernel(info_ref, second_ref, part_ref, *refs):
    o_ref = refs[-1]
    mixture = mixture_of(info_ref[...], refs[:-1])
    for tile in range(D // LANES):
        at = slice(tile * LANES, (tile + 1) * LANES)
        both = mixture[:, at] + part_ref[:, at].astype(F32)
        o_ref[:, at] = (second_ref[tile] + 0.5 * both).astype(BF16)


def crossed(count, direct, me, r):
    return me ^ r if direct else r


def trade(arrays, axis, direct=True):
    count = len(arrays)
    if not direct:
        mixed = lax.all_to_all(jnp.stack(arrays), axis, split_axis=0, concat_axis=0, tiled=True)
        return [mixed[r] for r in range(count)]
    moved = {
        r: lax.ppermute(arrays[r], axis, [(i, i ^ r) for i in range(count)])
        for r in range(count - 1, 0, -1)
    }
    return [arrays[0]] + [moved[r] for r in range(1, count)]


def far_first(count):
    return sorted(range(count), key=lambda r: (r == 0, -bin(r >> 1).count("1"), r))


def after(arrays, markers):
    return lax.optimization_barrier((*arrays, *markers))[: len(arrays)]


def body(
    query_rows,
    key_rows,
    value_rows,
    head_scale,
    out_proj,
    conv_taps,
    router,
    expert_in,
    expert_out,
    lengths,
    routes,
):
    rows = query_rows.shape[1]
    experts = lax.axis_size("dp")
    count = lax.axis_size("tm")
    half = count // 2
    heads = HEADS // count
    width = heads * HEAD_DIM
    window = rows + 2 * HALO
    capacity = -(-(3 * rows // experts) // 8) * 8
    direct = width % LANES == 0
    me = lax.axis_index("tm").astype(jnp.int32).reshape(1)
    expert = lax.axis_index("dp").astype(jnp.int32).reshape(1)
    partner = [(i, i ^ half) for i in range(count)]
    place = functools.partial(crossed, count, direct)

    packed = pl.pallas_call(
        functools.partial(pack_kernel, place),
        out_shape=(jax.ShapeDtypeStruct((3, rows, width), BF16),) * count,
        in_specs=[SMEM] + [pl.BlockSpec(memory_space=pltpu.HBM) if direct else VMEM] * 3,
        out_specs=(pl.BlockSpec(memory_space=pltpu.HBM) if direct else VMEM,) * count,
        scratch_shapes=[pltpu.SemaphoreType.DMA((3 * count,))],
        compiler_params=params(60),
        cost_estimate=cost(1),
        name="pack",
    )(me, query_rows[0], key_rows[0], value_rows[0])
    arrived = trade(packed, "tm", direct)
    scales = lax.dynamic_slice_in_dim(head_scale, me[0] * heads, heads)
    partner_routes = lax.ppermute(routes[0], "tm", partner)

    tiles = max(1, width // LANES)
    total = count * rows
    attended = pl.pallas_call(
        functools.partial(attend_kernel, count, rows, heads, place),
        out_shape=(jax.ShapeDtypeStruct((2, window, width), BF16),) * count,
        in_specs=[SMEM, SMEM, SMEM] + [VMEM] * count,
        out_specs=(VMEM,) * count,
        scratch_shapes=[
            pltpu.VMEM((tiles, total, 2 * LANES), BF16),
            pltpu.VMEM((tiles, total, 2 * LANES), BF16),
            pltpu.VMEM((total + 2 * HALO, width), BF16),
        ],
        compiler_params=params(16),
        cost_estimate=cost(6),
        name="attend",
    )(me, scales, lengths, *arrived[::-1])
    windows = trade(attended, "tm", direct)

    units = expert_in.shape[1]
    (shard,) = after((jnp.concatenate([expert_in[0], expert_out[0]]),), windows[::-1])
    if half == 2:
        moved = lax.ppermute(shard, "tm", [(i, i ^ 1) for i in range(count)])
        weights = [expert_in[0], expert_out[0], moved]
        spans = (((0, 0), (1, 0)), ((2, 0), (2, units)))
    else:
        groups = [list(range(i, i + half)) for i in (0, half)]
        weights = [
            lax.all_gather(one, "tm", axis=0, tiled=True, axis_index_groups=groups)
            for one in (shard[:units], shard[units:])
        ]
        units = units * half
        spans = (((0, 0), (1, 0)),)

    taps = jnp.transpose(conv_taps.reshape(KERNEL, D // LANES, LANES), (1, 0, 2))
    slots = experts * capacity

    def route(array):
        whole = array.reshape(experts, capacity, D)
        moved = lax.all_to_all(whole, "dp", split_axis=0, concat_axis=0, tiled=True)
        return (moved.reshape(slots, D),)

    def send_frames(windows, flip, block_routes):
        made = pl.pallas_call(
            functools.partial(frame_kernel, count, rows, experts, capacity, place, flip),
            out_shape=(
                jax.ShapeDtypeStruct((slots, D), BF16),
                jax.ShapeDtypeStruct((rows, LANES), F32),
                jax.ShapeDtypeStruct((D // LANES, rows, LANES), F32),
            ),
            in_specs=[SMEM, SMEM, SMEM] + [VMEM] * (5 + count),
            out_specs=(VMEM,) * 3,
            scratch_shapes=[
                pltpu.VMEM((D // LANES, window, LANES), F32),
                pltpu.VMEM((D // LANES, rows, LANES), F32),
                pltpu.VMEM((window, LANES), F32),
            ],
            compiler_params=params(56),
            cost_estimate=cost(7),
            name="frames",
        )(me, expert, lengths, out_proj, taps, router, block_routes, block_routes.T, *windows[::-1])
        return made

    def run_expert(tokens, matrices, parts, partial=(), last=True):
        operands = (*tokens, *matrices, *partial)
        if last:
            made = (jax.ShapeDtypeStruct((capacity, D), BF16),) * experts
        else:
            made = (jax.ShapeDtypeStruct((slots, D), F32),)
        kernel = functools.partial(
            expert_kernel, experts if last else 0, units, parts, len(partial) > 0
        )
        return pl.pallas_call(
            kernel,
            out_shape=made,
            in_specs=[SMEM] + [pl.BlockSpec(memory_space=pl.ANY)] * len(operands),
            out_specs=(VMEM,) * len(made),
            scratch_shapes=[pltpu.VMEM(one.shape, one.dtype) for one in operands]
            + [
                pltpu.VMEM((slots, D) if last else (8, LANES), F32),
                pltpu.SemaphoreType.DMA((len(operands),)),
            ],
            compiler_params=params(56),
            cost_estimate=cost(8 if last else 0),
            name="experts",
        )(expert, *operands)

    outgoing_a, info_a, _ = send_frames(windows, half, partner_routes)
    tokens_a = route(outgoing_a)
    windows = after(windows[::-1], (outgoing_a,))[::-1]
    outgoing_b, info_b, second = send_frames(windows, 0, routes[0])
    tokens_b = route(after((outgoing_b,), tokens_a)[0])
    if half == 2:
        begun = run_expert(tokens_a, weights[:2], spans[:1], last=False)
        rest = (((0, 0), (0, units)),)
        produced_a = run_expert(tokens_a, weights[2:], rest, begun)
    else:
        produced_a = run_expert(tokens_a, weights, spans)
    back_a = trade(after(produced_a, tokens_b), "dp")
    produced_b = run_expert(after(tokens_b, produced_a), weights, spans)
    back_b = trade(produced_b, "dp")
    order = far_first(experts)
    back_a = after([back_a[r] for r in order], back_b[1:2])
    back_b = [back_b[r] for r in order]

    theirs = pl.pallas_call(
        theirs_kernel,
        out_shape=jax.ShapeDtypeStruct((rows, D), BF16),
        in_specs=[VMEM] * (1 + len(back_a)),
        out_specs=VMEM,
        compiler_params=params(16),
        cost_estimate=cost(1),
        name="theirs",
    )(info_a, *back_a)
    received = lax.ppermute(theirs, "tm", partner)
    out = pl.pallas_call(
        mine_kernel,
        out_shape=jax.ShapeDtypeStruct((rows, D), BF16),
        in_specs=[VMEM] * (3 + len(back_b)),
        out_specs=VMEM,
        compiler_params=params(16),
        cost_estimate=cost(1),
        name="mine",
    )(info_b, second, received, *back_b)
    return out[None]


def solution(mesh):
    return jax.shard_map(
        body,
        mesh=mesh,
        in_specs=(
            P("dp", "tm", None),
            P("dp", "tm", None),
            P("dp", "tm", None),
            P(),
            P(),
            P(),
            P(),
            P("dp", "tm", None),
            P("dp", "tm", None),
            P("dp", None),
            P("dp", "tm", None),
        ),
        out_specs=P("dp", "tm", None),
        check_vma=False,
    )
```
